256 devices in a mesh: row: 32 (over z, x_hi, core), col: 8 (over x_lo, y).
Axes of the slice: x: 4 (x_hi: 2, x_lo: 2; x = x_hi * 2 + x_lo), y: 4, z: 8, core: 2. Of those that a mesh axis runs over, the one named last changes fastest.
Arguments:
- features: bfloat16 [8, 8192, 256], P('col', 'row'), may hold values from -6 to 6
- adj_tiles: bfloat16 [32, 8, 12, 256, 256], P('row', 'col')
- tile_row: int32 [32, 8, 12], P('row', 'col'), may hold values from 0 to 7, as said below
- tile_col: int32 [32, 8, 12], P('row', 'col'), may hold values from 0 to 31
- tile_count: int32 [32, 8], P('row', 'col'), may hold values from 1 to 12, as said below
- weight: bfloat16 [256, 256], replicated, may hold values from -0.375 to 0.375
- cotangent: bfloat16 [65536, 256], P(('row', 'col')), may hold values from -6 to 6
Outputs:
- activated: bfloat16 [65536, 256], P(('row', 'col'))
- weight_grad: float32 [256, 256], replicated
- feature_grad: bfloat16 [8, 8192, 256], P('col', 'row')
The draws below stay inside these ranges and needn't reach their ends.
Inputs may be any that keep to these rules, and one draw needn't show every extreme that they name: The pairs (tile_row, tile_col) of the 12 slots of one block pair are distinct. `tile_count`: some block pair uses all 12 slots in every draw.
All inputs are finite; a program needn't handle non-finite values.
Results may differ from the reference program's by a relative error of at most 0.015.
Values may be sent and summed in bfloat16 or wider, within the bound.
No kernel may reach another device: no remote copies, remote signals or barrier semaphores. Data moves between devices by JAX's collectives and lax.ppermute only.
A program may use at most 64 MiB of HBM per device.

```python
import math
import jax
import jax.numpy as jnp
from jax import lax

F = 256
TILE = 256
TILE_ROWS = 8
SLOTS = 12
ROW_BLOCKS = 32
COL_BLOCKS = 8
ROW_NODES = 2048
NODES = 65536
COL_NODES = 8192
COL_TILES = 32


def tile_positions(key):
    places = TILE_ROWS * COL_TILES
    device_keys = jax.random.split(key, ROW_BLOCKS * COL_BLOCKS)
    chosen = jax.vmap(lambda one_key: jax.random.permutation(one_key, places)[:SLOTS])(device_keys)
    return chosen.reshape(ROW_BLOCKS, COL_BLOCKS, SLOTS).astype(jnp.int32)


def draw_tile_row(key, part):
    return (tile_positions(key) // COL_TILES).astype(jnp.int32)


def draw_tile_col(key, part):
    return (tile_positions(key) % COL_TILES).astype(jnp.int32)


def draw_tile_count(key, part):
    key = jax.random.fold_in(key, 5)
    first_key, second_key, pick_key = jax.random.split(key, 3)
    first = jax.random.randint(first_key, (ROW_BLOCKS * COL_BLOCKS,), 0, SLOTS + 1)
    second = jax.random.randint(second_key, (ROW_BLOCKS * COL_BLOCKS,), 0, SLOTS + 1)
    counts = jnp.maximum(jnp.minimum(first, second), max(SLOTS // 8, 1))
    chosen = jax.random.randint(pick_key, (), 0, ROW_BLOCKS * COL_BLOCKS)
    counts = jnp.where(jnp.arange(ROW_BLOCKS * COL_BLOCKS) == chosen, SLOTS, counts)
    return counts.reshape(ROW_BLOCKS, COL_BLOCKS).astype(jnp.int32)


def draw_adj_tiles(key, part):
    key = jax.random.fold_in(key, 7)
    mask_key, value_key = jax.random.split(key, 2)
    shape = (ROW_BLOCKS, COL_BLOCKS, SLOTS, TILE, TILE)
    factor = (0.16 * TILE * SLOTS * COL_BLOCKS / TILE_ROWS) ** (-0.5)
    present = jax.random.bernoulli(mask_key, 0.4, shape).astype(jnp.float32)
    values = jax.random.uniform(value_key, shape, jnp.float32, 0.25, 1.75)
    return (present * values * factor).astype(jnp.bfloat16)


def block_levels(rng, extent, cuts, smallest, top_value):
    def one(position, blocks):
        draws = jax.random.uniform(jax.random.fold_in(jax.random.fold_in(rng, 6), position), (blocks,), jnp.float32, smallest / len(cuts), top_value / len(cuts))
        return jnp.repeat(jnp.exp(draws), extent[position] // blocks).reshape((-1,) + (1,) * (len(extent) - position - 1))

    level = one(*cuts[0])
    for cut in cuts[1:]:
        level = level * one(*cut)
    return level


def normal_values(key, dims, width, reach, cuts=(), held_as=jnp.bfloat16):
    loudness = block_levels(key, dims, cuts, -0.22, 0.18) if cuts else 1.0
    array = jax.random.normal(key, dims, jnp.float32) * width * loudness
    return jnp.minimum(jnp.maximum(array, -reach), reach).astype(held_as)


def setup_inputs(seed: int = 0) -> dict:
    splits = jax.random.split(jax.random.key(seed), 8)
    features = normal_values(splits[0], (COL_BLOCKS, COL_NODES, F), 1.0, 6.0, ((0, 8), (1, 32)))
    adj_tiles = draw_adj_tiles(jax.random.fold_in(splits[7], 71), 0)
    tile_row = draw_tile_row(jax.random.fold_in(splits[7], 71), 0)
    tile_col = draw_tile_col(jax.random.fold_in(splits[7], 71), 0)
    tile_count = draw_tile_count(jax.random.fold_in(splits[7], 71), 0)
    weight = normal_values(splits[5], (F, F), F ** -0.5, 0.375)
    cotangent = normal_values(splits[6], (NODES, F), 1.0, 6.0, ((0, 256),))
    return {"features": features, "adj_tiles": adj_tiles, "tile_row": tile_row, "tile_col": tile_col, "tile_count": tile_count, "weight": weight, "cotangent": cotangent}


def reference(features, adj_tiles, tile_row, tile_col, tile_count, weight, cotangent):
    feat = features.reshape(NODES, F)
    tiles = adj_tiles.reshape(ROW_BLOCKS * COL_BLOCKS * SLOTS, TILE, TILE)
    rows_flat = tile_row.reshape(-1).astype(jnp.int32)
    cols_flat = tile_col.reshape(-1).astype(jnp.int32)
    counts_flat = tile_count.reshape(-1).astype(jnp.int32)
    total_slots = ROW_BLOCKS * COL_BLOCKS * SLOTS

    def locate(index):
        device = index // SLOTS
        slot_pos = index % SLOTS
        block_row = device // COL_BLOCKS
        block_col = device % COL_BLOCKS
        live = slot_pos < counts_flat[device]
        row_first = (block_row * ROW_NODES + rows_flat[index] * TILE).astype(jnp.int32)
        col_first = (block_col * COL_NODES + cols_flat[index] * TILE).astype(jnp.int32)
        return (live, row_first, col_first)

    def forward_slot(index, total):
        index = jnp.asarray(index).astype(jnp.int32)
        live, row_first, col_first = locate(index)

        def add_tile(total):
            panel_block = lax.dynamic_slice_in_dim(feat, col_first, TILE, 0)
            term = jnp.dot(tiles[index], panel_block, preferred_element_type=jnp.float32)
            current = lax.dynamic_slice_in_dim(total, row_first, TILE, 0)
            return lax.dynamic_update_slice_in_dim(total, current + term, row_first, 0)
        return lax.cond(live, add_tile, lambda total: total, total)
    summed = lax.fori_loop(0, total_slots, forward_slot, jnp.zeros((NODES, F), jnp.float32))
    weight_full = weight.astype(jnp.float32)
    pre_act = jnp.dot(summed, weight_full, precision=lax.Precision.HIGHEST)
    activated, backward = jax.vjp(jax.nn.gelu, pre_act)
    grad_pre = backward(cotangent.astype(jnp.float32))[0]
    weight_grad = jnp.dot(summed.T, grad_pre, precision=lax.Precision.HIGHEST) * (1.0 / math.sqrt(NODES))
    back_rows = jnp.dot(grad_pre, weight_full.T, precision=lax.Precision.HIGHEST).astype(jnp.bfloat16)

    def backward_slot(index, total):
        index = jnp.asarray(index).astype(jnp.int32)
        live, row_first, col_first = locate(index)

        def add_tile(total):
            back_block = lax.dynamic_slice_in_dim(back_rows, row_first, TILE, 0)
            term = jnp.dot(tiles[index].T, back_block, preferred_element_type=jnp.float32)
            current = lax.dynamic_slice_in_dim(total, col_first, TILE, 0)
            return lax.dynamic_update_slice_in_dim(total, current + term, col_first, 0)
        return lax.cond(live, add_tile, lambda total: total, total)
    summed_back = lax.fori_loop(0, total_slots, backward_slot, jnp.zeros((NODES, F), jnp.float32))
    feature_grad = summed_back.astype(jnp.bfloat16).reshape(COL_BLOCKS, COL_NODES, F)
    return (activated.astype(jnp.bfloat16), weight_grad, feature_grad)
```

```python
import functools
import math

import jax
import jax.numpy as jnp
from jax import lax
from jax.experimental import pallas as pl
from jax.experimental.pallas import tpu as pltpu
from jax.sharding import PartitionSpec as P

NZ = 8
QUAD = 4
NCOL = 8
TILE = 256
HALF = 128
SLOTS = 12
W_ROWS = 32


def row_pairs(move):
    pairs = []
    for r in range(NZ * QUAD):
        z, q = move(r // QUAD, r % QUAD)
        pairs.append((r, (z % NZ) * QUAD + q))
    return pairs


def quad_permute(x, flip):
    return lax.ppermute(x, "row", row_pairs(lambda z, q: (z, q ^ flip)))


def z_shift(x, step):
    return lax.ppermute(x, "row", row_pairs(lambda z, q: (z + step, q)))


def z_flip(x, flip):
    return lax.ppermute(x, "row", row_pairs(lambda z, q: (z ^ flip, q)))


def col_flip(x, flip):
    return lax.ppermute(x, "col", [(c, c ^ flip) for c in range(NCOL)])


def load_live_tiles(meta, adj_refs, adj_vmem, adj_sem):
    for i in range(2):

        @pl.loop(0, meta[25 * i + 24])
        def _(s, i=i):
            pltpu.make_async_copy(
                adj_refs[i].at[s], adj_vmem.at[i, s], adj_sem.at[i, s]
            ).start()


def wait_tile(adj_refs, adj_vmem, adj_sem, i, s):
    pltpu.make_async_copy(adj_refs[i].at[s], adj_vmem.at[i, s], adj_sem.at[i, s]).wait()


def panel_place(meta, tile):
    z, q = meta[50], meta[51]
    return (((tile >> 2) - z) & 7) * QUAD + ((tile & 3) ^ q)


def forward_kernel(meta, adj0, adj1, *refs):
    pieces, (out, panel, adj_vmem, acc, panel_sem, adj_sem) = refs[:9], refs[9:]
    adj_refs = (adj0, adj1)
    starts = (0, 1, 2, 3, 4, 4.5, 5, 6, 7)
    copies = [
        pltpu.make_async_copy(
            piece,
            panel.at[pl.ds(int(start * QUAD), piece.shape[0])],
            panel_sem.at[n],
        )
        for n, (start, piece) in enumerate(zip(starts, pieces))
    ]
    for copy in copies:
        copy.start()
    load_live_tiles(meta, adj_refs, adj_vmem, adj_sem)
    acc[...] = jnp.zeros_like(acc)
    for copy in copies:
        copy.wait()
    for i in range(2):

        @pl.loop(0, meta[25 * i + 24])
        def _(s, i=i):
            wait_tile(adj_refs, adj_vmem, adj_sem, i, s)
            row = meta[25 * i + s]
            place = panel_place(meta, meta[25 * i + 12 + s])
            acc[row, i] += jnp.dot(
                adj_vmem[i, s], panel[place], preferred_element_type=jnp.float32
            )

    out[...] = acc[...].astype(jnp.bfloat16)


def backward_kernel(meta, adj0, adj1, back, out, adj_vmem, acc, adj_sem):
    adj_refs = (adj0, adj1)
    load_live_tiles(meta, adj_refs, adj_vmem, adj_sem)
    acc[...] = jnp.zeros_like(acc)
    for i in range(2):

        @pl.loop(0, meta[25 * i + 24])
        def _(s, i=i):
            wait_tile(adj_refs, adj_vmem, adj_sem, i, s)
            row = meta[25 * i + s]
            place = panel_place(meta, meta[25 * i + 12 + s])
            acc[place] += lax.dot_general(
                adj_vmem[i, s],
                back[row, pl.ds(i * TILE, TILE), :],
                (((0,), (0,)), ((), ())),
                preferred_element_type=jnp.float32,
            )

    out[...] = acc[...].astype(jnp.bfloat16)


def dense_kernel(meta, agg_own, agg_other, weight, cot_own, cot_other, act_out, send_out):
    core = meta[51] & 1
    first = core == 0
    own = agg_own[...]
    other = jnp.concatenate([agg_other[TILE:, :], agg_other[:TILE, :]], axis=0)
    low = jnp.where(first, own, other)
    high = jnp.where(first, other, own)
    w = weight[...].astype(jnp.float32)
    dot = functools.partial(
        lax.dot_general,
        precision=lax.Precision.HIGHEST,
        preferred_element_type=jnp.float32,
    )
    plain = (((1,), (0,)), ((), ()))
    v = dot(low, w[:HALF], plain) + dot(high, w[HALF:], plain)
    scale = math.sqrt(2.0 / math.pi)
    square = v * v
    t = jnp.tanh(scale * (v + 0.044715 * (square * v)))
    cdf = 0.5 * (1.0 + t)
    act_out[...] = (v[:TILE] * cdf[:TILE]).astype(jnp.bfloat16)
    slope = cdf + 0.5 * v * ((1.0 - t) * (1.0 + t)) * (scale * (1.0 + 3.0 * 0.044715 * square))
    cot = jnp.concatenate([cot_own[...], cot_other[...]], axis=0).astype(jnp.float32)
    grad = cot * slope
    w_half = jnp.where(first, w[:HALF], w[HALF:])
    back = dot(grad, w_half, (((1,), (1,)), ((), ()))).astype(jnp.bfloat16)
    w_part = dot(own, grad, (((0,), (0,)), ((), ()))).astype(jnp.bfloat16)
    for c in range(NCOL):
        send_out[c, : 2 * TILE, :] = back
        piece = w_part[16 * c : 16 * c + 16]
        send_out[c, 2 * TILE : 2 * TILE + 16, :] = piece[:, :HALF]
        send_out[c, 2 * TILE + 16 :, :] = piece[:, HALF:]


SMEM = pl.BlockSpec(memory_space=pltpu.SMEM)
VMEM = pl.BlockSpec(memory_space=pltpu.VMEM)
ANY = pl.BlockSpec(memory_space=pl.ANY)


def params(mib):
    return pltpu.CompilerParams(vmem_limit_bytes=mib << 20)


def forward_tiles(meta, adj0, adj1, pieces):
    return pl.pallas_call(
        forward_kernel,
        out_shape=jax.ShapeDtypeStruct((8, 2, TILE, HALF), jnp.bfloat16),
        in_specs=[SMEM] + [ANY] * 11,
        out_specs=VMEM,
        scratch_shapes=[
            pltpu.VMEM((NZ * QUAD, TILE, HALF), jnp.bfloat16),
            pltpu.VMEM((2, SLOTS, TILE, TILE), jnp.bfloat16),
            pltpu.VMEM((8, 2, TILE, HALF), jnp.float32),
            pltpu.SemaphoreType.DMA((9,)),
            pltpu.SemaphoreType.DMA((2, SLOTS)),
        ],
        compiler_params=params(20),
        name="forward_tiles",
    )(meta, adj0, adj1, *pieces)


def backward_tiles(meta, adj0, adj1, back):
    return pl.pallas_call(
        backward_kernel,
        out_shape=jax.ShapeDtypeStruct((NZ * QUAD, TILE, HALF), jnp.bfloat16),
        in_specs=[SMEM, ANY, ANY, VMEM],
        out_specs=VMEM,
        scratch_shapes=[
            pltpu.VMEM((2, SLOTS, TILE, TILE), jnp.bfloat16),
            pltpu.VMEM((NZ * QUAD, TILE, HALF), jnp.float32),
            pltpu.SemaphoreType.DMA((2, SLOTS)),
        ],
        compiler_params=params(20),
        name="backward_tiles",
    )(meta, adj0, adj1, back)


def dense(meta, agg_own, agg_other, weight, cot_own, cot_other):
    return pl.pallas_call(
        dense_kernel,
        out_shape=(
            jax.ShapeDtypeStruct((TILE, 2 * HALF), jnp.bfloat16),
            jax.ShapeDtypeStruct((NCOL, 2 * TILE + W_ROWS, HALF), jnp.bfloat16),
        ),
        in_specs=[SMEM] + [VMEM] * 5,
        out_specs=(VMEM, VMEM),
        compiler_params=params(20),
        name="dense",
    )(meta, agg_own, agg_other, weight, cot_own, cot_other)


def weight_total(received):
    piece = received[:, 2 * TILE :, :].astype(jnp.float32).sum(axis=0)
    for flip in (1, 2, 4):
        piece = piece + z_flip(piece, flip)
    piece = piece + quad_permute(piece, 2)
    piece = jnp.concatenate([piece[:16], piece[16:]], axis=1)
    core = lax.axis_index("row") & 1
    col = lax.axis_index("col")
    whole = piece[None]
    for flip in (1, 2, 4):
        whole = jnp.concatenate([whole, col_flip(whole, flip)], axis=0)
    whole = whole[jnp.arange(NCOL) ^ col].reshape(HALF, 2 * HALF)
    partner = quad_permute(whole, 1)
    first = core == 0
    return jnp.concatenate(
        [jnp.where(first, whole, partner), jnp.where(first, partner, whole)], axis=0
    ) * (1.0 / 256.0)


def per_device(features, adj_tiles, tile_row, tile_col, tile_count, weight, cotangent):
    row = lax.axis_index("row")
    z, quad = row // QUAD, row % QUAD
    first = (quad & 1) == 0
    adj0 = adj_tiles[0, 0]
    block = features[0]

    mine = jnp.where(first, block[:, :HALF], block[:, HALF:])
    theirs = jnp.where(first, block[:, HALF:], block[:, :HALF])
    chunk = jnp.stack(
        [mine, quad_permute(theirs, 1), quad_permute(mine, 2), quad_permute(theirs, 3)]
    )

    meta0 = jnp.concatenate([tile_row[0, 0], tile_col[0, 0], tile_count[0]])
    meta1 = quad_permute(meta0, 1)
    meta = jnp.concatenate([meta0, meta1, jnp.stack([z, quad]).astype(jnp.int32)])
    adj1 = quad_permute(adj0, 1)
    cot1 = quad_permute(cotangent, 1)

    ups, downs = [chunk], [chunk]
    for _ in range(3):
        ups.append(z_shift(ups[-1], 1))
        downs.append(z_shift(downs[-1], -1))
    far_a = z_shift(ups[-1][:2], 1)
    far_b = z_shift(downs[-1][2:], -1)
    pieces = [chunk, downs[1], downs[2], downs[3], far_a, far_b, ups[3], ups[2], ups[1]]

    partial = forward_tiles(meta, adj0, adj1, pieces)
    shares = lax.all_to_all(partial, "col", 0, 0, tiled=True)
    agg = shares.reshape(NCOL, 2 * TILE, HALF).astype(jnp.float32).sum(axis=0)
    agg_other = quad_permute(agg, 1)
    activated, send = dense(meta, agg, agg_other, weight, cotangent, cot1)
    received = lax.all_to_all(send, "col", 0, 0, tiled=True)
    weight_grad = weight_total(received)
    parts = backward_tiles(meta, adj0, adj1, received).reshape(NZ, QUAD, TILE, HALF)

    def add(a, b):
        return (a.astype(jnp.float32) + b.astype(jnp.float32)).astype(jnp.bfloat16)

    up = z_shift(parts[4, :2], 1)
    down = z_shift(parts[4, 2:], -1)
    up = jnp.concatenate([add(parts[3, :2], up), parts[3, 2:]])
    down = jnp.concatenate([parts[5, :2], add(parts[5, 2:], down)])
    up, down = z_shift(up, 1), z_shift(down, -1)
    for step in (2, 1):
        up, down = add(parts[step], up), add(parts[8 - step], down)
        up, down = z_shift(up, 1), z_shift(down, -1)
    total = (
        parts[0].astype(jnp.float32) + up.astype(jnp.float32) + down.astype(jnp.float32)
    )
    to_send = total.astype(jnp.bfloat16)
    from_core = quad_permute(to_send[1], 1).astype(jnp.float32)
    from_x = quad_permute(to_send[2], 2).astype(jnp.float32)
    from_both = quad_permute(to_send[3], 3).astype(jnp.float32)
    own_half = total[0] + from_x
    other_half = from_core + from_both
    grad = jnp.concatenate(
        [jnp.where(first, own_half, other_half), jnp.where(first, other_half, own_half)],
        axis=1,
    )
    feature_grad = grad.astype(jnp.bfloat16)[None]
    return (activated, weight_grad, feature_grad)


def solution(mesh):
    return jax.shard_map(
        per_device,
        mesh=mesh,
        in_specs=(
            P("col", "row", None),
            P("row", "col", None, None, None),
            P("row", "col", None),
            P("row", "col", None),
            P("row", "col"),
            P(),
            P(("row", "col"), None),
        ),
        out_specs=(P(("row", "col"), None), P(), P("col", "row", None)),
        check_vma=False,
    )
```

```python
import functools
import math

import jax
import jax.numpy as jnp
from jax import lax
from jax.experimental import pallas as pl
from jax.experimental.pallas import tpu as pltpu
from jax.sharding import PartitionSpec as P

NZ = 8
QUAD = 4
NCOL = 8
TILE = 256
HALF = 128
SLOTS = 12
W_ROWS = 128


def row_pairs(move):
    pairs = []
    for r in range(NZ * QUAD):
        z, q = move(r // QUAD, r % QUAD)
        pairs.append((r, (z % NZ) * QUAD + q))
    return pairs


def quad_permute(x, flip):
    return lax.ppermute(x, "row", row_pairs(lambda z, q: (z, q ^ flip)))


def z_shift(x, step):
    return lax.ppermute(x, "row", row_pairs(lambda z, q: (z + step, q)))


def load_live_tiles(meta, adj_refs, adj_vmem, adj_sem):
    for i in range(2):

        @pl.loop(0, meta[25 * i + 24])
        def _(s, i=i):
            pltpu.make_async_copy(
                adj_refs[i].at[s], adj_vmem.at[i, s], adj_sem.at[i, s]
            ).start()


def wait_tile(adj_refs, adj_vmem, adj_sem, i, s):
    pltpu.make_async_copy(adj_refs[i].at[s], adj_vmem.at[i, s], adj_sem.at[i, s]).wait()


def panel_place(meta, tile):
    z, q = meta[50], meta[51]
    return (((tile >> 2) - z) & 7) * QUAD + ((tile & 3) ^ q)


def forward_kernel(meta, adj0, adj1, *refs):
    pieces, (out, panel, adj_vmem, acc, panel_sem, adj_sem) = refs[:8], refs[8:]
    adj_refs = (adj0, adj1)
    copies = [
        pltpu.make_async_copy(
            piece,
            panel.at[pl.ds(n * QUAD, QUAD)],
            panel_sem.at[n],
        )
        for n, piece in enumerate(pieces)
    ]
    for copy in copies:
        copy.start()
    load_live_tiles(meta, adj_refs, adj_vmem, adj_sem)
    acc[...] = jnp.zeros_like(acc)
    for copy in copies:
        copy.wait()
    for i in range(2):

        @pl.loop(0, meta[25 * i + 24])
        def _(s, i=i):
            wait_tile(adj_refs, adj_vmem, adj_sem, i, s)
            row = meta[25 * i + s]
            place = panel_place(meta, meta[25 * i + 12 + s])
            acc[row, i] += jnp.dot(
                adj_vmem[i, s], panel[place], preferred_element_type=jnp.float32
            )

    out[...] = acc[...].astype(jnp.bfloat16)


def backward_kernel(meta, adj0, adj1, back, out, adj_vmem, acc, adj_sem):
    adj_refs = (adj0, adj1)
    load_live_tiles(meta, adj_refs, adj_vmem, adj_sem)
    acc[...] = jnp.zeros_like(acc)
    for i in range(2):

        @pl.loop(0, meta[25 * i + 24])
        def _(s, i=i):
            wait_tile(adj_refs, adj_vmem, adj_sem, i, s)
            row = meta[25 * i + s]
            place = panel_place(meta, meta[25 * i + 12 + s])
            acc[place] += lax.dot_general(
                adj_vmem[i, s],
                back[row, pl.ds(i * TILE, TILE), :],
                (((0,), (0,)), ((), ())),
                preferred_element_type=jnp.float32,
            )

    out[...] = acc[...].astype(jnp.bfloat16)


def dense_kernel(meta, agg_own, agg_other, weight, cot_own, cot_other, act_out, send_out):
    core = meta[51] & 1
    first = core == 0
    own = agg_own[...]
    other = jnp.concatenate([agg_other[TILE:, :], agg_other[:TILE, :]], axis=0)
    low = jnp.where(first, own, other)
    high = jnp.where(first, other, own)
    w = weight[...].astype(jnp.float32)
    dot = functools.partial(
        lax.dot_general,
        precision=lax.Precision.HIGHEST,
        preferred_element_type=jnp.float32,
    )
    plain = (((1,), (0,)), ((), ()))
    v = dot(low, w[:HALF], plain) + dot(high, w[HALF:], plain)
    scale = math.sqrt(2.0 / math.pi)
    square = v * v
    t = jnp.tanh(scale * (v + 0.044715 * (square * v)))
    cdf = 0.5 * (1.0 + t)
    act_out[...] = (v[:TILE] * cdf[:TILE]).astype(jnp.bfloat16)
    slope = cdf + 0.5 * v * ((1.0 - t) * (1.0 + t)) * (scale * (1.0 + 3.0 * 0.044715 * square))
    cot = jnp.concatenate([cot_own[...], cot_other[...]], axis=0).astype(jnp.float32)
    grad = cot * slope
    w_half = jnp.where(first, w[:HALF], w[HALF:])
    back = dot(grad, w_half, (((1,), (1,)), ((), ()))).astype(jnp.bfloat16)
    w_part = dot(own, grad, (((0,), (0,)), ((), ()))).astype(jnp.bfloat16)
    for c in range(NCOL):
        send_out[c, : 2 * TILE, :] = back
        piece = w_part[64 * (c // 4) : 64 * (c // 4) + 64]
        send_out[c, 2 * TILE : 2 * TILE + 64, :] = piece[:, :HALF]
        send_out[c, 2 * TILE + 64 :, :] = piece[:, HALF:]


SMEM = pl.BlockSpec(memory_space=pltpu.SMEM)
VMEM = pl.BlockSpec(memory_space=pltpu.VMEM)
ANY = pl.BlockSpec(memory_space=pl.ANY)
HBM = pl.BlockSpec(memory_space=pltpu.HBM)


def params(mib):
    return pltpu.CompilerParams(vmem_limit_bytes=mib << 20)


def forward_tiles(meta, adj0, adj1, pieces):
    return pl.pallas_call(
        forward_kernel,
        out_shape=jax.ShapeDtypeStruct((8, 2, TILE, HALF), jnp.bfloat16),
        in_specs=[SMEM, HBM, HBM] + [ANY] * 8,
        out_specs=VMEM,
        scratch_shapes=[
            pltpu.VMEM((NZ * QUAD, TILE, HALF), jnp.bfloat16),
            pltpu.VMEM((2, SLOTS, TILE, TILE), jnp.bfloat16),
            pltpu.VMEM((8, 2, TILE, HALF), jnp.float32),
            pltpu.SemaphoreType.DMA((NZ,)),
            pltpu.SemaphoreType.DMA((2, SLOTS)),
        ],
        compiler_params=params(20),
        name="forward_tiles",
    )(meta, adj0, adj1, *pieces)


def backward_tiles(meta, adj0, adj1, back):
    return pl.pallas_call(
        backward_kernel,
        out_shape=jax.ShapeDtypeStruct((NZ * QUAD, TILE, HALF), jnp.bfloat16),
        in_specs=[SMEM, HBM, HBM, VMEM],
        out_specs=VMEM,
        scratch_shapes=[
            pltpu.VMEM((2, SLOTS, TILE, TILE), jnp.bfloat16),
            pltpu.VMEM((NZ * QUAD, TILE, HALF), jnp.float32),
            pltpu.SemaphoreType.DMA((2, SLOTS)),
        ],
        compiler_params=params(20),
        name="backward_tiles",
    )(meta, adj0, adj1, back)


def dense(meta, agg_own, agg_other, weight, cot_own, cot_other):
    return pl.pallas_call(
        dense_kernel,
        out_shape=(
            jax.ShapeDtypeStruct((TILE, 2 * HALF), jnp.bfloat16),
            jax.ShapeDtypeStruct((NCOL, 2 * TILE + W_ROWS, HALF), jnp.bfloat16),
        ),
        in_specs=[SMEM] + [VMEM] * 5,
        out_specs=(VMEM, VMEM),
        compiler_params=params(20),
        name="dense",
    )(meta, agg_own, agg_other, weight, cot_own, cot_other)


def z_both(x):
    return lax.ppermute(
        x, "row", row_pairs(lambda z, q: (z + 1 - 2 * (q & 1), q))
    )


def add(a, b):
    return (a.astype(jnp.float32) + b.astype(jnp.float32)).astype(jnp.bfloat16)


def per_device(features, adj_tiles, tile_row, tile_col, tile_count, weight, cotangent):
    row = lax.axis_index("row")
    z, quad = row // QUAD, row % QUAD
    first = (quad & 1) == 0
    adj0 = adj_tiles[0, 0]
    block = features[0]

    mine = jnp.where(first, block[:, :HALF], block[:, HALF:])
    theirs = jnp.where(first, block[:, HALF:], block[:, :HALF])
    chunk = jnp.stack(
        [mine, quad_permute(theirs, 1), quad_permute(mine, 2), quad_permute(theirs, 3)]
    )

    meta0 = jnp.concatenate([tile_row[0, 0], tile_col[0, 0], tile_count[0]])
    meta1 = quad_permute(meta0, 1)
    adj1 = quad_permute(adj0, 1)
    cot1 = quad_permute(cotangent, 1)

    up1, down1 = z_shift(chunk, 1), z_shift(chunk, -1)
    up1, down1, meta1 = lax.optimization_barrier((up1, down1, meta1))
    meta = jnp.concatenate([meta0, meta1, jnp.stack([z, quad]).astype(jnp.int32)])
    up2, down2 = z_shift(up1, 1), z_shift(down1, -1)
    up2, down2, cot1 = lax.optimization_barrier((up2, down2, cot1))
    up3, down3 = z_shift(up2, 1), z_shift(down2, -1)
    up3, down3, meta, adj1 = lax.optimization_barrier((up3, down3, meta, adj1))
    far = z_both(jnp.where(first, up3, down3))
    pieces = [chunk, down1, down2, down3, far, up3, up2, up1]

    partial = forward_tiles(meta, adj0, adj1, pieces)
    shares = lax.all_to_all(partial, "col", 0, 0, tiled=True)
    agg = shares.reshape(NCOL, 2 * TILE, HALF).astype(jnp.float32).sum(axis=0)
    agg_other = quad_permute(agg, 1)
    activated, send = dense(meta, agg, agg_other, weight, cotangent, cot1)
    received = lax.all_to_all(send, "col", 0, 0, tiled=True)
    w_piece = received[:, 2 * TILE :, :].astype(jnp.float32).sum(axis=0).astype(jnp.bfloat16)
    parts = backward_tiles(meta, adj0, adj1, received).reshape(NZ, QUAD * TILE, HALF)

    def pack(part, piece):
        return jnp.concatenate([part, piece], axis=0)

    size = QUAD * TILE
    got1 = z_both(pack(parts[4], w_piece))
    zero = jnp.zeros_like(got1[:size])
    up = add(parts[3], jnp.where(first, got1[:size], zero))
    down = add(parts[5], jnp.where(first, zero, got1[:size]))
    up = z_shift(pack(up, jnp.where(first, got1[size:], w_piece)), 1)
    down = z_shift(pack(down, jnp.where(first, w_piece, got1[size:])), -1)
    ups, downs = [up[size:]], [down[size:]]
    for step in (2, 1):
        up = z_shift(pack(add(parts[step], up[:size]), up[size:]), 1)
        down = z_shift(pack(add(parts[8 - step], down[:size]), down[size:]), -1)
        ups.append(up[size:])
        downs.append(down[size:])
    total = (
        parts[0].astype(jnp.float32)
        + up[:size].astype(jnp.float32)
        + down[:size].astype(jnp.float32)
    ).reshape(QUAD, TILE, HALF)

    near, far_w = jnp.where(first, got1[size:], ups[0]), ups[2]
    above = [jnp.where(first, d, e) for d, e in zip(downs, [got1[size:]] + downs[:2])]
    below = [near, jnp.where(first, ups[0], ups[1]), jnp.where(first, ups[1], ups[2])]
    opposite = jnp.where(first, far_w, downs[2])
    by_step = jnp.stack([w_piece] + above + [opposite] + below[::-1])
    w_sum = by_step[(jnp.arange(NZ) - z) & 7].astype(jnp.float32).sum(axis=0)

    w_send = w_sum.astype(jnp.bfloat16)
    to_send = total.astype(jnp.bfloat16)
    from_core = quad_permute(pack(to_send[1], w_send), 1)
    from_x = quad_permute(pack(to_send[2], w_send), 2)
    from_both = quad_permute(pack(to_send[3], w_send), 3)
    w_half = w_send.astype(jnp.float32) + from_x[TILE:].astype(jnp.float32)
    w_other = from_core[TILE:].astype(jnp.float32) + from_both[TILE:].astype(jnp.float32)
    w_here = jnp.stack([w_half, w_other])
    w_there = lax.ppermute(w_here, "col", [(c, c ^ 4) for c in range(NCOL)])
    low_x = lax.axis_index("col") < 4
    w_all = jnp.stack([jnp.where(low_x, w_here, w_there), jnp.where(low_x, w_there, w_here)])
    w_all = w_all.reshape(2, 2, 2, 64, HALF).transpose(1, 0, 3, 2, 4).reshape(2, HALF, 2 * HALF)
    weight_grad = jnp.where(
        first, w_all, w_all[::-1]
    ).reshape(2 * HALF, 2 * HALF) * (1.0 / 256.0)

    own_half = total[0] + from_x[:TILE].astype(jnp.float32)
    other_half = from_core[:TILE].astype(jnp.float32) + from_both[:TILE].astype(jnp.float32)
    grad = jnp.concatenate(
        [jnp.where(first, own_half, other_half), jnp.where(first, other_half, own_half)],
        axis=1,
    )
    feature_grad = grad.astype(jnp.bfloat16)[None]
    return (activated, weight_grad, feature_grad)


def solution(mesh):
    return jax.shard_map(
        per_device,
        mesh=mesh,
        in_specs=(
            P("col", "row", None),
            P("row", "col", None, None, None),
            P("row", "col", None),
            P("row", "col", None),
            P("row", "col"),
            P(),
            P(("row", "col"), None),
        ),
        out_specs=(P(("row", "col"), None), P(), P("col", "row", None)),
        check_vma=False,
    )
```

```python
import functools
import math

import jax
import jax.numpy as jnp
from jax import lax
from jax.experimental import pallas as pl
from jax.experimental.pallas import tpu as pltpu
from jax.sharding import PartitionSpec as P

NZ = 8
QUAD = 4
NCOL = 8
TILE = 256
HALF = 128
SLOTS = 12
W_ROWS = 128
UNROLL = 4


def row_pairs(move):
    pairs = []
    for r in range(NZ * QUAD):
        z, q = move(r // QUAD, r % QUAD)
        pairs.append((r, (z % NZ) * QUAD + q))
    return pairs


def quad_permute(x, flip):
    return lax.ppermute(x, "row", row_pairs(lambda z, q: (z, q ^ flip)))


def z_shift(x, step):
    return lax.ppermute(x, "row", row_pairs(lambda z, q: (z + step, q)))


def list_slots(meta, adj_refs, adj_vmem, adj_sem, rows, places, far, dummy):
    z, q = meta[50], meta[51]
    n = jnp.int32(0)
    for i in range(2):
        count = meta[25 * i + 24]
        for s in range(SLOTS):
            tile = meta[25 * i + 12 + s]
            place = (((tile >> 2) - z) & 7) * QUAD + ((tile & 3) ^ q)
            live = (s < count) & (((place >> 2) == 4) == far)
            rows[n] = meta[25 * i + s] * 2 + i
            places[n] = place

            @pl.when(live)
            def _(i=i, s=s, n=n):
                pltpu.make_async_copy(
                    adj_refs[i].at[s], adj_vmem.at[n], adj_sem.at[n]
                ).start()

            n = n + live.astype(jnp.int32)
    for u in range(UNROLL - 1):
        rows[n + u], places[n + u] = dummy
    return n


def slot_products(n, adj_ref, adj_vmem, adj_sem, product, add_to):
    @pl.loop(0, (n + UNROLL - 1) >> 2)
    def _(step):
        slots = [step * UNROLL + u for u in range(UNROLL)]
        for j in slots:

            @pl.when(j < n)
            def _(j=j):
                pltpu.make_async_copy(adj_ref.at[0], adj_vmem.at[j], adj_sem.at[j]).wait()

        values = [product(j) for j in slots]
        for j, value in zip(slots, values):
            add_to(j, value)


def forward_near_kernel(meta, adj0, adj1, *refs):
    pieces, (acc, panel, adj_vmem, rows, places, panel_sem, adj_sem) = refs[:7], refs[7:]
    copies = [
        pltpu.make_async_copy(piece, panel.at[pl.ds(place * QUAD, QUAD)], panel_sem.at[place])
        for place, piece in zip((0, 1, 2, 3, 5, 6, 7), pieces)
    ]
    for copy in copies:
        copy.start()
    n = list_slots(meta, (adj0, adj1), adj_vmem, adj_sem, rows, places, False, (16, 0))
    acc[...] = jnp.zeros_like(acc)
    for copy in copies:
        copy.wait()

    def product(j):
        return jnp.dot(adj_vmem[j], panel[places[j]], preferred_element_type=jnp.float32)

    def add_to(j, value):
        acc[rows[j]] += value

    slot_products(n, adj0, adj_vmem, adj_sem, product, add_to)


def forward_far_kernel(meta, adj0, adj1, near, far, out, acc, adj_vmem, rows, places, adj_sem):
    n = list_slots(meta, (adj0, adj1), adj_vmem, adj_sem, rows, places, True, (16, 16))
    acc[...] = near[...]

    def product(j):
        return jnp.dot(adj_vmem[j], far[places[j] - 16], preferred_element_type=jnp.float32)

    def add_to(j, value):
        acc[rows[j]] += value

    slot_products(n, adj0, adj_vmem, adj_sem, product, add_to)
    for row in range(8):
        for i in range(2):
            out[row, i] = acc[2 * row + i].astype(jnp.bfloat16)


def backward_kernel(far, meta, adj0, adj1, back, out, acc, adj_vmem, rows, places, adj_sem):
    base = 16 if far else 0
    spare = acc.shape[0] - 1
    n = list_slots(
        meta, (adj0, adj1), adj_vmem, adj_sem, rows, places, far, (0, base + spare)
    )
    acc[...] = jnp.zeros_like(acc)

    def product(j):
        row = rows[j]
        return lax.dot_general(
            adj_vmem[j],
            back[row >> 1, pl.ds((row & 1) * TILE, TILE), :],
            (((0,), (0,)), ((), ())),
            preferred_element_type=jnp.float32,
        )

    def add_to(j, value):
        acc[places[j] - base] += value

    slot_products(n, adj0, adj_vmem, adj_sem, product, add_to)
    out[...] = acc[:spare].astype(jnp.bfloat16)


def dense_kernel(meta, agg_own, agg_other, weight, cot_own, cot_other, act_out, send_out):
    core = meta[51] & 1
    first = core == 0
    own = agg_own[...]
    other = jnp.concatenate([agg_other[TILE:, :], agg_other[:TILE, :]], axis=0)
    low = jnp.where(first, own, other)
    high = jnp.where(first, other, own)
    w = weight[...].astype(jnp.float32)
    dot = functools.partial(
        lax.dot_general,
        precision=lax.Precision.HIGHEST,
        preferred_element_type=jnp.float32,
    )
    plain = (((1,), (0,)), ((), ()))
    v = dot(low, w[:HALF], plain) + dot(high, w[HALF:], plain)
    scale = math.sqrt(2.0 / math.pi)
    square = v * v
    t = jnp.tanh(scale * (v + 0.044715 * (square * v)))
    cdf = 0.5 * (1.0 + t)
    act_out[...] = (v[:TILE] * cdf[:TILE]).astype(jnp.bfloat16)
    slope = cdf + 0.5 * v * ((1.0 - t) * (1.0 + t)) * (scale * (1.0 + 3.0 * 0.044715 * square))
    cot = jnp.concatenate([cot_own[...], cot_other[...]], axis=0).astype(jnp.float32)
    grad = cot * slope
    w_half = jnp.where(first, w[:HALF], w[HALF:])
    back = dot(grad, w_half, (((1,), (1,)), ((), ()))).astype(jnp.bfloat16)
    w_part = dot(own, grad, (((0,), (0,)), ((), ()))).astype(jnp.bfloat16)
    for c in range(NCOL):
        send_out[c, : 2 * TILE, :] = back
        piece = w_part[64 * (c // 4) : 64 * (c // 4) + 64]
        send_out[c, 2 * TILE : 2 * TILE + 64, :] = piece[:, :HALF]
        send_out[c, 2 * TILE + 64 :, :] = piece[:, HALF:]


SMEM = pl.BlockSpec(memory_space=pltpu.SMEM)
VMEM = pl.BlockSpec(memory_space=pltpu.VMEM)
ANY = pl.BlockSpec(memory_space=pl.ANY)
HBM = pl.BlockSpec(memory_space=pltpu.HBM)


def params(mib):
    return pltpu.CompilerParams(vmem_limit_bytes=mib << 20)


LIST = 2 * SLOTS + UNROLL
SLOT_SCRATCH = [
    pltpu.VMEM((LIST, TILE, TILE), jnp.bfloat16),
    pltpu.SMEM((LIST,), jnp.int32),
    pltpu.SMEM((LIST,), jnp.int32),
]


def cost(slots, size):
    return pl.CostEstimate(
        flops=slots * 2 * TILE * TILE * HALF, bytes_accessed=size << 20, transcendentals=0
    )


def forward_near(meta, adj0, adj1, pieces):
    return pl.pallas_call(
        forward_near_kernel,
        out_shape=jax.ShapeDtypeStruct((17, TILE, HALF), jnp.float32),
        in_specs=[SMEM] + [ANY] * 9,
        out_specs=VMEM,
        scratch_shapes=[pltpu.VMEM((NZ * QUAD, TILE, HALF), jnp.bfloat16)]
        + SLOT_SCRATCH
        + [pltpu.SemaphoreType.DMA((NZ,)), pltpu.SemaphoreType.DMA((LIST,))],
        compiler_params=params(20),
        cost_estimate=cost(21, 6),
        name="forward_near",
    )(meta, adj0, adj1, *pieces)


def forward_far(meta, adj0, adj1, near, far):
    return pl.pallas_call(
        forward_far_kernel,
        out_shape=jax.ShapeDtypeStruct((8, 2, TILE, HALF), jnp.bfloat16),
        in_specs=[SMEM, ANY, ANY, VMEM, VMEM],
        out_specs=VMEM,
        scratch_shapes=[pltpu.VMEM((17, TILE, HALF), jnp.float32)]
        + SLOT_SCRATCH
        + [pltpu.SemaphoreType.DMA((LIST,))],
        compiler_params=params(20),
        cost_estimate=cost(3, 4),
        name="forward_far",
    )(meta, adj0, adj1, near, far)


def backward_tiles(meta, adj0, adj1, back, far):
    places = QUAD if far else NZ * QUAD
    return pl.pallas_call(
        functools.partial(backward_kernel, far),
        out_shape=jax.ShapeDtypeStruct((places, TILE, HALF), jnp.bfloat16),
        in_specs=[SMEM, ANY, ANY, VMEM],
        out_specs=VMEM,
        scratch_shapes=[pltpu.VMEM((places + 1, TILE, HALF), jnp.float32)]
        + SLOT_SCRATCH
        + [pltpu.SemaphoreType.DMA((LIST,))],
        compiler_params=params(20),
        cost_estimate=cost(3, 2) if far else cost(21, 6),
        name="backward_far" if far else "backward_near",
    )(meta, adj0, adj1, back)


def dense(meta, agg_own, agg_other, weight, cot_own, cot_other):
    return pl.pallas_call(
        dense_kernel,
        out_shape=(
            jax.ShapeDtypeStruct((TILE, 2 * HALF), jnp.bfloat16),
            jax.ShapeDtypeStruct((NCOL, 2 * TILE + W_ROWS, HALF), jnp.bfloat16),
        ),
        in_specs=[SMEM] + [VMEM] * 5,
        out_specs=(VMEM, VMEM),
        compiler_params=params(20),
        name="dense",
    )(meta, agg_own, agg_other, weight, cot_own, cot_other)


def z_both(x):
    return lax.ppermute(
        x, "row", row_pairs(lambda z, q: (z + 1 - 2 * (q & 1), q))
    )


def add(a, b):
    return (a.astype(jnp.float32) + b.astype(jnp.float32)).astype(jnp.bfloat16)


def per_device(features, adj_tiles, tile_row, tile_col, tile_count, weight, cotangent):
    row = lax.axis_index("row")
    z, quad = row // QUAD, row % QUAD
    first = (quad & 1) == 0
    adj0 = adj_tiles[0, 0]
    block = features[0]

    mine = jnp.where(first, block[:, :HALF], block[:, HALF:])
    theirs = jnp.where(first, block[:, HALF:], block[:, :HALF])
    meta0 = jnp.concatenate([tile_row[0, 0], tile_col[0, 0], tile_count[0]])
    listed = jnp.pad(meta0.astype(jnp.bfloat16)[None], ((0, 15), (0, HALF - 25)))
    from_core = quad_permute(jnp.concatenate([theirs, listed], axis=0), 1)
    chunk = jnp.stack(
        [mine, from_core[:TILE], quad_permute(mine, 2), quad_permute(theirs, 3)]
    )
    meta1 = from_core[TILE, :25].astype(jnp.int32)
    meta = jnp.concatenate([meta0, meta1, jnp.stack([z, quad]).astype(jnp.int32)])
    adj1 = quad_permute(adj0, 1)
    cot1 = quad_permute(cotangent, 1)

    up1, down1 = z_shift(chunk, 1), z_shift(chunk, -1)
    up2, down2 = z_shift(up1, 1), z_shift(down1, -1)
    up3, down3 = z_shift(up2, 1), z_shift(down2, -1)
    far = z_both(jnp.where(first, up3, down3))
    near = forward_near(meta, adj0, adj1, [chunk, down1, down2, down3, up3, up2, up1])
    partial = forward_far(meta, adj0, adj1, near, far)
    shares = lax.all_to_all(partial, "col", 0, 0, tiled=True)
    agg = shares.reshape(NCOL, 2 * TILE, HALF).astype(jnp.float32).sum(axis=0)
    agg_other = quad_permute(agg, 1)
    activated, send = dense(meta, agg, agg_other, weight, cotangent, cot1)
    received = lax.all_to_all(send, "col", 0, 0, tiled=True)
    w_piece = received[:, 2 * TILE :, :].astype(jnp.float32).sum(axis=0).astype(jnp.bfloat16)
    size = QUAD * TILE
    far_part = backward_tiles(meta, adj0, adj1, received, True).reshape(size, HALF)
    parts = backward_tiles(meta, adj0, adj1, received, False).reshape(NZ, size, HALF)

    def pack(part, piece):
        return jnp.concatenate([part, piece], axis=0)

    got1 = z_both(pack(far_part, w_piece))
    zero = jnp.zeros_like(got1[:size])
    up = add(parts[3], jnp.where(first, got1[:size], zero))
    down = add(parts[5], jnp.where(first, zero, got1[:size]))
    up = z_shift(pack(up, jnp.where(first, got1[size:], w_piece)), 1)
    down = z_shift(pack(down, jnp.where(first, w_piece, got1[size:])), -1)
    ups, downs = [up[size:]], [down[size:]]
    for step in (2, 1):
        up = z_shift(pack(add(parts[step], up[:size]), up[size:]), 1)
        down = z_shift(pack(add(parts[8 - step], down[:size]), down[size:]), -1)
        ups.append(up[size:])
        downs.append(down[size:])
    total = (
        parts[0].astype(jnp.float32)
        + up[:size].astype(jnp.float32)
        + down[:size].astype(jnp.float32)
    ).reshape(QUAD, TILE, HALF)

    near, far_w = jnp.where(first, got1[size:], ups[0]), ups[2]
    above = [jnp.where(first, d, e) for d, e in zip(downs, [got1[size:]] + downs[:2])]
    below = [near, jnp.where(first, ups[0], ups[1]), jnp.where(first, ups[1], ups[2])]
    opposite = jnp.where(first, far_w, downs[2])
    by_step = jnp.stack([w_piece] + above + [opposite] + below[::-1])
    w_sum = by_step[(jnp.arange(NZ) - z) & 7].astype(jnp.float32).sum(axis=0)

    w_send = w_sum.astype(jnp.bfloat16)
    to_send = total.astype(jnp.bfloat16)
    from_core = quad_permute(pack(to_send[1], w_send), 1)
    from_x = quad_permute(pack(to_send[2], w_send), 2)
    from_both = quad_permute(pack(to_send[3], w_send), 3)
    w_half = w_send.astype(jnp.float32) + from_x[TILE:].astype(jnp.float32)
    w_other = from_core[TILE:].astype(jnp.float32) + from_both[TILE:].astype(jnp.float32)
    w_here = jnp.stack([w_half, w_other])
    w_there = lax.ppermute(w_here, "col", [(c, c ^ 4) for c in range(NCOL)])
    low_x = lax.axis_index("col") < 4
    w_all = jnp.stack([jnp.where(low_x, w_here, w_there), jnp.where(low_x, w_there, w_here)])
    w_all = w_all.reshape(2, 2, 2, 64, HALF).transpose(1, 0, 3, 2, 4).reshape(2, HALF, 2 * HALF)
    weight_grad = jnp.where(
        first, w_all, w_all[::-1]
    ).reshape(2 * HALF, 2 * HALF) * (1.0 / 256.0)

    own_half = total[0] + from_x[:TILE].astype(jnp.float32)
    other_half = from_core[:TILE].astype(jnp.float32) + from_both[:TILE].astype(jnp.float32)
    grad = jnp.concatenate(
        [jnp.where(first, own_half, other_half), jnp.where(first, other_half, own_half)],
        axis=1,
    )
    feature_grad = grad.astype(jnp.bfloat16)[None]
    return (activated, weight_grad, feature_grad)


def solution(mesh):
    return jax.shard_map(
        per_device,
        mesh=mesh,
        in_specs=(
            P("col", "row", None),
            P("row", "col", None, None, None),
            P("row", "col", None),
            P("row", "col", None),
            P("row", "col"),
            P(),
            P(("row", "col"), None),
        ),
        out_specs=(P(("row", "col"), None), P(), P("col", "row", None)),
        check_vma=False,
    )
```

```python
import functools
import math

import jax
import jax.numpy as jnp
from jax import lax
from jax.experimental import pallas as pl
from jax.experimental.pallas import tpu as pltpu
from jax.sharding import PartitionSpec as P

NZ = 8
QUAD = 4
NCOL = 8
TILE = 256
HALF = 128
SLOTS = 12
W_ROWS = 128
UNROLL = 4


def row_pairs(move):
    pairs = []
    for r in range(NZ * QUAD):
        z, q = move(r // QUAD, r % QUAD)
        pairs.append((r, (z % NZ) * QUAD + q))
    return pairs


def quad_permute(x, flip):
    return lax.ppermute(x, "row", row_pairs(lambda z, q: (z, q ^ flip)))


def z_shift(x, step):
    return lax.ppermute(x, "row", row_pairs(lambda z, q: (z + step, q)))


def prepare_kernel(rows, cols, count, block, mine, message):
    core = lax.axis_index("row") & 1

    @pl.when(core == 0)
    def _():
        mine[...] = block[:, :HALF]
        message[:TILE, :] = block[:, HALF:]

    @pl.when(core == 1)
    def _():
        mine[...] = block[:, HALF:]
        message[:TILE, :] = block[:, :HALF]

    lane = lax.broadcasted_iota(jnp.int32, (16, HALF), 1)
    values = jnp.zeros((16, HALF), jnp.float32)
    listed = [rows[s] for s in range(SLOTS)] + [cols[s] for s in range(SLOTS)] + [count[0]]
    for n, value in enumerate(listed):
        values = jnp.where(lane == n, value.astype(jnp.float32), values)
    message[TILE:, :] = values.astype(jnp.bfloat16)


def list_slots(lists, adj_refs, adj_vmem, adj_sem, rows, places, far, dummy):
    own_rows, own_cols, own_count, partner = lists
    device = lax.axis_index("row")
    z, q = device >> 2, device & 3
    n = jnp.int32(0)
    for i in range(2):
        count = partner[24] if i else own_count[0]
        for s in range(SLOTS):
            tile = partner[12 + s] if i else own_cols[s]
            row = partner[s] if i else own_rows[s]
            place = (((tile >> 2) - z) & 7) * QUAD + ((tile & 3) ^ q)
            live = (s < count) & (((place >> 2) == 4) == far)
            rows[n] = row * 2 + i
            places[n] = place

            @pl.when(live)
            def _(i=i, s=s, n=n):
                pltpu.make_async_copy(
                    adj_refs[i].at[s], adj_vmem.at[n], adj_sem.at[n]
                ).start()

            n = n + live.astype(jnp.int32)
    for u in range(UNROLL - 1):
        rows[n + u], places[n + u] = dummy
    return n


def slot_products(n, adj_ref, adj_vmem, adj_sem, product, add_to):
    @pl.loop(0, (n + UNROLL - 1) >> 2)
    def _(step):
        slots = [step * UNROLL + u for u in range(UNROLL)]
        for j in slots:

            @pl.when(j < n)
            def _(j=j):
                pltpu.make_async_copy(adj_ref.at[0], adj_vmem.at[j], adj_sem.at[j]).wait()

        values = [product(j) for j in slots]
        for j, value in zip(slots, values):
            add_to(j, value)


def forward_near_kernel(*refs):
    lists, (adj0, adj1), refs = refs[:4], refs[4:6], refs[6:]
    pieces, (acc, panel, adj_vmem, rows, places, panel_sem, adj_sem) = refs[:7], refs[7:]
    copies = [
        pltpu.make_async_copy(piece, panel.at[pl.ds(place * QUAD, QUAD)], panel_sem.at[place])
        for place, piece in zip((0, 1, 2, 3, 5, 6, 7), pieces)
    ]
    for copy in copies:
        copy.start()
    n = list_slots(lists, (adj0, adj1), adj_vmem, adj_sem, rows, places, False, (16, 0))
    acc[...] = jnp.zeros_like(acc)
    for copy in copies:
        copy.wait()

    def product(j):
        return jnp.dot(adj_vmem[j], panel[places[j]], preferred_element_type=jnp.float32)

    def add_to(j, value):
        acc[rows[j]] += value

    slot_products(n, adj0, adj_vmem, adj_sem, product, add_to)


def forward_far_kernel(*refs):
    lists, refs = refs[:4], refs[4:]
    adj0, adj1, near, far, out, acc, adj_vmem, rows, places, adj_sem = refs
    n = list_slots(lists, (adj0, adj1), adj_vmem, adj_sem, rows, places, True, (16, 16))
    acc[...] = near[...]

    def product(j):
        return jnp.dot(adj_vmem[j], far[places[j] - 16], preferred_element_type=jnp.float32)

    def add_to(j, value):
        acc[rows[j]] += value

    slot_products(n, adj0, adj_vmem, adj_sem, product, add_to)
    for row in range(8):
        for i in range(2):
            out[row, i] = acc[2 * row + i].astype(jnp.bfloat16)


def backward_kernel(far, *refs):
    lists, refs = refs[:4], refs[4:]
    adj0, adj1, back, out, acc, adj_vmem, rows, places, adj_sem = refs
    base = 16 if far else 0
    spare = acc.shape[0] - 1
    n = list_slots(
        lists, (adj0, adj1), adj_vmem, adj_sem, rows, places, far, (0, base + spare)
    )
    acc[...] = jnp.zeros_like(acc)

    def product(j):
        row = rows[j]
        return lax.dot_general(
            adj_vmem[j],
            back[row >> 1, pl.ds((row & 1) * TILE, TILE), :],
            (((0,), (0,)), ((), ())),
            preferred_element_type=jnp.float32,
        )

    def add_to(j, value):
        acc[places[j] - base] += value

    slot_products(n, adj0, adj_vmem, adj_sem, product, add_to)
    if not far:
        out[...] = acc[:spare].astype(jnp.bfloat16)
        return
    for k in range(QUAD):
        out[k * TILE : (k + 1) * TILE, :] = acc[k].astype(jnp.bfloat16)
    piece = back[0, 2 * TILE :, :].astype(jnp.float32)
    for c in range(1, NCOL):
        piece = piece + back[c, 2 * TILE :, :].astype(jnp.float32)
    out[QUAD * TILE :, :] = piece.astype(jnp.bfloat16)


def split(x):
    high = x.astype(jnp.bfloat16)
    return high, (x - high.astype(jnp.float32)).astype(jnp.bfloat16)


def dense_kernel(agg_own, agg_other, weight, cot_own, cot_other, act_out, send_out):
    first = (lax.axis_index("row") & 1) == 0
    own = agg_own[...]
    other = jnp.concatenate([agg_other[TILE:, :], agg_other[:TILE, :]], axis=0)
    w = weight[...]
    w_other_half = jnp.where(first, w[HALF:], w[:HALF])
    w_half = jnp.where(first, w[:HALF], w[HALF:])

    def dot(a, b, dims=((1,), (0,))):
        return lax.dot_general(a, b, (dims, ((), ())), preferred_element_type=jnp.float32)

    own_hi, own_lo = split(own)
    other_hi, other_lo = split(other)
    v = (dot(own_hi, w_half) + dot(own_lo, w_half)) + (
        dot(other_hi, w_other_half) + dot(other_lo, w_other_half)
    )
    scale = math.sqrt(2.0 / math.pi)
    square = v * v
    t = jnp.tanh(scale * (v + 0.044715 * (square * v)))
    cdf = 0.5 * (1.0 + t)
    act_out[...] = (v[:TILE] * cdf[:TILE]).astype(jnp.bfloat16)
    slope = cdf + 0.5 * v * ((1.0 - t) * (1.0 + t)) * (scale * (1.0 + 3.0 * 0.044715 * square))
    cot = jnp.concatenate([cot_own[...], cot_other[...]], axis=0).astype(jnp.float32)
    grad_hi, grad_lo = split(cot * slope)
    nodes = ((1,), (1,))
    back = (dot(grad_hi, w_half, nodes) + dot(grad_lo, w_half, nodes)).astype(jnp.bfloat16)
    rows = ((0,), (0,))
    w_part = (
        dot(own_hi, grad_hi, rows) + dot(own_lo, grad_hi, rows) + dot(own_hi, grad_lo, rows)
    ).astype(jnp.bfloat16)
    for c in range(NCOL):
        send_out[c, : 2 * TILE, :] = back
        piece = w_part[64 * (c // 4) : 64 * (c // 4) + 64]
        send_out[c, 2 * TILE : 2 * TILE + 64, :] = piece[:, :HALF]
        send_out[c, 2 * TILE + 64 :, :] = piece[:, HALF:]


def sum_kernel(parts, own, got1, up2, up3, up4, down2, down3, down4, kept, *refs):
    messages, by_step = refs[:3], refs[3]
    device = lax.axis_index("row")
    z, core = device >> 2, device & 1
    size = QUAD * TILE
    by_step[0] = own[size:, :]

    @pl.when(core == 0)
    def _():
        for k, ref in enumerate((down2, down3, down4, up4, up3, up2, got1)):
            by_step[k + 1] = ref[size:, :]

    @pl.when(core == 1)
    def _():
        for k, ref in enumerate((got1, down2, down3, down4, up4, up3, up2)):
            by_step[k + 1] = ref[size:, :]

    w_sum = by_step[(0 - z) & 7].astype(jnp.float32)
    for a in range(1, NZ):
        w_sum = w_sum + by_step[(a - z) & 7].astype(jnp.float32)
    w_send = w_sum.astype(jnp.bfloat16)
    for k in range(QUAD):
        rows = pl.ds(k * TILE, TILE)
        total = (
            parts[k].astype(jnp.float32)
            + up4[rows, :].astype(jnp.float32)
            + down4[rows, :].astype(jnp.float32)
        )
        if k == 0:
            kept[...] = total
        else:
            messages[k - 1][:TILE, :] = total.astype(jnp.bfloat16)
            messages[k - 1][TILE:, :] = w_send


def last_kernel(kept, sent, from_core, from_x, from_both, grad_out, w_out):
    core = lax.axis_index("row") & 1

    def f32(ref, rows):
        return ref[rows, :].astype(jnp.float32)

    grads, pieces = pl.ds(0, TILE), pl.ds(TILE, W_ROWS)
    mine = (kept[...] + f32(from_x, grads)).astype(jnp.bfloat16)
    theirs = (f32(from_core, grads) + f32(from_both, grads)).astype(jnp.bfloat16)
    w_mine = f32(sent, pieces) + f32(from_x, pieces)
    w_theirs = f32(from_core, pieces) + f32(from_both, pieces)

    @pl.when(core == 0)
    def _():
        grad_out[:, :HALF] = mine
        grad_out[:, HALF:] = theirs

    @pl.when(core == 1)
    def _():
        grad_out[:, HALF:] = mine
        grad_out[:, :HALF] = theirs

    w_out[core] = w_mine
    w_out[1 - core] = w_theirs


def weight_kernel(here, there, out):
    x = lax.axis_index("col") >> 2
    scale = 1.0 / 256.0

    def place(ref, x_lo):
        for core in range(2):
            rows = pl.ds(core * HALF + x_lo * 64, 64)
            out[rows, :HALF] = ref[core, :64, :] * scale
            out[rows, HALF:] = ref[core, 64:, :] * scale

    @pl.when(x == 0)
    def _():
        place(here, 0)
        place(there, 1)

    @pl.when(x == 1)
    def _():
        place(there, 0)
        place(here, 1)


SMEM = pl.BlockSpec(memory_space=pltpu.SMEM)
VMEM = pl.BlockSpec(memory_space=pltpu.VMEM)
ANY = pl.BlockSpec(memory_space=pl.ANY)


def params(mib):
    return pltpu.CompilerParams(vmem_limit_bytes=mib << 20)


LIST = 2 * SLOTS + UNROLL
SLOT_SCRATCH = [
    pltpu.VMEM((LIST, TILE, TILE), jnp.bfloat16),
    pltpu.SMEM((LIST,), jnp.int32),
    pltpu.SMEM((LIST,), jnp.int32),
]


def cost(slots, size):
    return pl.CostEstimate(
        flops=slots * 2 * TILE * TILE * HALF, bytes_accessed=size << 20, transcendentals=0
    )


LISTS = [SMEM] * 4


def local(kernel, out_shape, n_in, mib=20, scratch=(), name=None, scalars=0, any_in=0, cost=None):
    n_out = len(out_shape) if isinstance(out_shape, tuple) else None
    return pl.pallas_call(
        kernel,
        out_shape=out_shape,
        in_specs=[SMEM] * scalars + [ANY] * any_in + [VMEM] * (n_in - scalars - any_in),
        out_specs=(VMEM,) * n_out if n_out else VMEM,
        scratch_shapes=scratch,
        compiler_params=params(mib),
        cost_estimate=cost,
        name=name,
    )


def shape(*dims, dtype=jnp.bfloat16):
    return jax.ShapeDtypeStruct(dims, dtype)


def prepare(rows, cols, count, block):
    return local(
        prepare_kernel,
        (shape(TILE, HALF), shape(TILE + 16, HALF)),
        4,
        scalars=3,
        name="prepare",
    )(rows, cols, count, block)


def forward_near(lists, adj0, adj1, pieces):
    return local(
        forward_near_kernel,
        shape(17, TILE, HALF, dtype=jnp.float32),
        13,
        scalars=4,
        any_in=9,
        scratch=[pltpu.VMEM((NZ * QUAD, TILE, HALF), jnp.bfloat16)]
        + SLOT_SCRATCH
        + [pltpu.SemaphoreType.DMA((NZ,)), pltpu.SemaphoreType.DMA((LIST,))],
        cost=cost(21, 6),
        name="forward_near",
    )(*lists, adj0, adj1, *pieces)


def forward_far(lists, adj0, adj1, near, far):
    return local(
        forward_far_kernel,
        shape(8, 2, TILE, HALF),
        8,
        scalars=4,
        any_in=2,
        scratch=[pltpu.VMEM((17, TILE, HALF), jnp.float32)]
        + SLOT_SCRATCH
        + [pltpu.SemaphoreType.DMA((LIST,))],
        cost=cost(3, 4),
        name="forward_far",
    )(*lists, adj0, adj1, near, far)


def backward_tiles(lists, adj0, adj1, back, far):
    places = QUAD if far else NZ * QUAD
    return local(
        functools.partial(backward_kernel, far),
        shape(QUAD * TILE + W_ROWS, HALF) if far else shape(places, TILE, HALF),
        7,
        scalars=4,
        any_in=2,
        scratch=[pltpu.VMEM((places + 1, TILE, HALF), jnp.float32)]
        + SLOT_SCRATCH
        + [pltpu.SemaphoreType.DMA((LIST,))],
        cost=cost(3, 2) if far else cost(21, 6),
        name="backward_far" if far else "backward_near",
    )(*lists, adj0, adj1, back)


def dense(agg_own, agg_other, weight, cot_own, cot_other):
    return local(
        dense_kernel,
        (shape(TILE, 2 * HALF), shape(NCOL, 2 * TILE + W_ROWS, HALF)),
        5,
        name="dense",
    )(agg_own, agg_other, weight, cot_own, cot_other)


def ring_end(parts, messages):
    message = shape(TILE + W_ROWS, HALF)
    return local(
        sum_kernel,
        (shape(TILE, HALF, dtype=jnp.float32), message, message, message),
        9,
        scratch=[pltpu.VMEM((NZ, W_ROWS, HALF), jnp.bfloat16)],
        name="ring_end",
    )(parts, *messages)


def last(kept, sent, from_core, from_x, from_both):
    return local(
        last_kernel,
        (shape(TILE, 2 * HALF), shape(2, W_ROWS, HALF, dtype=jnp.float32)),
        5,
        name="last",
    )(kept, sent, from_core, from_x, from_both)


def weight_places(here, there):
    return local(
        weight_kernel, shape(2 * HALF, 2 * HALF, dtype=jnp.float32), 2, name="weight_places"
    )(here, there)


def z_both(x):
    return lax.ppermute(
        x, "row", row_pairs(lambda z, q: (z + 1 - 2 * (q & 1), q))
    )


def add(a, b):
    return (a.astype(jnp.float32) + b.astype(jnp.float32)).astype(jnp.bfloat16)


def per_device(features, adj_tiles, tile_row, tile_col, tile_count, weight, cotangent):
    first = (lax.axis_index("row") & 1) == 0
    adj0 = adj_tiles[0, 0]
    own_lists = (tile_row[0, 0], tile_col[0, 0], tile_count[0])

    mine, theirs = prepare(*own_lists, features[0])
    from_core = quad_permute(theirs, 1)
    from_both = quad_permute(theirs, 3)
    chunk = jnp.stack([mine, from_core[:TILE], quad_permute(mine, 2), from_both[:TILE]])
    lists = own_lists + (from_core[TILE, :25].astype(jnp.int32),)
    adj1 = quad_permute(adj0, 1)
    cot1 = quad_permute(cotangent, 1)

    up1, down1 = z_shift(chunk, 1), z_shift(chunk, -1)
    up2, down2 = z_shift(up1, 1), z_shift(down1, -1)
    up3, down3 = z_shift(up2, 1), z_shift(down2, -1)
    far = z_both(jnp.where(first, up3, down3))
    near = forward_near(lists, adj0, adj1, [chunk, down1, down2, down3, up3, up2, up1])
    partial = forward_far(lists, adj0, adj1, near, far)

    shares = lax.all_to_all(partial, "col", 0, 0, tiled=True)
    agg = shares.reshape(NCOL, 2 * TILE, HALF).astype(jnp.float32).sum(axis=0)
    agg_other = quad_permute(agg, 1)
    activated, send = dense(agg, agg_other, weight, cotangent, cot1)
    received = lax.all_to_all(send, "col", 0, 0, tiled=True)

    size = QUAD * TILE
    far_part = backward_tiles(lists, adj0, adj1, received, True)
    blocks = backward_tiles(lists, adj0, adj1, received, False)
    parts = blocks.reshape(NZ, size, HALF)

    def pack(part, message, piece):
        return jnp.concatenate([add(part, message), piece], axis=0)

    w_piece = far_part[size:]
    got1 = z_both(far_part)
    zero = jnp.zeros((size, HALF), jnp.bfloat16)
    up = pack(
        parts[3], jnp.where(first, got1[:size], zero), jnp.where(first, got1[size:], w_piece)
    )
    down = pack(
        parts[5], jnp.where(first, zero, got1[:size]), jnp.where(first, w_piece, got1[size:])
    )
    up2, down2 = z_shift(up, 1), z_shift(down, -1)
    up3 = z_shift(pack(parts[2], up2[:size], up2[size:]), 1)
    down3 = z_shift(pack(parts[6], down2[:size], down2[size:]), -1)
    up4 = z_shift(pack(parts[1], up3[:size], up3[size:]), 1)
    down4 = z_shift(pack(parts[7], down3[:size], down3[size:]), -1)

    kept, to_core, to_x, to_both = ring_end(
        blocks, (far_part, got1, up2, up3, up4, down2, down3, down4)
    )
    grad, w_here = last(
        kept, to_core, quad_permute(to_core, 1), quad_permute(to_x, 2), quad_permute(to_both, 3)
    )
    w_there = lax.ppermute(w_here, "col", [(c, c ^ 4) for c in range(NCOL)])
    return (activated, weight_places(w_here, w_there), grad[None])


def solution(mesh):
    return jax.shard_map(
        per_device,
        mesh=mesh,
        in_specs=(
            P("col", "row", None),
            P("row", "col", None, None, None),
            P("row", "col", None),
            P("row", "col", None),
            P("row", "col"),
            P(),
            P(("row", "col"), None),
        ),
        out_specs=(P(("row", "col"), None), P(), P("col", "row", None)),
        check_vma=False,
    )
```

```python
import functools
import math

import jax
import jax.numpy as jnp
from jax import lax
from jax.experimental import pallas as pl
from jax.experimental.pallas import tpu as pltpu
from jax.sharding import PartitionSpec as P

NZ = 8
QUAD = 4
NCOL = 8
TILE = 256
HALF = 128
SLOTS = 12
W_ROWS = 128
UNROLL = 4


def row_pairs(move):
    pairs = []
    for r in range(NZ * QUAD):
        z, q = move(r // QUAD, r % QUAD)
        pairs.append((r, (z % NZ) * QUAD + q))
    return pairs


def quad_permute(x, flip):
    return lax.ppermute(x, "row", row_pairs(lambda z, q: (z, q ^ flip)))


def z_shift(x, step):
    return lax.ppermute(x, "row", row_pairs(lambda z, q: (z + step, q)))


def prepare_kernel(rows, cols, count, block, keep, message, own_lists):
    core = lax.axis_index("row") & 1

    @pl.when(core == 0)
    def _():
        keep[...] = block[:, :HALF]
        message[16:, :] = block[:, HALF:]

    @pl.when(core == 1)
    def _():
        keep[...] = block[:, HALF:]
        message[16:, :] = block[:, :HALF]

    lane = lax.broadcasted_iota(jnp.int32, (16, HALF), 1)
    values = jnp.zeros((16, HALF), jnp.float32)
    listed = [rows[s] for s in range(SLOTS)] + [cols[s] for s in range(SLOTS)] + [count[0, 0]]
    for n, value in enumerate(listed):
        values = jnp.where(lane == n, value.astype(jnp.float32), values)
        own_lists[n] = value
    message[:16, :] = values.astype(jnp.bfloat16)


def join_kernel(own_keep, own_message, x_block, keep, message):
    core = lax.axis_index("row") & 1
    keep[0] = own_keep[...]
    message[: TILE + 16, :] = own_message[...]

    @pl.when(core == 0)
    def _():
        keep[1] = x_block[:, :HALF]
        message[TILE + 16 :, :] = x_block[:, HALF:]

    @pl.when(core == 1)
    def _():
        keep[1] = x_block[:, HALF:]
        message[TILE + 16 :, :] = x_block[:, :HALF]


def list_slots(lists, adj_refs, adj_vmem, adj_sem, rows, places, far, dummy):
    device = lax.axis_index("row")
    z, q = device >> 2, device & 3
    n = jnp.int32(0)
    for i in range(2):
        count = lists[i][24]
        for s in range(SLOTS):
            tile = lists[i][12 + s]
            row = lists[i][s]
            other = (tile & 3) ^ q
            place = (((tile >> 2) - z) & 7) * QUAD + ((other & 1) * 2 + (other >> 1))
            live = (s < count) & (((place >> 2) == 4) == far)
            rows[n] = row * 2 + i
            places[n] = place

            @pl.when(live)
            def _(i=i, s=s, n=n):
                pltpu.make_async_copy(
                    adj_refs[i].at[s], adj_vmem.at[n], adj_sem.at[n]
                ).start()

            n = n + live.astype(jnp.int32)
    for u in range(UNROLL - 1):
        rows[n + u], places[n + u] = dummy
    return n


def slot_products(n, adj_ref, adj_vmem, adj_sem, product, add_to):
    @pl.loop(0, (n + UNROLL - 1) >> 2)
    def _(step):
        slots = [step * UNROLL + u for u in range(UNROLL)]
        for j in slots:

            @pl.when(j < n)
            def _(j=j):
                pltpu.make_async_copy(adj_ref.at[0], adj_vmem.at[j], adj_sem.at[j]).wait()

        values = [product(j) for j in slots]
        for j, value in zip(slots, values):
            add_to(j, value)


def forward_near_kernel(*refs):
    lists, (adj0, adj1), refs = refs[:2], refs[2:4], refs[4:]
    pieces, (acc, panel, adj_vmem, rows, places, panel_sem, adj_sem) = refs[:7], refs[7:]
    copies = [
        pltpu.make_async_copy(piece, panel.at[pl.ds(place * QUAD, QUAD)], panel_sem.at[place])
        for place, piece in zip((0, 1, 2, 3, 5, 6, 7), pieces)
    ]
    for copy in copies:
        copy.start()
    n = list_slots(lists, (adj0, adj1), adj_vmem, adj_sem, rows, places, False, (16, 0))
    acc[...] = jnp.zeros_like(acc)
    for copy in copies:
        copy.wait()

    def product(j):
        return jnp.dot(adj_vmem[j], panel[places[j]], preferred_element_type=jnp.float32)

    def add_to(j, value):
        acc[rows[j]] += value

    slot_products(n, adj0, adj_vmem, adj_sem, product, add_to)


def forward_far_kernel(*refs):
    lists, refs = refs[:2], refs[2:]
    adj0, adj1, near, far_a, far_b, out, acc, far, adj_vmem, rows, places, adj_sem = refs
    n = list_slots(lists, (adj0, adj1), adj_vmem, adj_sem, rows, places, True, (16, 16))
    far[:2] = far_a[...]
    far[2:] = far_b[...]
    acc[...] = near[...]

    def product(j):
        return jnp.dot(adj_vmem[j], far[places[j] - 16], preferred_element_type=jnp.float32)

    def add_to(j, value):
        acc[rows[j]] += value

    slot_products(n, adj0, adj_vmem, adj_sem, product, add_to)
    for row in range(8):
        for i in range(2):
            out[row, i] = acc[2 * row + i].astype(jnp.bfloat16)


def backward_kernel(far, *refs):
    lists, refs = refs[:2], refs[2:]
    adj0, adj1, back = refs[:3]
    acc, adj_vmem, rows, places, adj_sem = refs[-5:]
    outs = refs[3:-5]
    base = 16 if far else 0
    spare = acc.shape[0] - 1
    n = list_slots(
        lists, (adj0, adj1), adj_vmem, adj_sem, rows, places, far, (0, base + spare)
    )
    acc[...] = jnp.zeros_like(acc)

    def product(j):
        row = rows[j]
        return lax.dot_general(
            adj_vmem[j],
            back[row >> 1, pl.ds((row & 1) * TILE, TILE), :],
            (((0,), (0,)), ((), ())),
            preferred_element_type=jnp.float32,
        )

    def add_to(j, value):
        acc[places[j] - base] += value

    slot_products(n, adj0, adj_vmem, adj_sem, product, add_to)
    if not far:
        outs[0][...] = acc[:spare].astype(jnp.bfloat16)
        return
    for k in range(QUAD):
        rows = pl.ds((k & 1) * TILE, TILE)
        outs[k >> 1][rows, :] = acc[k].astype(jnp.bfloat16)
    piece = back[0, 2 * TILE :, :].astype(jnp.float32)
    for c in range(1, NCOL):
        piece = piece + back[c, 2 * TILE :, :].astype(jnp.float32)
    for out in outs:
        out[2 * TILE :, :] = piece.astype(jnp.bfloat16)


def split(x):
    high = x.astype(jnp.bfloat16)
    return high, (x - high.astype(jnp.float32)).astype(jnp.bfloat16)


def dense_kernel(agg_own, agg_other, weight, cot_own, cot_other, act_out, send_out):
    first = (lax.axis_index("row") & 1) == 0
    own = agg_own[...]
    other = jnp.concatenate([agg_other[TILE:, :], agg_other[:TILE, :]], axis=0)
    w = weight[...]
    w_other_half = jnp.where(first, w[HALF:], w[:HALF])
    w_half = jnp.where(first, w[:HALF], w[HALF:])

    def dot(a, b, dims=((1,), (0,))):
        return lax.dot_general(a, b, (dims, ((), ())), preferred_element_type=jnp.float32)

    own_hi, own_lo = split(own)
    other_hi, other_lo = split(other)
    v = (dot(own_hi, w_half) + dot(own_lo, w_half)) + (
        dot(other_hi, w_other_half) + dot(other_lo, w_other_half)
    )
    scale = math.sqrt(2.0 / math.pi)
    square = v * v
    t = jnp.tanh(scale * (v + 0.044715 * (square * v)))
    cdf = 0.5 * (1.0 + t)
    act_out[...] = (v[:TILE] * cdf[:TILE]).astype(jnp.bfloat16)
    slope = cdf + 0.5 * v * ((1.0 - t) * (1.0 + t)) * (scale * (1.0 + 3.0 * 0.044715 * square))
    cot = jnp.concatenate([cot_own[...], cot_other[...]], axis=0).astype(jnp.float32)
    grad_hi, grad_lo = split(cot * slope)
    nodes = ((1,), (1,))
    back = (dot(grad_hi, w_half, nodes) + dot(grad_lo, w_half, nodes)).astype(jnp.bfloat16)
    rows = ((0,), (0,))
    w_part = (
        dot(own_hi, grad_hi, rows) + dot(own_lo, grad_hi, rows) + dot(own_hi, grad_lo, rows)
    ).astype(jnp.bfloat16)
    for c in range(NCOL):
        send_out[c, : 2 * TILE, :] = back
        piece = w_part[64 * (c // 4) : 64 * (c // 4) + 64]
        send_out[c, 2 * TILE : 2 * TILE + 64, :] = piece[:, :HALF]
        send_out[c, 2 * TILE + 64 :, :] = piece[:, HALF:]


def sum_kernel(parts, own, up1, up2, up3, up4, down1, down2, down3, down4, kept, message, by_step):
    z = lax.axis_index("row") >> 2
    size = QUAD * TILE
    by_step[0] = own[2 * TILE :, :]
    by_step[1] = down1[2 * TILE :, :]
    by_step[7] = up1[2 * TILE :, :]
    for k, ref in ((2, down2), (3, down3), (4, up4), (5, up3), (6, up2)):
        by_step[k] = ref[size:, :]
    w_sum = by_step[(0 - z) & 7].astype(jnp.float32)
    for a in range(1, NZ):
        w_sum = w_sum + by_step[(a - z) & 7].astype(jnp.float32)
    message[2 * TILE :, :] = w_sum.astype(jnp.bfloat16)
    for k in range(QUAD):
        rows = pl.ds(k * TILE, TILE)
        total = (
            parts[k].astype(jnp.float32)
            + up4[rows, :].astype(jnp.float32)
            + down4[rows, :].astype(jnp.float32)
        )
        if k & 1:
            message[(k >> 1) * TILE : ((k >> 1) + 1) * TILE, :] = total.astype(jnp.bfloat16)
        else:
            kept[k >> 1] = total


def middle_kernel(kept, sent, from_x, mine, message, w_mine):
    mine[...] = (kept[0] + from_x[:TILE, :].astype(jnp.float32)).astype(jnp.bfloat16)
    message[:TILE, :] = (
        kept[1] + from_x[TILE : 2 * TILE, :].astype(jnp.float32)
    ).astype(jnp.bfloat16)
    w_sum = sent[2 * TILE :, :].astype(jnp.float32) + from_x[2 * TILE :, :].astype(jnp.float32)
    high, low = split(w_sum)
    message[TILE : TILE + W_ROWS, :] = high
    message[TILE + W_ROWS :, :] = low
    w_mine[...] = high.astype(jnp.float32) + low.astype(jnp.float32)


def last_kernel(mine, from_core, w_mine, w_x, w_both, grad_out, w_out):
    core = lax.axis_index("row") & 1
    x_lo = lax.axis_index("col") >> 2
    scale = 1.0 / 256.0
    w_core = from_core[TILE : TILE + W_ROWS, :].astype(jnp.float32) + from_core[
        TILE + W_ROWS :, :
    ].astype(jnp.float32)

    def place(value, start):
        rows = pl.ds(pl.multiple_of(start, 64), 64)
        w_out[rows, :HALF] = value[:64, :] * scale
        w_out[rows, HALF:] = value[64:, :] * scale

    place(w_mine[...], core * HALF + x_lo * 64)
    place(w_x[...], core * HALF + (1 - x_lo) * 64)
    place(w_core, (1 - core) * HALF + x_lo * 64)
    place(w_both[...], (1 - core) * HALF + (1 - x_lo) * 64)

    @pl.when(core == 0)
    def _():
        grad_out[:, :HALF] = mine[...]
        grad_out[:, HALF:] = from_core[:TILE, :]

    @pl.when(core == 1)
    def _():
        grad_out[:, HALF:] = mine[...]
        grad_out[:, :HALF] = from_core[:TILE, :]


SMEM = pl.BlockSpec(memory_space=pltpu.SMEM)
VMEM = pl.BlockSpec(memory_space=pltpu.VMEM)
ANY = pl.BlockSpec(memory_space=pl.ANY)


def params(mib):
    return pltpu.CompilerParams(vmem_limit_bytes=mib << 20)


LIST = 2 * SLOTS + UNROLL
SLOT_SCRATCH = [
    pltpu.VMEM((LIST, TILE, TILE), jnp.bfloat16),
    pltpu.SMEM((LIST,), jnp.int32),
    pltpu.SMEM((LIST,), jnp.int32),
]


def cost(slots, size):
    return pl.CostEstimate(
        flops=slots * 2 * TILE * TILE * HALF, bytes_accessed=size << 20, transcendentals=0
    )


LISTS = [SMEM] * 4


def shape(*dims, dtype=jnp.bfloat16):
    return jax.ShapeDtypeStruct(dims, dtype)


def local(kernel, outs, n_in, name, scalars=0, any_in=0, scratch=(), cost=None, scalar_out=0):
    return pl.pallas_call(
        kernel,
        out_shape=outs,
        in_specs=[SMEM] * scalars + [ANY] * any_in + [VMEM] * (n_in - scalars - any_in),
        out_specs=(VMEM,) * (len(outs) - scalar_out) + (SMEM,) * scalar_out,
        scratch_shapes=scratch,
        compiler_params=params(20),
        cost_estimate=cost,
        name=name,
    )


def prepare(rows, cols, count, block):
    return local(
        prepare_kernel,
        (shape(TILE, HALF), shape(TILE + 16, HALF), shape(25, dtype=jnp.int32)),
        4,
        "prepare",
        scalars=3,
        scalar_out=1,
    )(rows, cols, count, block)


def join(own_keep, own_message, x_block):
    return local(
        join_kernel, (shape(2, TILE, HALF), shape(2 * TILE + 16, HALF)), 3, "join"
    )(own_keep, own_message, x_block)


def forward_near(lists, adj0, adj1, pieces):
    return local(
        forward_near_kernel,
        (shape(17, TILE, HALF, dtype=jnp.float32),),
        11,
        "forward_near",
        scalars=2,
        any_in=9,
        scratch=[pltpu.VMEM((NZ * QUAD, TILE, HALF), jnp.bfloat16)]
        + SLOT_SCRATCH
        + [pltpu.SemaphoreType.DMA((NZ,)), pltpu.SemaphoreType.DMA((LIST,))],
        cost=cost(21, 6),
    )(*lists, adj0, adj1, *pieces)[0]


def forward_far(lists, adj0, adj1, near, far_a, far_b):
    return local(
        forward_far_kernel,
        (shape(8, 2, TILE, HALF),),
        7,
        "forward_far",
        scalars=2,
        any_in=2,
        scratch=[
            pltpu.VMEM((17, TILE, HALF), jnp.float32),
            pltpu.VMEM((QUAD, TILE, HALF), jnp.bfloat16),
        ]
        + SLOT_SCRATCH
        + [pltpu.SemaphoreType.DMA((LIST,))],
        cost=cost(3, 4),
    )(*lists, adj0, adj1, near, far_a, far_b)[0]


def backward_tiles(lists, adj0, adj1, back, far):
    places = QUAD if far else NZ * QUAD
    message = shape(2 * TILE + W_ROWS, HALF)
    return local(
        functools.partial(backward_kernel, far),
        (message, message) if far else (shape(places, TILE, HALF),),
        5,
        "backward_far" if far else "backward_near",
        scalars=2,
        any_in=2,
        scratch=[pltpu.VMEM((places + 1, TILE, HALF), jnp.float32)]
        + SLOT_SCRATCH
        + [pltpu.SemaphoreType.DMA((LIST,))],
        cost=cost(3, 2) if far else cost(21, 6),
    )(*lists, adj0, adj1, back)


def dense(agg_own, agg_other, weight, cot_own, cot_other):
    return local(
        dense_kernel,
        (shape(TILE, 2 * HALF), shape(NCOL, 2 * TILE + W_ROWS, HALF)),
        5,
        "dense",
    )(agg_own, agg_other, weight, cot_own, cot_other)


def ring_end(parts, *messages):
    return local(
        sum_kernel,
        (shape(2, TILE, HALF, dtype=jnp.float32), shape(2 * TILE + W_ROWS, HALF)),
        10,
        "ring_end",
        scratch=[pltpu.VMEM((NZ, W_ROWS, HALF), jnp.bfloat16)],
    )(parts, *messages)


def middle(kept, sent, from_x):
    return local(
        middle_kernel,
        (
            shape(TILE, HALF),
            shape(TILE + 2 * W_ROWS, HALF),
            shape(W_ROWS, HALF, dtype=jnp.float32),
        ),
        3,
        "middle",
    )(kept, sent, from_x)


def last(mine, from_core, w_mine, w_x, w_both):
    return local(
        last_kernel,
        (shape(TILE, 2 * HALF), shape(2 * HALF, 2 * HALF, dtype=jnp.float32)),
        5,
        "last",
    )(mine, from_core, w_mine, w_x, w_both)


def add(a, b):
    return (a.astype(jnp.float32) + b.astype(jnp.float32)).astype(jnp.bfloat16)


def per_device(features, adj_tiles, tile_row, tile_col, tile_count, weight, cotangent):
    adj0 = adj_tiles[0, 0]
    block = features[0]

    x_block = quad_permute(block, 2)
    keep, message, own_lists = prepare(tile_row[0, 0], tile_col[0, 0], tile_count, block)
    keep, message = join(keep, message, x_block)
    from_core = quad_permute(message, 1)
    chunk = jnp.concatenate([keep, from_core[16:].reshape(2, TILE, HALF)], axis=0)
    lists = (own_lists, from_core[0, :25].astype(jnp.int32))
    adj1 = quad_permute(adj0, 1)
    cot1 = quad_permute(cotangent, 1)

    up1, down1 = z_shift(chunk, 1), z_shift(chunk, -1)
    up2, down2 = z_shift(up1, 1), z_shift(down1, -1)
    up3, down3 = z_shift(up2, 1), z_shift(down2, -1)
    far_a, far_b = z_shift(up3[:2], 1), z_shift(down3[2:], -1)
    near = forward_near(lists, adj0, adj1, [chunk, down1, down2, down3, up3, up2, up1])
    partial = forward_far(lists, adj0, adj1, near, far_a, far_b)

    shares = lax.all_to_all(partial, "col", 0, 0, tiled=True)
    agg = shares.reshape(NCOL, 2 * TILE, HALF).astype(jnp.float32).sum(axis=0)
    agg_other = quad_permute(agg, 1)
    activated, send = dense(agg, agg_other, weight, cotangent, cot1)
    received = lax.all_to_all(send, "col", 0, 0, tiled=True)

    half, size = 2 * TILE, QUAD * TILE
    own, own_down = backward_tiles(lists, adj0, adj1, received, True)
    (blocks,) = backward_tiles(lists, adj0, adj1, received, False)
    parts = blocks.reshape(NZ, size, HALF)
    up1, down1 = z_shift(own, 1), z_shift(own_down, -1)
    up = [add(parts[3, :half], up1[:half]), parts[3, half:], up1[half:]]
    down = [parts[5, :half], add(parts[5, half:], down1[:half]), down1[half:]]
    up2, down2 = z_shift(jnp.concatenate(up), 1), z_shift(jnp.concatenate(down), -1)
    up = [add(parts[2], up2[:size]), up2[size:]]
    down = [add(parts[6], down2[:size]), down2[size:]]
    up3, down3 = z_shift(jnp.concatenate(up), 1), z_shift(jnp.concatenate(down), -1)
    up4 = z_shift(jnp.concatenate([add(parts[1], up3[:size]), up3[size:]]), 1)
    down4 = z_shift(add(parts[7], down3[:size]), -1)

    kept, to_x = ring_end(blocks, own, up1, up2, up3, up4, down1, down2, down3, down4)
    mine, to_core, w_mine = middle(kept, to_x, quad_permute(to_x, 2))
    across = [(c, c ^ 4) for c in range(NCOL)]
    both = [
        (r * NCOL + c, (r ^ 1) * NCOL + (c ^ 4)) for r in range(NZ * QUAD) for c in range(NCOL)
    ]
    w_x = lax.ppermute(w_mine, "col", across)
    w_both = lax.ppermute(w_mine, ("row", "col"), both)
    grad, weight_grad = last(mine, quad_permute(to_core, 1), w_mine, w_x, w_both)
    return (activated, weight_grad, grad[None])


def solution(mesh):
    return jax.shard_map(
        per_device,
        mesh=mesh,
        in_specs=(
            P("col", "row", None),
            P("row", "col", None, None, None),
            P("row", "col", None),
            P("row", "col", None),
            P("row", "col"),
            P(),
            P(("row", "col"), None),
        ),
        out_specs=(P(("row", "col"), None), P(), P("col", "row", None)),
        check_vma=False,
    )
```

```python
import functools
import math

import jax
import jax.numpy as jnp
from jax import lax
from jax.experimental import pallas as pl
from jax.experimental.pallas import tpu as pltpu
from jax.sharding import PartitionSpec as P

NZ = 8
QUAD = 4
NCOL = 8
TILE = 256
HALF = 128
SLOTS = 12
W_ROWS = 128
UNROLL = 4


def row_pairs(move):
    pairs = []
    for r in range(NZ * QUAD):
        z, q = move(r // QUAD, r % QUAD)
        pairs.append((r, (z % NZ) * QUAD + q))
    return pairs


def quad_permute(x, flip):
    return lax.ppermute(x, "row", row_pairs(lambda z, q: (z, q ^ flip)))


def z_shift(x, step):
    return lax.ppermute(x, "row", row_pairs(lambda z, q: (z + step, q)))


def prepare_kernel(rows, cols, count, block, keep, message, own_lists):
    core = lax.axis_index("row") & 1

    @pl.when(core == 0)
    def _():
        keep[...] = block[:, :HALF]
        message[16:, :] = block[:, HALF:]

    @pl.when(core == 1)
    def _():
        keep[...] = block[:, HALF:]
        message[16:, :] = block[:, :HALF]

    lane = lax.broadcasted_iota(jnp.int32, (16, HALF), 1)
    values = jnp.zeros((16, HALF), jnp.float32)
    listed = [rows[s] for s in range(SLOTS)] + [cols[s] for s in range(SLOTS)] + [count[0, 0]]
    for n, value in enumerate(listed):
        values = jnp.where(lane == n, value.astype(jnp.float32), values)
        own_lists[n] = value
    message[:16, :] = values.astype(jnp.bfloat16)


def join_kernel(own_keep, own_message, x_block, keep, message):
    core = lax.axis_index("row") & 1
    keep[0] = own_keep[...]
    message[: TILE + 16, :] = own_message[...]

    @pl.when(core == 0)
    def _():
        keep[1] = x_block[:, :HALF]
        message[TILE + 16 :, :] = x_block[:, HALF:]

    @pl.when(core == 1)
    def _():
        keep[1] = x_block[:, HALF:]
        message[TILE + 16 :, :] = x_block[:, :HALF]


def list_slots(lists, adj_refs, adj_vmem, adj_sem, rows, places, far, dummy):
    device = lax.axis_index("row")
    z, q = device >> 2, device & 3
    n = jnp.int32(0)
    for i in range(2):
        count = lists[i][24]
        for s in range(SLOTS):
            tile = lists[i][12 + s]
            row = lists[i][s]
            place = (((tile >> 2) - z) & 7) * QUAD + ((tile & 3) ^ q)
            live = (s < count) & (((place >> 2) == 4) == far)
            rows[n] = row * 2 + i
            places[n] = place

            @pl.when(live)
            def _(i=i, s=s, n=n):
                pltpu.make_async_copy(
                    adj_refs[i].at[s], adj_vmem.at[n], adj_sem.at[n]
                ).start()

            n = n + live.astype(jnp.int32)
    for u in range(UNROLL - 1):
        rows[n + u], places[n + u] = dummy
    return n


def slot_products(n, adj_ref, adj_vmem, adj_sem, product, add_to):
    @pl.loop(0, (n + UNROLL - 1) >> 2)
    def _(step):
        slots = [step * UNROLL + u for u in range(UNROLL)]
        for j in slots:

            @pl.when(j < n)
            def _(j=j):
                pltpu.make_async_copy(adj_ref.at[0], adj_vmem.at[j], adj_sem.at[j]).wait()

        values = [product(j) for j in slots]
        for j, value in zip(slots, values):
            add_to(j, value)


def forward_near_kernel(*refs):
    lists, (adj0, adj1), refs = refs[:2], refs[2:4], refs[4:]
    pieces, (acc, panel, adj_vmem, rows, places, panel_sem, adj_sem) = refs[:7], refs[7:]
    copies = [
        pltpu.make_async_copy(piece, panel.at[pl.ds(place * QUAD, QUAD)], panel_sem.at[place])
        for place, piece in zip((0, 1, 2, 3, 5, 6, 7), pieces)
    ]
    for copy in copies:
        copy.start()
    n = list_slots(lists, (adj0, adj1), adj_vmem, adj_sem, rows, places, False, (16, 0))
    acc[...] = jnp.zeros_like(acc)
    for copy in copies:
        copy.wait()

    def product(j):
        return jnp.dot(adj_vmem[j], panel[places[j]], preferred_element_type=jnp.float32)

    def add_to(j, value):
        acc[rows[j]] += value

    slot_products(n, adj0, adj_vmem, adj_sem, product, add_to)


def forward_far_kernel(*refs):
    lists, refs = refs[:2], refs[2:]
    adj0, adj1, near, far_a, far_b, out, acc, far, adj_vmem, rows, places, adj_sem = refs
    n = list_slots(lists, (adj0, adj1), adj_vmem, adj_sem, rows, places, True, (16, 16))
    far[:2] = far_a[...]
    far[2:] = far_b[...]
    acc[...] = near[...]

    def product(j):
        return jnp.dot(adj_vmem[j], far[places[j] - 16], preferred_element_type=jnp.float32)

    def add_to(j, value):
        acc[rows[j]] += value

    slot_products(n, adj0, adj_vmem, adj_sem, product, add_to)
    for row in range(8):
        for i in range(2):
            out[row, i] = acc[2 * row + i].astype(jnp.bfloat16)


def backward_kernel(far, *refs):
    lists, refs = refs[:2], refs[2:]
    adj0, adj1, back = refs[:3]
    acc, adj_vmem, rows, places, adj_sem = refs[-5:]
    outs = refs[3:-5]
    base = 16 if far else 0
    spare = acc.shape[0] - 1
    n = list_slots(
        lists, (adj0, adj1), adj_vmem, adj_sem, rows, places, far, (0, base + spare)
    )
    acc[...] = jnp.zeros_like(acc)

    def product(j):
        row = rows[j]
        return lax.dot_general(
            adj_vmem[j],
            back[row >> 1, pl.ds((row & 1) * TILE, TILE), :],
            (((0,), (0,)), ((), ())),
            preferred_element_type=jnp.float32,
        )

    def add_to(j, value):
        acc[places[j] - base] += value

    slot_products(n, adj0, adj_vmem, adj_sem, product, add_to)
    if not far:
        outs[0][...] = acc[:spare].astype(jnp.bfloat16)
        return
    for k in range(QUAD):
        rows = pl.ds((k & 1) * TILE, TILE)
        outs[k >> 1][rows, :] = acc[k].astype(jnp.bfloat16)
    piece = back[0, 2 * TILE :, :].astype(jnp.float32)
    for c in range(1, NCOL):
        piece = piece + back[c, 2 * TILE :, :].astype(jnp.float32)
    for out in outs:
        out[2 * TILE :, :] = piece.astype(jnp.bfloat16)


def split(x):
    high = x.astype(jnp.bfloat16)
    return high, (x - high.astype(jnp.float32)).astype(jnp.bfloat16)


def dense_kernel(agg_own, agg_other, weight, cot_own, cot_other, act_out, send_out):
    first = (lax.axis_index("row") & 1) == 0
    own = agg_own[...]
    other = jnp.concatenate([agg_other[TILE:, :], agg_other[:TILE, :]], axis=0)
    w = weight[...]
    w_other_half = jnp.where(first, w[HALF:], w[:HALF])
    w_half = jnp.where(first, w[:HALF], w[HALF:])

    def dot(a, b, dims=((1,), (0,))):
        return lax.dot_general(a, b, (dims, ((), ())), preferred_element_type=jnp.float32)

    own_hi, own_lo = split(own)
    other_hi, other_lo = split(other)
    v = (dot(own_hi, w_half) + dot(own_lo, w_half)) + (
        dot(other_hi, w_other_half) + dot(other_lo, w_other_half)
    )
    scale = math.sqrt(2.0 / math.pi)
    square = v * v
    t = jnp.tanh(scale * (v + 0.044715 * (square * v)))
    cdf = 0.5 * (1.0 + t)
    act_out[...] = (v[:TILE] * cdf[:TILE]).astype(jnp.bfloat16)
    slope = cdf + 0.5 * v * ((1.0 - t) * (1.0 + t)) * (scale * (1.0 + 3.0 * 0.044715 * square))
    cot = jnp.concatenate([cot_own[...], cot_other[...]], axis=0).astype(jnp.float32)
    grad_hi, grad_lo = split(cot * slope)
    nodes = ((1,), (1,))
    back = (dot(grad_hi, w_half, nodes) + dot(grad_lo, w_half, nodes)).astype(jnp.bfloat16)
    rows = ((0,), (0,))
    w_part = (
        dot(own_hi, grad_hi, rows) + dot(own_lo, grad_hi, rows) + dot(own_hi, grad_lo, rows)
    ).astype(jnp.bfloat16)
    for c in range(NCOL):
        send_out[c, : 2 * TILE, :] = back
        piece = w_part[64 * (c // 4) : 64 * (c // 4) + 64]
        send_out[c, 2 * TILE : 2 * TILE + 64, :] = piece[:, :HALF]
        send_out[c, 2 * TILE + 64 :, :] = piece[:, HALF:]


def f32(ref, start, rows=TILE):
    return ref[start : start + rows, :].astype(jnp.float32)


def away_kernel(parts, own, up1, up2, up3, up4, down1, down2, down3, down4, message, w_z):
    z = lax.axis_index("row") >> 2
    half, size = 2 * TILE, QUAD * TILE
    by_step = (
        (own, half),
        (down1, half),
        (down2, size),
        (down3, size),
        (up4, half),
        (up3, size),
        (up2, size),
        (up1, half),
    )
    for k, (ref, start) in enumerate(by_step):
        w_z[(k + z) & 7] = ref[start:, :]
    w_sum = w_z[0].astype(jnp.float32)
    for a in range(1, NZ):
        w_sum = w_sum + w_z[a].astype(jnp.float32)
    message[half:, :] = w_sum.astype(jnp.bfloat16)
    for k in range(2):
        start = k * TILE
        total = parts[2 + k].astype(jnp.float32) + f32(up4, start) + f32(down4, start)
        message[start : start + TILE, :] = total.astype(jnp.bfloat16)


def middle_kernel(parts, up4, down4, sent, from_x, w_lo, w_both, mine, message, w_here):
    x_lo = lax.axis_index("col") >> 2
    half = 2 * TILE
    for k, ref in enumerate((mine, message)):
        start = k * TILE
        total = parts[k].astype(jnp.float32) + f32(up4, start) + f32(down4, start)
        ref[:TILE, :] = (total + f32(from_x, start)).astype(jnp.bfloat16)
    sums = (
        f32(sent, half, W_ROWS) + f32(from_x, half, W_ROWS),
        w_lo[...].astype(jnp.float32) + w_both[...].astype(jnp.float32),
    )
    for value, place in zip(sums, (x_lo, 1 - x_lo)):
        high, low = split(value)
        w_here[place] = high.astype(jnp.float32) + low.astype(jnp.float32)
        start = pl.multiple_of(TILE + place * 2 * W_ROWS, W_ROWS)
        message[pl.ds(start, W_ROWS), :] = high
        message[pl.ds(start + W_ROWS, W_ROWS), :] = low


def last_kernel(mine, from_core, w_here, grad_out, w_out):
    core = lax.axis_index("row") & 1
    scale = 1.0 / 256.0

    def place(value, start):
        rows = pl.ds(pl.multiple_of(start, 64), 64)
        w_out[rows, :HALF] = value[:64, :] * scale
        w_out[rows, HALF:] = value[64:, :] * scale

    for x_lo in range(2):
        start = TILE + x_lo * 2 * W_ROWS
        place(w_here[x_lo], core * HALF + x_lo * 64)
        w_core = f32(from_core, start, W_ROWS) + f32(from_core, start + W_ROWS, W_ROWS)
        place(w_core, (1 - core) * HALF + x_lo * 64)

    @pl.when(core == 0)
    def _():
        grad_out[:, :HALF] = mine[...]
        grad_out[:, HALF:] = from_core[:TILE, :]

    @pl.when(core == 1)
    def _():
        grad_out[:, HALF:] = mine[...]
        grad_out[:, :HALF] = from_core[:TILE, :]


SMEM = pl.BlockSpec(memory_space=pltpu.SMEM)
VMEM = pl.BlockSpec(memory_space=pltpu.VMEM)
ANY = pl.BlockSpec(memory_space=pl.ANY)


def params(mib):
    return pltpu.CompilerParams(vmem_limit_bytes=mib << 20)


LIST = 2 * SLOTS + UNROLL
SLOT_SCRATCH = [
    pltpu.VMEM((LIST, TILE, TILE), jnp.bfloat16),
    pltpu.SMEM((LIST,), jnp.int32),
    pltpu.SMEM((LIST,), jnp.int32),
]


def cost(slots, size):
    return pl.CostEstimate(
        flops=slots * 2 * TILE * TILE * HALF, bytes_accessed=size << 20, transcendentals=0
    )


LISTS = [SMEM] * 4


def shape(*dims, dtype=jnp.bfloat16):
    return jax.ShapeDtypeStruct(dims, dtype)


def local(kernel, outs, n_in, name, scalars=0, any_in=0, scratch=(), cost=None, scalar_out=0):
    return pl.pallas_call(
        kernel,
        out_shape=outs,
        in_specs=[SMEM] * scalars + [ANY] * any_in + [VMEM] * (n_in - scalars - any_in),
        out_specs=(VMEM,) * (len(outs) - scalar_out) + (SMEM,) * scalar_out,
        scratch_shapes=scratch,
        compiler_params=params(20),
        cost_estimate=cost,
        name=name,
    )


def prepare(rows, cols, count, block):
    return local(
        prepare_kernel,
        (shape(TILE, HALF), shape(TILE + 16, HALF), shape(25, dtype=jnp.int32)),
        4,
        "prepare",
        scalars=3,
        scalar_out=1,
    )(rows, cols, count, block)


def join(own_keep, own_message, x_block):
    return local(
        join_kernel, (shape(2, TILE, HALF), shape(2 * TILE + 16, HALF)), 3, "join"
    )(own_keep, own_message, x_block)


def forward_near(lists, adj0, adj1, pieces):
    return local(
        forward_near_kernel,
        (shape(17, TILE, HALF, dtype=jnp.float32),),
        11,
        "forward_near",
        scalars=2,
        any_in=9,
        scratch=[pltpu.VMEM((NZ * QUAD, TILE, HALF), jnp.bfloat16)]
        + SLOT_SCRATCH
        + [pltpu.SemaphoreType.DMA((NZ,)), pltpu.SemaphoreType.DMA((LIST,))],
        cost=cost(21, 6),
    )(*lists, adj0, adj1, *pieces)[0]


def forward_far(lists, adj0, adj1, near, far_a, far_b):
    return local(
        forward_far_kernel,
        (shape(8, 2, TILE, HALF),),
        7,
        "forward_far",
        scalars=2,
        any_in=2,
        scratch=[
            pltpu.VMEM((17, TILE, HALF), jnp.float32),
            pltpu.VMEM((QUAD, TILE, HALF), jnp.bfloat16),
        ]
        + SLOT_SCRATCH
        + [pltpu.SemaphoreType.DMA((LIST,))],
        cost=cost(3, 4),
    )(*lists, adj0, adj1, near, far_a, far_b)[0]


def backward_tiles(lists, adj0, adj1, back, far):
    places = QUAD if far else NZ * QUAD
    message = shape(2 * TILE + W_ROWS, HALF)
    return local(
        functools.partial(backward_kernel, far),
        (message, message) if far else (shape(places, TILE, HALF),),
        5,
        "backward_far" if far else "backward_near",
        scalars=2,
        any_in=2,
        scratch=[pltpu.VMEM((places + 1, TILE, HALF), jnp.float32)]
        + SLOT_SCRATCH
        + [pltpu.SemaphoreType.DMA((LIST,))],
        cost=cost(3, 2) if far else cost(21, 6),
    )(*lists, adj0, adj1, back)


def dense(agg_own, agg_other, weight, cot_own, cot_other):
    return local(
        dense_kernel,
        (shape(TILE, 2 * HALF), shape(NCOL, 2 * TILE + W_ROWS, HALF)),
        5,
        "dense",
    )(agg_own, agg_other, weight, cot_own, cot_other)


def away(parts, *messages):
    return local(
        away_kernel,
        (shape(2 * TILE + W_ROWS, HALF),),
        10,
        "away",
        scratch=[pltpu.VMEM((NZ, W_ROWS, HALF), jnp.bfloat16)],
    )(parts, *messages)[0]


def middle(*operands):
    return local(
        middle_kernel,
        (
            shape(TILE, HALF),
            shape(TILE + 4 * W_ROWS, HALF),
            shape(2, W_ROWS, HALF, dtype=jnp.float32),
        ),
        7,
        "middle",
    )(*operands)


def last(mine, from_core, w_here):
    return local(
        last_kernel,
        (shape(TILE, 2 * HALF), shape(2 * HALF, 2 * HALF, dtype=jnp.float32)),
        3,
        "last",
    )(mine, from_core, w_here)


def add(a, b):
    return (a.astype(jnp.float32) + b.astype(jnp.float32)).astype(jnp.bfloat16)


def per_device(features, adj_tiles, tile_row, tile_col, tile_count, weight, cotangent):
    adj0 = adj_tiles[0, 0]
    block = features[0]

    x_block = quad_permute(block, 2)
    keep, message, own_lists = prepare(tile_row[0, 0], tile_col[0, 0], tile_count, block)
    keep, message = join(keep, message, x_block)
    from_core = quad_permute(message, 1)
    core_keep = from_core[16:].reshape(2, TILE, HALF)
    chunk = jnp.stack([keep[0], core_keep[0], keep[1], core_keep[1]])
    lists = (own_lists, from_core[0, :25].astype(jnp.int32))
    adj1 = quad_permute(adj0, 1)
    cot1 = quad_permute(cotangent, 1)

    up1, down1 = z_shift(chunk, 1), z_shift(chunk, -1)
    up2, down2 = z_shift(up1, 1), z_shift(down1, -1)
    up3, down3 = z_shift(up2, 1), z_shift(down2, -1)
    far_a, far_b = z_shift(up3[:2], 1), z_shift(down3[2:], -1)
    near = forward_near(lists, adj0, adj1, [chunk, down1, down2, down3, up3, up2, up1])
    partial = forward_far(lists, adj0, adj1, near, far_a, far_b)

    shares = lax.all_to_all(partial, "col", 0, 0, tiled=True)
    agg = shares.reshape(NCOL, 2 * TILE, HALF).astype(jnp.float32).sum(axis=0)
    agg_other = quad_permute(agg, 1)
    activated, send = dense(agg, agg_other, weight, cotangent, cot1)
    received = lax.all_to_all(send, "col", 0, 0, tiled=True)

    half, size = 2 * TILE, QUAD * TILE
    own, own_down = backward_tiles(lists, adj0, adj1, received, True)
    (blocks,) = backward_tiles(lists, adj0, adj1, received, False)
    parts = blocks.reshape(NZ, size, HALF)
    up1, down1 = z_shift(own, 1), z_shift(own_down, -1)
    up = [add(parts[3, :half], up1[:half]), parts[3, half:], up1[half:]]
    down = [parts[5, :half], add(parts[5, half:], down1[:half]), down1[half:]]
    up2, down2 = z_shift(jnp.concatenate(up), 1), z_shift(jnp.concatenate(down), -1)
    up = [add(parts[2], up2[:size]), up2[size:]]
    down = [add(parts[6], down2[:size]), down2[size:]]
    up3, down3 = z_shift(jnp.concatenate(up), 1), z_shift(jnp.concatenate(down), -1)
    up = add(parts[1], up3[:size])
    down = add(parts[7], down3[:size])
    up4_away = z_shift(jnp.concatenate([up[half:], up3[size:]]), 1)
    down4_away = z_shift(down[half:], -1)
    up4, down4 = z_shift(up[:half], 1), z_shift(down[:half], -1)

    to_x = away(blocks, own, up1, up2, up3, up4_away, down1, down2, down3, down4_away)
    w_send = to_x[half:]
    from_x = quad_permute(to_x, 2)
    w_lo = lax.ppermute(w_send, "col", [(c, c ^ 4) for c in range(NCOL)])
    both = [
        (r * NCOL + c, (r ^ 2) * NCOL + (c ^ 4)) for r in range(NZ * QUAD) for c in range(NCOL)
    ]
    w_both = lax.ppermute(w_send, ("row", "col"), both)
    mine, to_core, w_here = middle(blocks, up4, down4, to_x, from_x, w_lo, w_both)
    grad, weight_grad = last(mine, quad_permute(to_core, 1), w_here)
    return (activated, weight_grad, grad[None])


def solution(mesh):
    return jax.shard_map(
        per_device,
        mesh=mesh,
        in_specs=(
            P("col", "row", None),
            P("row", "col", None, None, None),
            P("row", "col", None),
            P("row", "col", None),
            P("row", "col"),
            P(),
            P(("row", "col"), None),
        ),
        out_specs=(P(("row", "col"), None), P(), P("col", "row", None)),
        check_vma=False,
    )
```

```python
import functools
import math

import jax
import jax.numpy as jnp
from jax import lax
from jax.experimental import pallas as pl
from jax.experimental.pallas import tpu as pltpu
from jax.sharding import PartitionSpec as P

NZ = 8
QUAD = 4
NCOL = 8
TILE = 256
HALF = 128
SLOTS = 12
W_ROWS = 128
UNROLL = 4


def row_pairs(move):
    pairs = []
    for r in range(NZ * QUAD):
        z, q = move(r // QUAD, r % QUAD)
        pairs.append((r, (z % NZ) * QUAD + q))
    return pairs


def quad_permute(x, flip):
    return lax.ppermute(x, "row", row_pairs(lambda z, q: (z, q ^ flip)))


def z_shift(x, step):
    return lax.ppermute(x, "row", row_pairs(lambda z, q: (z + step, q)))


def prepare_kernel(rows, cols, count, block, keep, message, own_lists):
    core = lax.axis_index("row") & 1

    @pl.when(core == 0)
    def _():
        keep[...] = block[:, :HALF]
        message[16:, :] = block[:, HALF:]

    @pl.when(core == 1)
    def _():
        keep[...] = block[:, HALF:]
        message[16:, :] = block[:, :HALF]

    lane = lax.broadcasted_iota(jnp.int32, (16, HALF), 1)
    values = jnp.zeros((16, HALF), jnp.float32)
    listed = [rows[s] for s in range(SLOTS)] + [cols[s] for s in range(SLOTS)] + [count[0, 0]]
    for n, value in enumerate(listed):
        values = jnp.where(lane == n, value.astype(jnp.float32), values)
        own_lists[n] = value
    message[:16, :] = values.astype(jnp.bfloat16)


def list_slots(lists, adj_refs, adj_vmem, adj_sem, rows, places, chosen, dummy):
    device = lax.axis_index("row")
    z, q = device >> 2, device & 3
    n = jnp.int32(0)
    for i in range(2):
        count = lists[i][24]
        for s in range(SLOTS):
            tile = lists[i][12 + s]
            row = lists[i][s]
            place = (((tile >> 2) - z) & 7) * QUAD + ((tile & 3) ^ q)
            live = (s < count) & chosen(place)
            rows[n] = row * 2 + i
            places[n] = place

            @pl.when(live)
            def _(i=i, s=s, n=n):
                pltpu.make_async_copy(
                    adj_refs[i].at[s], adj_vmem.at[n], adj_sem.at[n]
                ).start()

            n = n + live.astype(jnp.int32)
    for u in range(UNROLL - 1):
        rows[n + u], places[n + u] = dummy
    return n


def slot_products(n, adj_ref, adj_vmem, adj_sem, product, add_to):
    @pl.loop(0, (n + UNROLL - 1) >> 2)
    def _(step):
        slots = [step * UNROLL + u for u in range(UNROLL)]
        for j in slots:

            @pl.when(j < n)
            def _(j=j):
                pltpu.make_async_copy(adj_ref.at[0], adj_vmem.at[j], adj_sem.at[j]).wait()

        values = [product(j) for j in slots]
        for j, value in zip(slots, values):
            add_to(j, value)


NEAR_PIECES = (
    [(0, 0, 2, 0), (1, 0, 2, 2)]
    + [(2, 0, 2, 28), (3, 0, 2, 4), (4, 0, 2, 30), (4, 2, 2, 6)]
    + [(5, 0, 2, 24), (6, 0, 2, 8), (7, 0, 2, 26), (7, 2, 2, 10)]
    + [(8, 0, 2, 20), (9, 0, 2, 12), (10, 0, 2, 22), (10, 2, 2, 14)]
    + [(11, 0, 1, 16), (12, 0, 1, 17)]
)


def forward_near_kernel(*refs):
    lists, (adj0, adj1), pieces, refs = refs[:2], refs[2:4], refs[4:17], refs[17:]
    acc, panel, adj_vmem, rows, places, panel_sem, adj_sem = refs
    copies = [
        pltpu.make_async_copy(
            pieces[piece].at[pl.ds(start, blocks)],
            panel.at[pl.ds(place, blocks)],
            panel_sem.at[k],
        )
        for k, (piece, start, blocks, place) in enumerate(NEAR_PIECES)
    ]
    for copy in copies:
        copy.start()
    n = list_slots(
        lists,
        (adj0, adj1),
        adj_vmem,
        adj_sem,
        rows,
        places,
        lambda place: (place >> 1) != 9,
        (16, 0),
    )
    acc[...] = jnp.zeros_like(acc)
    for copy in copies:
        copy.wait()

    def product(j):
        return jnp.dot(adj_vmem[j], panel[places[j]], preferred_element_type=jnp.float32)

    def add_to(j, value):
        acc[rows[j]] += value

    slot_products(n, adj0, adj_vmem, adj_sem, product, add_to)


def forward_far_kernel(*refs):
    lists, refs = refs[:2], refs[2:]
    adj0, adj1, near, far, out, acc, adj_vmem, rows, places, adj_sem = refs
    n = list_slots(
        lists,
        (adj0, adj1),
        adj_vmem,
        adj_sem,
        rows,
        places,
        lambda place: (place >> 1) == 9,
        (16, 18),
    )
    acc[...] = near[...]

    def product(j):
        return jnp.dot(adj_vmem[j], far[places[j] - 18], preferred_element_type=jnp.float32)

    def add_to(j, value):
        acc[rows[j]] += value

    slot_products(n, adj0, adj_vmem, adj_sem, product, add_to)
    for row in range(8):
        for i in range(2):
            out[row, i] = acc[2 * row + i].astype(jnp.bfloat16)


def backward_kernel(far, *refs):
    lists, refs = refs[:2], refs[2:]
    adj0, adj1, back = refs[:3]
    acc, adj_vmem, rows, places, adj_sem = refs[-5:]
    outs = refs[3:-5]
    base = 16 if far else 0
    spare = acc.shape[0] - 1
    n = list_slots(
        lists,
        (adj0, adj1),
        adj_vmem,
        adj_sem,
        rows,
        places,
        lambda place: ((place >> 2) == 4) == far,
        (0, base + spare),
    )
    acc[...] = jnp.zeros_like(acc)

    def product(j):
        row = rows[j]
        return lax.dot_general(
            adj_vmem[j],
            back[row >> 1, pl.ds((row & 1) * TILE, TILE), :],
            (((0,), (0,)), ((), ())),
            preferred_element_type=jnp.float32,
        )

    def add_to(j, value):
        acc[places[j] - base] += value

    slot_products(n, adj0, adj_vmem, adj_sem, product, add_to)

    def write(out, start, place):
        for k in range(2):
            rows = pl.ds(start + k * TILE, TILE)
            out[rows, :] = acc[place - base + k].astype(jnp.bfloat16)

    if far:
        own, to_x = outs
        write(own, 0, 16)
        write(to_x, 0, 18)
        piece = back[0, 2 * TILE :, :].astype(jnp.float32)
        for c in range(1, NCOL):
            piece = piece + back[c, 2 * TILE :, :].astype(jnp.float32)
        to_x[2 * TILE :, :] = piece.astype(jnp.bfloat16)
        return
    own, to_x3, to_x2, to_x1, to_x0 = outs
    for z in (0, 1, 2, 3, 5, 6, 7):
        write(own, z * 2 * TILE, z * QUAD)
    for step, out in ((3, to_x3), (2, to_x2), (1, to_x1)):
        write(out, 0, step * QUAD + 2)
        write(out, 2 * TILE, (NZ - step) * QUAD + 2)
    write(to_x0, 0, 2)


def split(x):
    high = x.astype(jnp.bfloat16)
    return high, (x - high.astype(jnp.float32)).astype(jnp.bfloat16)


def dense_kernel(agg_own, agg_other, weight, cot_own, cot_other, act_out, send_out):
    first = (lax.axis_index("row") & 1) == 0
    own = agg_own[...]
    other = jnp.concatenate([agg_other[TILE:, :], agg_other[:TILE, :]], axis=0)
    w = weight[...]
    w_other_half = jnp.where(first, w[HALF:], w[:HALF])
    w_half = jnp.where(first, w[:HALF], w[HALF:])

    def dot(a, b, dims=((1,), (0,))):
        return lax.dot_general(a, b, (dims, ((), ())), preferred_element_type=jnp.float32)

    own_hi, own_lo = split(own)
    other_hi, other_lo = split(other)
    v = (dot(own_hi, w_half) + dot(own_lo, w_half)) + (
        dot(other_hi, w_other_half) + dot(other_lo, w_other_half)
    )
    scale = math.sqrt(2.0 / math.pi)
    square = v * v
    t = jnp.tanh(scale * (v + 0.044715 * (square * v)))
    cdf = 0.5 * (1.0 + t)
    act_out[...] = (v[:TILE] * cdf[:TILE]).astype(jnp.bfloat16)
    slope = cdf + 0.5 * v * ((1.0 - t) * (1.0 + t)) * (scale * (1.0 + 3.0 * 0.044715 * square))
    cot = jnp.concatenate([cot_own[...], cot_other[...]], axis=0).astype(jnp.float32)
    grad_hi, grad_lo = split(cot * slope)
    nodes = ((1,), (1,))
    back = (dot(grad_hi, w_half, nodes) + dot(grad_lo, w_half, nodes)).astype(jnp.bfloat16)
    rows = ((0,), (0,))
    w_part = (
        dot(own_hi, grad_hi, rows) + dot(own_lo, grad_hi, rows) + dot(own_hi, grad_lo, rows)
    ).astype(jnp.bfloat16)
    for c in range(NCOL):
        send_out[c, : 2 * TILE, :] = back
        piece = w_part[64 * (c // 4) : 64 * (c // 4) + 64]
        send_out[c, 2 * TILE : 2 * TILE + 64, :] = piece[:, :HALF]
        send_out[c, 2 * TILE + 64 :, :] = piece[:, HALF:]


def f32(ref, start, rows=TILE):
    return ref[start : start + rows, :].astype(jnp.float32)


def enter_kernel(own, sent, from_x, w_lo, w_both, up, down):
    half = 2 * TILE
    sums = (
        f32(sent, half, W_ROWS) + f32(from_x, half, W_ROWS),
        w_lo[...].astype(jnp.float32) + w_both[...].astype(jnp.float32),
    )
    for k, out in enumerate((up, down)):
        start = k * TILE
        out[:TILE, :] = (f32(own, start) + f32(from_x, start)).astype(jnp.bfloat16)
        for j, value in enumerate(sums):
            rows = pl.ds(TILE + j * W_ROWS, W_ROWS)
            out[rows, :] = value.astype(jnp.bfloat16)


def leave_kernel(
    own, from_x, up, up1, up2, up3, up4, down1, down2, down3, down4, mine, message, w_here, by_step
):
    z = lax.axis_index("row") >> 2
    x_lo = lax.axis_index("col") >> 2
    half = 2 * TILE
    pieces = (
        (up, TILE),
        (down1, TILE),
        (down2, half),
        (down3, half),
        (up4, half),
        (up3, half),
        (up2, half),
        (up1, TILE),
    )
    for k, (ref, start) in enumerate(pieces):
        by_step[(k + z) & 7] = ref[start : start + 2 * W_ROWS, :]
    w_sum = by_step[0].astype(jnp.float32)
    for a in range(1, NZ):
        w_sum = w_sum + by_step[a].astype(jnp.float32)
    for k, ref in enumerate((mine, message)):
        start = k * TILE
        total = f32(own, start) + f32(from_x, start) + f32(up4, start) + f32(down4, start)
        ref[:TILE, :] = total.astype(jnp.bfloat16)
    for k, place in enumerate((x_lo, 1 - x_lo)):
        high, low = split(w_sum[k * W_ROWS : (k + 1) * W_ROWS])
        w_here[place] = high.astype(jnp.float32) + low.astype(jnp.float32)
        start = pl.multiple_of(TILE + place * 2 * W_ROWS, W_ROWS)
        message[pl.ds(start, W_ROWS), :] = high
        message[pl.ds(start + W_ROWS, W_ROWS), :] = low


def last_kernel(mine, from_core, w_here, grad_out, w_out):
    core = lax.axis_index("row") & 1
    scale = 1.0 / 256.0

    def place(value, start):
        rows = pl.ds(pl.multiple_of(start, 64), 64)
        w_out[rows, :HALF] = value[:64, :] * scale
        w_out[rows, HALF:] = value[64:, :] * scale

    for x_lo in range(2):
        start = TILE + x_lo * 2 * W_ROWS
        place(w_here[x_lo], core * HALF + x_lo * 64)
        w_core = f32(from_core, start, W_ROWS) + f32(from_core, start + W_ROWS, W_ROWS)
        place(w_core, (1 - core) * HALF + x_lo * 64)

    @pl.when(core == 0)
    def _():
        grad_out[:, :HALF] = mine[...]
        grad_out[:, HALF:] = from_core[:TILE, :]

    @pl.when(core == 1)
    def _():
        grad_out[:, HALF:] = mine[...]
        grad_out[:, :HALF] = from_core[:TILE, :]


SMEM = pl.BlockSpec(memory_space=pltpu.SMEM)
VMEM = pl.BlockSpec(memory_space=pltpu.VMEM)
ANY = pl.BlockSpec(memory_space=pl.ANY)


def params(mib):
    return pltpu.CompilerParams(vmem_limit_bytes=mib << 20)


LIST = 2 * SLOTS + UNROLL
SLOT_SCRATCH = [
    pltpu.VMEM((LIST, TILE, TILE), jnp.bfloat16),
    pltpu.SMEM((LIST,), jnp.int32),
    pltpu.SMEM((LIST,), jnp.int32),
]


def cost(slots, size):
    return pl.CostEstimate(
        flops=slots * 2 * TILE * TILE * HALF, bytes_accessed=size << 20, transcendentals=0
    )


LISTS = [SMEM] * 4


def shape(*dims, dtype=jnp.bfloat16):
    return jax.ShapeDtypeStruct(dims, dtype)


def local(kernel, outs, n_in, name, scalars=0, any_in=0, scratch=(), cost=None, scalar_out=0):
    return pl.pallas_call(
        kernel,
        out_shape=outs,
        in_specs=[SMEM] * scalars + [ANY] * any_in + [VMEM] * (n_in - scalars - any_in),
        out_specs=(VMEM,) * (len(outs) - scalar_out) + (SMEM,) * scalar_out,
        scratch_shapes=scratch,
        compiler_params=params(20),
        cost_estimate=cost,
        name=name,
    )


def prepare(rows, cols, count, block):
    return local(
        prepare_kernel,
        (shape(TILE, HALF), shape(TILE + 16, HALF), shape(25, dtype=jnp.int32)),
        4,
        "prepare",
        scalars=3,
        scalar_out=1,
    )(rows, cols, count, block)


def forward_near(lists, adj0, adj1, pieces):
    return local(
        forward_near_kernel,
        (shape(17, TILE, HALF, dtype=jnp.float32),),
        17,
        "forward_near",
        scalars=2,
        any_in=15,
        scratch=[pltpu.VMEM((NZ * QUAD, TILE, HALF), jnp.bfloat16)]
        + SLOT_SCRATCH
        + [pltpu.SemaphoreType.DMA((len(NEAR_PIECES),)), pltpu.SemaphoreType.DMA((LIST,))],
        cost=cost(22, 6),
    )(*lists, adj0, adj1, *pieces)[0]


def forward_far(lists, adj0, adj1, near, far):
    return local(
        forward_far_kernel,
        (shape(8, 2, TILE, HALF),),
        6,
        "forward_far",
        scalars=2,
        any_in=2,
        scratch=[pltpu.VMEM((17, TILE, HALF), jnp.float32)]
        + SLOT_SCRATCH
        + [pltpu.SemaphoreType.DMA((LIST,))],
        cost=cost(2, 4),
    )(*lists, adj0, adj1, near, far)[0]


def backward_tiles(lists, adj0, adj1, back, far):
    half = 2 * TILE
    if far:
        outs = (shape(half, HALF), shape(half + W_ROWS, HALF))
    else:
        outs = (shape(NZ * half, HALF),) + (shape(2 * half, HALF),) * 3 + (shape(half, HALF),)
    return local(
        functools.partial(backward_kernel, far),
        outs,
        5,
        "backward_far" if far else "backward_near",
        scalars=2,
        any_in=2,
        scratch=[pltpu.VMEM(((QUAD if far else NZ * QUAD) + 1, TILE, HALF), jnp.float32)]
        + SLOT_SCRATCH
        + [pltpu.SemaphoreType.DMA((LIST,))],
        cost=cost(3, 2) if far else cost(21, 6),
    )(*lists, adj0, adj1, back)


def dense(agg_own, agg_other, weight, cot_own, cot_other):
    return local(
        dense_kernel,
        (shape(TILE, 2 * HALF), shape(NCOL, 2 * TILE + W_ROWS, HALF)),
        5,
        "dense",
    )(agg_own, agg_other, weight, cot_own, cot_other)


def enter(*operands):
    message = shape(TILE + 2 * W_ROWS, HALF)
    return local(enter_kernel, (message, message), 5, "enter")(*operands)


def leave(*operands):
    return local(
        leave_kernel,
        (
            shape(TILE, HALF),
            shape(TILE + 4 * W_ROWS, HALF),
            shape(2, W_ROWS, HALF, dtype=jnp.float32),
        ),
        11,
        "leave",
        scratch=[pltpu.VMEM((NZ, 2 * W_ROWS, HALF), jnp.bfloat16)],
    )(*operands)


def last(mine, from_core, w_here):
    return local(
        last_kernel,
        (shape(TILE, 2 * HALF), shape(2 * HALF, 2 * HALF, dtype=jnp.float32)),
        3,
        "last",
    )(mine, from_core, w_here)


def add(*terms):
    return sum(term.astype(jnp.float32) for term in terms).astype(jnp.bfloat16)


def per_device(features, adj_tiles, tile_row, tile_col, tile_count, weight, cotangent):
    adj0 = adj_tiles[0, 0]

    keep, message, own_lists = prepare(tile_row[0, 0], tile_col[0, 0], tile_count, features[0])
    from_core = quad_permute(message, 1)
    chunk = jnp.stack([keep, from_core[16:]])
    lists = (own_lists, from_core[0, :25].astype(jnp.int32))
    adj1 = quad_permute(adj0, 1)
    cot1 = quad_permute(cotangent, 1)

    x0 = quad_permute(chunk, 2)
    up1, down1 = z_shift(chunk, 1), z_shift(chunk, -1)
    x1 = quad_permute(jnp.concatenate([up1, down1]), 2)
    up2, down2 = z_shift(up1, 1), z_shift(down1, -1)
    up2, down2, x0 = lax.optimization_barrier((up2, down2, x0))
    x2 = quad_permute(jnp.concatenate([up2, down2]), 2)
    up3, down3 = z_shift(up2, 1), z_shift(down2, -1)
    up3, down3, x1 = lax.optimization_barrier((up3, down3, x1))
    x3 = quad_permute(jnp.concatenate([up3, down3]), 2)
    far_a, far_b = z_shift(up3[:1], 1), z_shift(down3[1:], -1)
    far_a, far_b, x2 = lax.optimization_barrier((far_a, far_b, x2))
    far = quad_permute(jnp.concatenate([far_a, far_b]), 2)
    pieces = [chunk, x0, up1, down1, x1, up2, down2, x2, up3, down3, x3]
    near = forward_near(lists, adj0, adj1, pieces + [far_a, far_b])
    partial = forward_far(lists, adj0, adj1, near, far)

    shares = lax.all_to_all(partial, "col", 0, 0, tiled=True)
    agg = shares.reshape(NCOL, 2 * TILE, HALF).astype(jnp.float32).sum(axis=0)
    agg_other = quad_permute(agg, 1)
    activated, send = dense(agg, agg_other, weight, cotangent, cot1)
    received = lax.all_to_all(send, "col", 0, 0, tiled=True)

    half = 2 * TILE
    own4, to_x4 = backward_tiles(lists, adj0, adj1, received, True)
    w_send = to_x4[half:]
    both = [
        (r * NCOL + c, (r ^ 2) * NCOL + (c ^ 4)) for r in range(NZ * QUAD) for c in range(NCOL)
    ]
    x4 = quad_permute(to_x4, 2)
    w_lo = lax.ppermute(w_send, "col", [(c, c ^ 4) for c in range(NCOL)])
    w_both = lax.ppermute(w_send, ("row", "col"), both)
    own, to_x3, to_x2, to_x1, to_x0 = backward_tiles(lists, adj0, adj1, received, False)
    own = own.reshape(NZ, half, HALF)
    x3, x2, x1, x0 = (quad_permute(x, 2) for x in (to_x3, to_x2, to_x1, to_x0))
    up_first, down_first = enter(own4, to_x4, x4, w_lo, w_both)
    up1, down1 = z_shift(up_first, 1), z_shift(down_first, -1)
    up = [
        add(own[3, :TILE], x3[:TILE], up1[:TILE]),
        add(own[3, TILE:], x3[TILE:half]),
        up1[TILE:],
    ]
    down = [
        add(own[5, :TILE], x3[half : half + TILE]),
        add(own[5, TILE:], x3[half + TILE :], down1[:TILE]),
        down1[TILE:],
    ]
    up2, down2 = z_shift(jnp.concatenate(up), 1), z_shift(jnp.concatenate(down), -1)
    up = [add(own[2], x2[:half], up2[:half]), up2[half:]]
    down = [add(own[6], x2[half:], down2[:half]), down2[half:]]
    up3, down3 = z_shift(jnp.concatenate(up), 1), z_shift(jnp.concatenate(down), -1)
    up = [add(own[1], x1[:half], up3[:half]), up3[half:]]
    up4 = z_shift(jnp.concatenate(up), 1)
    down4 = z_shift(add(own[7], x1[half:], down3[:half]), -1)
    mine, to_core, w_here = leave(
        own[0], x0, up_first, up1, up2, up3, up4, down1, down2, down3, down4
    )
    grad, weight_grad = last(mine, quad_permute(to_core, 1), w_here)
    return (activated, weight_grad, grad[None])


def solution(mesh):
    return jax.shard_map(
        per_device,
        mesh=mesh,
        in_specs=(
            P("col", "row", None),
            P("row", "col", None, None, None),
            P("row", "col", None),
            P("row", "col", None),
            P("row", "col"),
            P(),
            P(("row", "col"), None),
        ),
        out_specs=(P(("row", "col"), None), P(), P("col", "row", None)),
        check_vma=False,
    )
```

```python
import functools
import math

import jax
import jax.numpy as jnp
from jax import lax
from jax.experimental import pallas as pl
from jax.experimental.pallas import tpu as pltpu
from jax.sharding import PartitionSpec as P

NZ = 8
QUAD = 4
NCOL = 8
TILE = 256
HALF = 128
SLOTS = 12
W_ROWS = 128
UNROLL = 4
MOVES = (0, 6, 2, 5, 7, 1, 3, 4)


def row_pairs(move):
    pairs = []
    for r in range(NZ * QUAD):
        z, q = move(r // QUAD, r % QUAD)
        pairs.append((r, (z % NZ) * QUAD + q))
    return pairs


def quad_permute(x, flip):
    return lax.ppermute(x, "row", row_pairs(lambda z, q: (z, q ^ flip)))


def col_move(x, k):
    pairs = [(c, ((c >> 2) ^ (k >> 2)) * 4 + (c + k) % 4) for c in range(NCOL)]
    return lax.ppermute(x, "col", pairs)


def col_target(k, sign):
    c = lax.axis_index("col")
    return (((c >> 2) ^ (k >> 2)) << 2) + ((c + sign * (k & 3)) & 3)


def z_shift(x, step):
    return lax.ppermute(x, "row", row_pairs(lambda z, q: (z + step, q)))


def prepare_kernel(rows, cols, count, block, keep, message, own_lists):
    core = lax.axis_index("row") & 1

    @pl.when(core == 0)
    def _():
        keep[...] = block[:, :HALF]
        message[16:, :] = block[:, HALF:]

    @pl.when(core == 1)
    def _():
        keep[...] = block[:, HALF:]
        message[16:, :] = block[:, :HALF]

    lane = lax.broadcasted_iota(jnp.int32, (16, HALF), 1)
    values = jnp.zeros((16, HALF), jnp.float32)
    listed = [rows[s] for s in range(SLOTS)] + [cols[s] for s in range(SLOTS)] + [count[0, 0]]
    for n, value in enumerate(listed):
        values = jnp.where(lane == n, value.astype(jnp.float32), values)
        own_lists[n] = value
    message[:16, :] = values.astype(jnp.bfloat16)


def join_kernel(own_keep, own_message, x_block, keep, message):
    core = lax.axis_index("row") & 1
    keep[0] = own_keep[...]
    message[: TILE + 16, :] = own_message[...]

    @pl.when(core == 0)
    def _():
        keep[1] = x_block[:, :HALF]
        message[TILE + 16 :, :] = x_block[:, HALF:]

    @pl.when(core == 1)
    def _():
        keep[1] = x_block[:, HALF:]
        message[TILE + 16 :, :] = x_block[:, :HALF]


def list_slots(lists, adj_refs, adj_vmem, adj_sem, rows, places, far, dummy):
    device = lax.axis_index("row")
    z, q = device >> 2, device & 3
    n = jnp.int32(0)
    for i in range(2):
        count = lists[i][24]
        for s in range(SLOTS):
            tile = lists[i][12 + s]
            row = lists[i][s]
            place = (((tile >> 2) - z) & 7) * QUAD + ((tile & 3) ^ q)
            live = (s < count) & (((place >> 2) == 4) == far)
            rows[n] = row * 2 + i
            places[n] = place

            @pl.when(live)
            def _(i=i, s=s, n=n):
                pltpu.make_async_copy(
                    adj_refs[i].at[s], adj_vmem.at[n], adj_sem.at[n]
                ).start()

            n = n + live.astype(jnp.int32)
    for u in range(UNROLL - 1):
        rows[n + u], places[n + u] = dummy
    return n


def slot_products(n, adj_ref, adj_vmem, adj_sem, product, add_to):
    @pl.loop(0, (n + UNROLL - 1) >> 2)
    def _(step):
        slots = [step * UNROLL + u for u in range(UNROLL)]
        for j in slots:

            @pl.when(j < n)
            def _(j=j):
                pltpu.make_async_copy(adj_ref.at[0], adj_vmem.at[j], adj_sem.at[j]).wait()

        values = [product(j) for j in slots]
        for j, value in zip(slots, values):
            add_to(j, value)


def forward_near_kernel(*refs):
    lists, (adj0, adj1), refs = refs[:2], refs[2:4], refs[4:]
    pieces, (acc, panel, adj_vmem, rows, places, panel_sem, adj_sem) = refs[:7], refs[7:]
    copies = [
        pltpu.make_async_copy(piece, panel.at[pl.ds(place * QUAD, QUAD)], panel_sem.at[place])
        for place, piece in zip((0, 1, 2, 3, 5, 6, 7), pieces)
    ]
    for copy in copies:
        copy.start()
    n = list_slots(lists, (adj0, adj1), adj_vmem, adj_sem, rows, places, False, (16, 0))
    acc[...] = jnp.zeros_like(acc)
    for copy in copies:
        copy.wait()

    def product(j):
        return jnp.dot(adj_vmem[j], panel[places[j]], preferred_element_type=jnp.float32)

    def add_to(j, value):
        acc[rows[j]] += value

    slot_products(n, adj0, adj_vmem, adj_sem, product, add_to)


def forward_far_kernel(*refs):
    lists, refs = refs[:2], refs[2:]
    adj0, adj1, near, far_a, far_b = refs[:5]
    outs, (acc, far, adj_vmem, rows, places, adj_sem) = refs[5:13], refs[13:]
    n = list_slots(lists, (adj0, adj1), adj_vmem, adj_sem, rows, places, True, (16, 16))
    far[:2] = far_a[...]
    far[2:] = far_b[...]
    acc[...] = near[...]

    def product(j):
        return jnp.dot(adj_vmem[j], far[places[j] - 16], preferred_element_type=jnp.float32)

    def add_to(j, value):
        acc[rows[j]] += value

    slot_products(n, adj0, adj_vmem, adj_sem, product, add_to)
    for k, out in zip(MOVES, outs):
        row = col_target(k, 1)
        for i in range(2):
            out[i] = acc[2 * row + i].astype(jnp.bfloat16)


def backward_products(lists, adj_refs, back, acc, adj_vmem, rows, places, adj_sem, far):
    base = 16 if far else 0
    spare = acc.shape[0] - 1
    n = list_slots(lists, adj_refs, adj_vmem, adj_sem, rows, places, far, (0, base + spare))
    acc[...] = jnp.zeros_like(acc)

    def product(j):
        row = rows[j]
        return lax.dot_general(
            adj_vmem[j],
            back[row >> 1, pl.ds((row & 1) * TILE, TILE), :],
            (((0,), (0,)), ((), ())),
            preferred_element_type=jnp.float32,
        )

    def add_to(j, value):
        acc[places[j] - base] += value

    slot_products(n, adj_refs[0], adj_vmem, adj_sem, product, add_to)


def backward_far_kernel(*refs):
    lists, adj_refs, received, refs = refs[:2], refs[2:4], refs[4:12], refs[12:]
    up, down, back, acc, adj_vmem, rows, places, adj_sem, pieces = refs
    for k, ref in zip(MOVES, received):
        source = col_target(k, -1)
        back[source] = ref[: 2 * TILE, :]
        pieces[source] = ref[2 * TILE :, :]
    backward_products(lists, adj_refs, back, acc, adj_vmem, rows, places, adj_sem, True)
    for k in range(QUAD):
        part = pl.ds((k & 1) * TILE, TILE)
        (up, down)[k >> 1][part, :] = acc[k].astype(jnp.bfloat16)
    piece = pieces[0].astype(jnp.float32)
    for c in range(1, NCOL):
        piece = piece + pieces[c].astype(jnp.float32)
    for out in (up, down):
        out[2 * TILE :, :] = piece.astype(jnp.bfloat16)


def backward_near_kernel(*refs):
    lists, adj_refs, refs = refs[:2], refs[2:4], refs[4:]
    back, out, acc, adj_vmem, rows, places, adj_sem = refs
    backward_products(lists, adj_refs, back, acc, adj_vmem, rows, places, adj_sem, False)
    out[...] = acc[: NZ * QUAD].astype(jnp.bfloat16)


def split(x):
    high = x.astype(jnp.bfloat16)
    return high, (x - high.astype(jnp.float32)).astype(jnp.bfloat16)


def dense_kernel(agg_own, agg_other, weight, cot_own, cot_other, act_out, send, send_x):
    first = (lax.axis_index("row") & 1) == 0
    own = agg_own[...]
    other = jnp.concatenate([agg_other[TILE:, :], agg_other[:TILE, :]], axis=0)
    w = weight[...]
    w_other_half = jnp.where(first, w[HALF:], w[:HALF])
    w_half = jnp.where(first, w[:HALF], w[HALF:])

    def dot(a, b, dims=((1,), (0,))):
        return lax.dot_general(a, b, (dims, ((), ())), preferred_element_type=jnp.float32)

    own_hi, own_lo = split(own)
    other_hi, other_lo = split(other)
    v = (dot(own_hi, w_half) + dot(own_lo, w_half)) + (
        dot(other_hi, w_other_half) + dot(other_lo, w_other_half)
    )
    scale = math.sqrt(2.0 / math.pi)
    square = v * v
    t = jnp.tanh(scale * (v + 0.044715 * (square * v)))
    cdf = 0.5 * (1.0 + t)
    act_out[...] = (v[:TILE] * cdf[:TILE]).astype(jnp.bfloat16)
    slope = cdf + 0.5 * v * ((1.0 - t) * (1.0 + t)) * (scale * (1.0 + 3.0 * 0.044715 * square))
    cot = jnp.concatenate([cot_own[...], cot_other[...]], axis=0).astype(jnp.float32)
    grad_hi, grad_lo = split(cot * slope)
    nodes = ((1,), (1,))
    back = (dot(grad_hi, w_half, nodes) + dot(grad_lo, w_half, nodes)).astype(jnp.bfloat16)
    rows = ((0,), (0,))
    w_part = (
        dot(own_hi, grad_hi, rows) + dot(own_lo, grad_hi, rows) + dot(own_hi, grad_lo, rows)
    )
    x_lo = lax.axis_index("col") >> 2
    for out, dest in ((send, x_lo), (send_x, 1 - x_lo)):
        out[: 2 * TILE, :] = back
        piece = jnp.where(dest == 0, w_part[:64], w_part[64:]).astype(jnp.bfloat16)
        out[2 * TILE : 2 * TILE + 64, :] = piece[:, :HALF]
        out[2 * TILE + 64 :, :] = piece[:, HALF:]


def f32(ref, start, rows=TILE):
    return ref[start : start + rows, :].astype(jnp.float32)


def ring_end_kernel(
    parts, own, up1, up2, up3, up4, down1, down2, down3, down4, kept, message, by_step
):
    z = lax.axis_index("row") >> 2
    half, size = 2 * TILE, QUAD * TILE
    pieces = (
        (own, half),
        (down1, half),
        (down2, size),
        (down3, size),
        (up4, size),
        (up3, size),
        (up2, size),
        (up1, half),
    )
    for k, (ref, start) in enumerate(pieces):
        by_step[(k + z) & 7] = ref[start:, :]
    w_sum = by_step[0].astype(jnp.float32)
    for a in range(1, NZ):
        w_sum = w_sum + by_step[a].astype(jnp.float32)
    message[half:, :] = w_sum.astype(jnp.bfloat16)
    for k in range(QUAD):
        start = k * TILE
        total = parts[k].astype(jnp.float32) + f32(up4, start) + f32(down4, start)
        if k < 2:
            kept[k] = total
        else:
            message[start - half : start - half + TILE, :] = total.astype(jnp.bfloat16)


def middle_kernel(kept, sent, from_x, w_lo, w_both, mine, message, w_here):
    x_lo = lax.axis_index("col") >> 2
    half = 2 * TILE
    for k, ref in enumerate((mine, message)):
        ref[:TILE, :] = (kept[k] + f32(from_x, k * TILE)).astype(jnp.bfloat16)
    sums = (
        f32(sent, half, W_ROWS) + f32(from_x, half, W_ROWS),
        w_lo[...].astype(jnp.float32) + w_both[...].astype(jnp.float32),
    )
    for value, place in zip(sums, (x_lo, 1 - x_lo)):
        high, low = split(value)
        w_here[place] = high.astype(jnp.float32) + low.astype(jnp.float32)
        start = pl.multiple_of(TILE + place * 2 * W_ROWS, W_ROWS)
        message[pl.ds(start, W_ROWS), :] = high
        message[pl.ds(start + W_ROWS, W_ROWS), :] = low


def last_kernel(mine, from_core, w_here, grad_out, w_out):
    core = lax.axis_index("row") & 1
    scale = 1.0 / 256.0

    def place(value, start):
        rows = pl.ds(pl.multiple_of(start, 64), 64)
        w_out[rows, :HALF] = value[:64, :] * scale
        w_out[rows, HALF:] = value[64:, :] * scale

    for x_lo in range(2):
        start = TILE + x_lo * 2 * W_ROWS
        place(w_here[x_lo], core * HALF + x_lo * 64)
        w_core = f32(from_core, start, W_ROWS) + f32(from_core, start + W_ROWS, W_ROWS)
        place(w_core, (1 - core) * HALF + x_lo * 64)

    @pl.when(core == 0)
    def _():
        grad_out[:, :HALF] = mine[...]
        grad_out[:, HALF:] = from_core[:TILE, :]

    @pl.when(core == 1)
    def _():
        grad_out[:, HALF:] = mine[...]
        grad_out[:, :HALF] = from_core[:TILE, :]


SMEM = pl.BlockSpec(memory_space=pltpu.SMEM)
VMEM = pl.BlockSpec(memory_space=pltpu.VMEM)
ANY = pl.BlockSpec(memory_space=pl.ANY)


def params(mib):
    return pltpu.CompilerParams(vmem_limit_bytes=mib << 20)


LIST = 2 * SLOTS + UNROLL
SLOT_SCRATCH = [
    pltpu.VMEM((LIST, TILE, TILE), jnp.bfloat16),
    pltpu.SMEM((LIST,), jnp.int32),
    pltpu.SMEM((LIST,), jnp.int32),
]


def cost(slots, size):
    return pl.CostEstimate(
        flops=slots * 2 * TILE * TILE * HALF, bytes_accessed=size << 20, transcendentals=0
    )


LISTS = [SMEM] * 4


def shape(*dims, dtype=jnp.bfloat16):
    return jax.ShapeDtypeStruct(dims, dtype)


def local(kernel, outs, n_in, name, scalars=0, any_in=0, scratch=(), cost=None, scalar_out=0):
    return pl.pallas_call(
        kernel,
        out_shape=outs,
        in_specs=[SMEM] * scalars + [ANY] * any_in + [VMEM] * (n_in - scalars - any_in),
        out_specs=(VMEM,) * (len(outs) - scalar_out) + (SMEM,) * scalar_out,
        scratch_shapes=scratch,
        compiler_params=params(20),
        cost_estimate=cost,
        name=name,
    )


def prepare(rows, cols, count, block):
    return local(
        prepare_kernel,
        (shape(TILE, HALF), shape(TILE + 16, HALF), shape(25, dtype=jnp.int32)),
        4,
        "prepare",
        scalars=3,
        scalar_out=1,
    )(rows, cols, count, block)


def join(own_keep, own_message, x_block):
    return local(
        join_kernel, (shape(2, TILE, HALF), shape(2 * TILE + 16, HALF)), 3, "join"
    )(own_keep, own_message, x_block)


def forward_near(lists, adj0, adj1, pieces):
    return local(
        forward_near_kernel,
        (shape(17, TILE, HALF, dtype=jnp.float32),),
        11,
        "forward_near",
        scalars=2,
        any_in=9,
        scratch=[pltpu.VMEM((NZ * QUAD, TILE, HALF), jnp.bfloat16)]
        + SLOT_SCRATCH
        + [pltpu.SemaphoreType.DMA((NZ,)), pltpu.SemaphoreType.DMA((LIST,))],
        cost=cost(21, 6),
    )(*lists, adj0, adj1, *pieces)[0]


def forward_far(lists, adj0, adj1, near, far_a, far_b):
    return local(
        forward_far_kernel,
        (shape(2, TILE, HALF),) * NCOL,
        7,
        "forward_far",
        scalars=2,
        any_in=2,
        scratch=[
            pltpu.VMEM((17, TILE, HALF), jnp.float32),
            pltpu.VMEM((QUAD, TILE, HALF), jnp.bfloat16),
        ]
        + SLOT_SCRATCH
        + [pltpu.SemaphoreType.DMA((LIST,))],
        cost=cost(3, 4),
    )(*lists, adj0, adj1, near, far_a, far_b)


def backward_far(lists, adj0, adj1, received):
    message = shape(2 * TILE + W_ROWS, HALF)
    return local(
        backward_far_kernel,
        (message, message, shape(NCOL, 2 * TILE, HALF)),
        12,
        "backward_far",
        scalars=2,
        any_in=2,
        scratch=[pltpu.VMEM((QUAD + 1, TILE, HALF), jnp.float32)]
        + SLOT_SCRATCH
        + [pltpu.SemaphoreType.DMA((LIST,)), pltpu.VMEM((NCOL, W_ROWS, HALF), jnp.bfloat16)],
        cost=cost(3, 2),
    )(*lists, adj0, adj1, *received)


def backward_near(lists, adj0, adj1, back):
    return local(
        backward_near_kernel,
        (shape(NZ * QUAD, TILE, HALF),),
        5,
        "backward_near",
        scalars=2,
        any_in=2,
        scratch=[pltpu.VMEM((NZ * QUAD + 1, TILE, HALF), jnp.float32)]
        + SLOT_SCRATCH
        + [pltpu.SemaphoreType.DMA((LIST,))],
        cost=cost(21, 6),
    )(*lists, adj0, adj1, back)[0]


def dense(agg_own, agg_other, weight, cot_own, cot_other):
    return local(
        dense_kernel,
        (shape(TILE, 2 * HALF),) + (shape(2 * TILE + W_ROWS, HALF),) * 2,
        5,
        "dense",
    )(agg_own, agg_other, weight, cot_own, cot_other)


def ring_end(parts, *messages):
    return local(
        ring_end_kernel,
        (shape(2, TILE, HALF, dtype=jnp.float32), shape(2 * TILE + W_ROWS, HALF)),
        10,
        "ring_end",
        scratch=[pltpu.VMEM((NZ, W_ROWS, HALF), jnp.bfloat16)],
    )(parts, *messages)


def middle(*operands):
    return local(
        middle_kernel,
        (
            shape(TILE, HALF),
            shape(TILE + 4 * W_ROWS, HALF),
            shape(2, W_ROWS, HALF, dtype=jnp.float32),
        ),
        5,
        "middle",
    )(*operands)


def last(mine, from_core, w_here):
    return local(
        last_kernel,
        (shape(TILE, 2 * HALF), shape(2 * HALF, 2 * HALF, dtype=jnp.float32)),
        3,
        "last",
    )(mine, from_core, w_here)


def add(a, b):
    return (a.astype(jnp.float32) + b.astype(jnp.float32)).astype(jnp.bfloat16)


def per_device(features, adj_tiles, tile_row, tile_col, tile_count, weight, cotangent):
    adj0 = adj_tiles[0, 0]
    block = features[0]

    x_block = quad_permute(block, 2)
    keep, message, own_lists = prepare(tile_row[0, 0], tile_col[0, 0], tile_count, block)
    keep, message = join(keep, message, x_block)
    from_core = quad_permute(message, 1)
    core_keep = from_core[16:].reshape(2, TILE, HALF)
    chunk = jnp.stack([keep[0], core_keep[0], keep[1], core_keep[1]])
    lists = (own_lists, from_core[0, :25].astype(jnp.int32))
    adj1 = quad_permute(adj0, 1)
    cot1 = quad_permute(cotangent, 1)

    up1, down1 = z_shift(chunk, 1), z_shift(chunk, -1)
    up2, down2 = z_shift(up1, 1), z_shift(down1, -1)
    up3, down3 = z_shift(up2, 1), z_shift(down2, -1)
    far_a, far_b = z_shift(up3[:2], 1), z_shift(down3[2:], -1)
    near = forward_near(lists, adj0, adj1, [chunk, down1, down2, down3, up3, up2, up1])
    shares = forward_far(lists, adj0, adj1, near, far_a, far_b)
    agg = sum(
        (col_move(share, k) if k else share).astype(jnp.float32)
        for k, share in zip(MOVES, shares)
    ).reshape(2 * TILE, HALF)
    agg_other = quad_permute(agg, 1)
    activated, send, send_x = dense(agg, agg_other, weight, cotangent, cot1)
    received = [col_move(send if k < 4 else send_x, k) if k else send for k in MOVES]

    half, size = 2 * TILE, QUAD * TILE
    own, own_down, back = backward_far(lists, adj0, adj1, received)
    blocks = backward_near(lists, adj0, adj1, back)
    parts = blocks.reshape(NZ, size, HALF)
    up1, down1 = z_shift(own, 1), z_shift(own_down, -1)
    up = [add(parts[3, :half], up1[:half]), parts[3, half:], up1[half:]]
    down = [parts[5, :half], add(parts[5, half:], down1[:half]), down1[half:]]
    up2, down2 = z_shift(jnp.concatenate(up), 1), z_shift(jnp.concatenate(down), -1)
    up = [add(parts[2], up2[:size]), up2[size:]]
    down = [add(parts[6], down2[:size]), down2[size:]]
    up3, down3 = z_shift(jnp.concatenate(up), 1), z_shift(jnp.concatenate(down), -1)
    up4 = z_shift(jnp.concatenate([add(parts[1], up3[:size]), up3[size:]]), 1)
    down4 = z_shift(add(parts[7], down3[:size]), -1)

    kept, to_x = ring_end(blocks, own, up1, up2, up3, up4, down1, down2, down3, down4)
    w_send = to_x[half:]
    from_x = quad_permute(to_x, 2)
    w_lo = lax.ppermute(w_send, "col", [(c, c ^ 4) for c in range(NCOL)])
    both = [
        (r * NCOL + c, (r ^ 2) * NCOL + (c ^ 4)) for r in range(NZ * QUAD) for c in range(NCOL)
    ]
    w_both = lax.ppermute(w_send, ("row", "col"), both)
    mine, to_core, w_here = middle(kept, to_x, from_x, w_lo, w_both)
    grad, weight_grad = last(mine, quad_permute(to_core, 1), w_here)
    return (activated, weight_grad, grad[None])


def solution(mesh):
    return jax.shard_map(
        per_device,
        mesh=mesh,
        in_specs=(
            P("col", "row", None),
            P("row", "col", None, None, None),
            P("row", "col", None),
            P("row", "col", None),
            P("row", "col"),
            P(),
            P(("row", "col"), None),
        ),
        out_specs=(P(("row", "col"), None), P(), P("col", "row", None)),
        check_vma=False,
    )
```

```python
import functools
import math

import jax
import jax.numpy as jnp
from jax import lax
from jax.experimental import pallas as pl
from jax.experimental.pallas import tpu as pltpu
from jax.sharding import PartitionSpec as P

NZ = 8
QUAD = 4
NCOL = 8
TILE = 256
HALF = 128
SLOTS = 12
W_ROWS = 128
UNROLL = 4
PART = 16
LIST = 4 * PART + 4
MOVES = (0, 6, 2, 5, 7, 1, 3, 4)


def row_pairs(move):
    pairs = []
    for r in range(NZ * QUAD):
        z, q = move(r // QUAD, r % QUAD)
        pairs.append((r, (z % NZ) * QUAD + q))
    return pairs


def quad_permute(x, flip):
    return lax.ppermute(x, "row", row_pairs(lambda z, q: (z, q ^ flip)))


def col_move(x, k):
    pairs = [(c, ((c >> 2) ^ (k >> 2)) * 4 + (c + k) % 4) for c in range(NCOL)]
    return lax.ppermute(x, "col", pairs)


def col_target(k, sign):
    c = lax.axis_index("col")
    return (((c >> 2) ^ (k >> 2)) << 2) + ((c + sign * (k & 3)) & 3)


def z_shift(x, step):
    return lax.ppermute(x, "row", row_pairs(lambda z, q: (z + step, q)))


def prepare_kernel(rows, cols, count, block, keep, message, own_lists):
    core = lax.axis_index("row") & 1

    @pl.when(core == 0)
    def _():
        keep[...] = block[:, :HALF]
        message[16:, :] = block[:, HALF:]

    @pl.when(core == 1)
    def _():
        keep[...] = block[:, HALF:]
        message[16:, :] = block[:, :HALF]

    lane = lax.broadcasted_iota(jnp.int32, (16, HALF), 1)
    values = jnp.zeros((16, HALF), jnp.float32)
    listed = [rows[s] for s in range(SLOTS)] + [cols[s] for s in range(SLOTS)] + [count[0, 0]]
    for n, value in enumerate(listed):
        values = jnp.where(lane == n, value.astype(jnp.float32), values)
        own_lists[n] = value
    message[:16, :] = values.astype(jnp.bfloat16)


def join_kernel(own_keep, own_message, x_block, keep, message):
    core = lax.axis_index("row") & 1
    keep[0] = own_keep[...]
    message[: TILE + 16, :] = own_message[...]

    @pl.when(core == 0)
    def _():
        keep[1] = x_block[:, :HALF]
        message[TILE + 16 :, :] = x_block[:, HALF:]

    @pl.when(core == 1)
    def _():
        keep[1] = x_block[:, HALF:]
        message[TILE + 16 :, :] = x_block[:, :HALF]


def list_slots(own, partner, lists):
    device = lax.axis_index("row")
    z, q = device >> 2, device & 3
    for i, slots in enumerate((own, partner)):
        near, far = jnp.int32(0), jnp.int32(0)
        for s in range(SLOTS):
            tile = slots[12 + s]
            place = (((tile >> 2) - z) & 7) * QUAD + ((tile & 3) ^ q)
            live = (s < slots[24]).astype(jnp.int32)
            is_far = ((place >> 2) == 4).astype(jnp.int32)
            lists[i * PART + is_far * (2 * PART + far - near) + near] = (
                s * 1024 + slots[s] * 64 + place
            )
            far = far + live * is_far
            near = near + live * (1 - is_far)
        for u in range(UNROLL - 1):
            lists[i * PART + near + u] = 8 * 64 + 32
        lists[4 * PART + i] = near
        lists[4 * PART + 2 + i] = far


def slot_products(lists, far, adj_refs, product, add_to):
    unroll = 1 if far else UNROLL
    for i, adj in enumerate(adj_refs):
        part = 2 * far + i

        @pl.loop(0, (lists[4 * PART + part] + unroll - 1) // unroll)
        def _(step, i=i, adj=adj, part=part):
            codes = [lists[part * PART + step * unroll + u] for u in range(unroll)]
            places = [((code >> 6) & 15, i, code & 63) for code in codes]
            values = [product(adj[code >> 10], *at) for code, at in zip(codes, places)]
            for value, at in zip(values, places):
                add_to(value, *at)


def forward_near_kernel(own_any, partner_any, adj0, adj1, *refs):
    pieces, (acc, lists, panel, own, partner, sems) = refs[:7], refs[7:]
    copies = [
        pltpu.make_async_copy(own_any, own, sems.at[0]),
        pltpu.make_async_copy(partner_any, partner, sems.at[1]),
    ]
    for copy in copies:
        copy.start()
    for place, piece in zip((0, 1, 2, 3, 5, 6, 7), pieces):
        panel[place * QUAD : (place + 1) * QUAD] = piece[...]
    acc[...] = jnp.zeros_like(acc)
    for copy in copies:
        copy.wait()
    list_slots(own, partner, lists)

    def product(tile, row, i, place):
        return jnp.dot(tile, panel[place & 31], preferred_element_type=jnp.float32)

    def add_to(value, row, i, place):
        acc[2 * row + i] += value

    slot_products(lists, False, (adj0, adj1), product, add_to)


def forward_far_kernel(lists_any, adj0, adj1, near, far_a, far_b, *refs):
    outs, (acc, far, lists, sem) = refs[:NCOL], refs[NCOL:]
    copy = pltpu.make_async_copy(lists_any, lists, sem)
    copy.start()
    far[:2] = far_a[...]
    far[2:] = far_b[...]
    acc[...] = near[...]
    copy.wait()

    def product(tile, row, i, place):
        return jnp.dot(tile, far[place & 3], preferred_element_type=jnp.float32)

    def add_to(value, row, i, place):
        acc[2 * row + i] += value

    slot_products(lists, True, (adj0, adj1), product, add_to)
    for k, out in zip(MOVES, outs):
        row = col_target(k, 1)
        for i in range(2):
            out[i] = acc[2 * row + i].astype(jnp.bfloat16)


def backward_products(lists, adj_refs, back, acc, far):
    def product(tile, row, i, place):
        return lax.dot_general(
            tile,
            back[row & 7, pl.ds(i * TILE, TILE), :],
            (((0,), (0,)), ((), ())),
            preferred_element_type=jnp.float32,
        )

    def add_to(value, row, i, place):
        acc[place & 3 if far else place] += value

    slot_products(lists, far, adj_refs, product, add_to)


def backward_far_kernel(lists_any, adj0, adj1, *refs):
    received, (up, down, back, acc, lists, sem, pieces) = refs[:NCOL], refs[NCOL:]
    copy = pltpu.make_async_copy(lists_any, lists, sem)
    copy.start()
    for k, ref in zip(MOVES, received):
        source = col_target(k, -1)
        back[source] = ref[: 2 * TILE, :]
        pieces[source] = ref[2 * TILE :, :]
    acc[...] = jnp.zeros_like(acc)
    piece = pieces[0].astype(jnp.float32)
    for c in range(1, NCOL):
        piece = piece + pieces[c].astype(jnp.float32)
    for out in (up, down):
        out[2 * TILE :, :] = piece.astype(jnp.bfloat16)
    copy.wait()
    backward_products(lists, (adj0, adj1), back, acc, True)
    for k in range(QUAD):
        part = pl.ds((k & 1) * TILE, TILE)
        (up, down)[k >> 1][part, :] = acc[k].astype(jnp.bfloat16)


def backward_near_kernel(lists_any, adj0, adj1, back, out, acc, lists, sem):
    copy = pltpu.make_async_copy(lists_any, lists, sem)
    copy.start()
    acc[...] = jnp.zeros_like(acc)
    copy.wait()
    backward_products(lists, (adj0, adj1), back, acc, False)
    out[...] = acc[: NZ * QUAD].astype(jnp.bfloat16)


def split(x):
    high = x.astype(jnp.bfloat16)
    return high, (x - high.astype(jnp.float32)).astype(jnp.bfloat16)


def dense_kernel(agg_own, agg_other, weight, cot_own, cot_other, act_out, send, send_x):
    first = (lax.axis_index("row") & 1) == 0
    own = agg_own[...]
    other = jnp.concatenate([agg_other[TILE:, :], agg_other[:TILE, :]], axis=0)
    w = weight[...]
    w_other_half = jnp.where(first, w[HALF:], w[:HALF])
    w_half = jnp.where(first, w[:HALF], w[HALF:])

    def dot(a, b, dims=((1,), (0,))):
        return lax.dot_general(a, b, (dims, ((), ())), preferred_element_type=jnp.float32)

    own_hi, own_lo = split(own)
    other_hi, other_lo = split(other)
    v = (dot(own_hi, w_half) + dot(own_lo, w_half)) + (
        dot(other_hi, w_other_half) + dot(other_lo, w_other_half)
    )
    scale = math.sqrt(2.0 / math.pi)
    square = v * v
    t = jnp.tanh(scale * (v + 0.044715 * (square * v)))
    cdf = 0.5 * (1.0 + t)
    act_out[...] = (v[:TILE] * cdf[:TILE]).astype(jnp.bfloat16)
    slope = cdf + 0.5 * v * ((1.0 - t) * (1.0 + t)) * (scale * (1.0 + 3.0 * 0.044715 * square))
    cot = jnp.concatenate([cot_own[...], cot_other[...]], axis=0).astype(jnp.float32)
    grad_hi, grad_lo = split(cot * slope)
    nodes = ((1,), (1,))
    back = (dot(grad_hi, w_half, nodes) + dot(grad_lo, w_half, nodes)).astype(jnp.bfloat16)
    rows = ((0,), (0,))
    w_part = (
        dot(own_hi, grad_hi, rows) + dot(own_lo, grad_hi, rows) + dot(own_hi, grad_lo, rows)
    )
    x_lo = lax.axis_index("col") >> 2
    for out, dest in ((send, x_lo), (send_x, 1 - x_lo)):
        out[: 2 * TILE, :] = back
        piece = jnp.where(dest == 0, w_part[:64], w_part[64:]).astype(jnp.bfloat16)
        out[2 * TILE : 2 * TILE + 64, :] = piece[:, :HALF]
        out[2 * TILE + 64 :, :] = piece[:, HALF:]


def f32(ref, start, rows=TILE):
    return ref[start : start + rows, :].astype(jnp.float32)


def ring_end_kernel(
    parts, own, up1, up2, up3, up4, down1, down2, down3, down4, kept, message, by_step
):
    z = lax.axis_index("row") >> 2
    half, size = 2 * TILE, QUAD * TILE
    pieces = (
        (own, half),
        (down1, half),
        (down2, size),
        (down3, size),
        (up4, size),
        (up3, size),
        (up2, size),
        (up1, half),
    )
    for k, (ref, start) in enumerate(pieces):
        by_step[(k + z) & 7] = ref[start:, :]
    w_sum = by_step[0].astype(jnp.float32)
    for a in range(1, NZ):
        w_sum = w_sum + by_step[a].astype(jnp.float32)
    message[half:, :] = w_sum.astype(jnp.bfloat16)
    for k in range(QUAD):
        start = k * TILE
        total = parts[k].astype(jnp.float32) + f32(up4, start) + f32(down4, start)
        if k < 2:
            kept[k] = total
        else:
            message[start - half : start - half + TILE, :] = total.astype(jnp.bfloat16)


def middle_kernel(kept, sent, from_x, w_lo, w_both, mine, message, w_here):
    x_lo = lax.axis_index("col") >> 2
    half = 2 * TILE
    for k, ref in enumerate((mine, message)):
        ref[:TILE, :] = (kept[k] + f32(from_x, k * TILE)).astype(jnp.bfloat16)
    sums = (
        f32(sent, half, W_ROWS) + f32(from_x, half, W_ROWS),
        w_lo[...].astype(jnp.float32) + w_both[...].astype(jnp.float32),
    )
    for value, place in zip(sums, (x_lo, 1 - x_lo)):
        high, low = split(value)
        w_here[place] = high.astype(jnp.float32) + low.astype(jnp.float32)
        start = pl.multiple_of(TILE + place * 2 * W_ROWS, W_ROWS)
        message[pl.ds(start, W_ROWS), :] = high
        message[pl.ds(start + W_ROWS, W_ROWS), :] = low


def last_kernel(mine, from_core, w_here, grad_out, w_out):
    core = lax.axis_index("row") & 1
    scale = 1.0 / 256.0

    def place(value, start):
        rows = pl.ds(pl.multiple_of(start, 64), 64)
        w_out[rows, :HALF] = value[:64, :] * scale
        w_out[rows, HALF:] = value[64:, :] * scale

    for x_lo in range(2):
        start = TILE + x_lo * 2 * W_ROWS
        place(w_here[x_lo], core * HALF + x_lo * 64)
        w_core = f32(from_core, start, W_ROWS) + f32(from_core, start + W_ROWS, W_ROWS)
        place(w_core, (1 - core) * HALF + x_lo * 64)

    @pl.when(core == 0)
    def _():
        grad_out[:, :HALF] = mine[...]
        grad_out[:, HALF:] = from_core[:TILE, :]

    @pl.when(core == 1)
    def _():
        grad_out[:, HALF:] = mine[...]
        grad_out[:, :HALF] = from_core[:TILE, :]


SMEM = pl.BlockSpec(memory_space=pltpu.SMEM)
VMEM = pl.BlockSpec(memory_space=pltpu.VMEM)
ANY = pl.BlockSpec(memory_space=pl.ANY)


def params(mib):
    return pltpu.CompilerParams(vmem_limit_bytes=mib << 20)


LIST_SCRATCH = [pltpu.SMEM((LIST,), jnp.int32), pltpu.SemaphoreType.DMA]


def cost(slots, size):
    return pl.CostEstimate(
        flops=slots * 2 * TILE * TILE * HALF, bytes_accessed=size << 20, transcendentals=0
    )


LISTS = [SMEM] * 4


def shape(*dims, dtype=jnp.bfloat16):
    return jax.ShapeDtypeStruct(dims, dtype)


def local(kernel, outs, n_in, name, scalars=0, any_in=0, scratch=(), cost=None, scalar_out=0):
    return pl.pallas_call(
        kernel,
        out_shape=outs,
        in_specs=[SMEM] * scalars + [ANY] * any_in + [VMEM] * (n_in - scalars - any_in),
        out_specs=(VMEM,) * (len(outs) - scalar_out) + (SMEM,) * scalar_out,
        scratch_shapes=scratch,
        compiler_params=params(20),
        cost_estimate=cost,
        name=name,
    )


def prepare(rows, cols, count, block):
    return local(
        prepare_kernel,
        (shape(TILE, HALF), shape(TILE + 16, HALF), shape(25, dtype=jnp.int32)),
        4,
        "prepare",
        scalars=3,
        scalar_out=1,
    )(rows, cols, count, block)


def join(own_keep, own_message, x_block):
    return local(
        join_kernel, (shape(2, TILE, HALF), shape(2 * TILE + 16, HALF)), 3, "join"
    )(own_keep, own_message, x_block)


def forward_near(own, partner, adj0, adj1, pieces):
    return local(
        forward_near_kernel,
        (shape(18, TILE, HALF, dtype=jnp.float32), shape(LIST, dtype=jnp.int32)),
        11,
        "forward_near",
        any_in=2,
        scalar_out=1,
        scratch=[
            pltpu.VMEM((NZ * QUAD, TILE, HALF), jnp.bfloat16),
            pltpu.SMEM((25,), jnp.int32),
            pltpu.SMEM((25,), jnp.int32),
            pltpu.SemaphoreType.DMA((2,)),
        ],
        cost=cost(21, 6),
    )(own, partner, adj0, adj1, *pieces)


def forward_far(lists, adj0, adj1, near, far_a, far_b):
    return local(
        forward_far_kernel,
        (shape(2, TILE, HALF),) * NCOL,
        6,
        "forward_far",
        any_in=1,
        scratch=[
            pltpu.VMEM((18, TILE, HALF), jnp.float32),
            pltpu.VMEM((QUAD, TILE, HALF), jnp.bfloat16),
        ]
        + LIST_SCRATCH,
        cost=cost(3, 4),
    )(lists, adj0, adj1, near, far_a, far_b)


def backward_far(lists, adj0, adj1, received):
    message = shape(2 * TILE + W_ROWS, HALF)
    return local(
        backward_far_kernel,
        (message, message, shape(NCOL, 2 * TILE, HALF)),
        11,
        "backward_far",
        any_in=1,
        scratch=[pltpu.VMEM((QUAD, TILE, HALF), jnp.float32)]
        + LIST_SCRATCH
        + [pltpu.VMEM((NCOL, W_ROWS, HALF), jnp.bfloat16)],
        cost=cost(3, 2),
    )(lists, adj0, adj1, *received)


def backward_near(lists, adj0, adj1, back):
    return local(
        backward_near_kernel,
        (shape(NZ * QUAD, TILE, HALF),),
        4,
        "backward_near",
        any_in=1,
        scratch=[pltpu.VMEM((NZ * QUAD + 1, TILE, HALF), jnp.float32)] + LIST_SCRATCH,
        cost=cost(21, 6),
    )(lists, adj0, adj1, back)[0]


def dense(agg_own, agg_other, weight, cot_own, cot_other):
    return local(
        dense_kernel,
        (shape(TILE, 2 * HALF),) + (shape(2 * TILE + W_ROWS, HALF),) * 2,
        5,
        "dense",
    )(agg_own, agg_other, weight, cot_own, cot_other)


def ring_end(parts, *messages):
    return local(
        ring_end_kernel,
        (shape(2, TILE, HALF, dtype=jnp.float32), shape(2 * TILE + W_ROWS, HALF)),
        10,
        "ring_end",
        scratch=[pltpu.VMEM((NZ, W_ROWS, HALF), jnp.bfloat16)],
    )(parts, *messages)


def middle(*operands):
    return local(
        middle_kernel,
        (
            shape(TILE, HALF),
            shape(TILE + 4 * W_ROWS, HALF),
            shape(2, W_ROWS, HALF, dtype=jnp.float32),
        ),
        5,
        "middle",
    )(*operands)


def last(mine, from_core, w_here):
    return local(
        last_kernel,
        (shape(TILE, 2 * HALF), shape(2 * HALF, 2 * HALF, dtype=jnp.float32)),
        3,
        "last",
    )(mine, from_core, w_here)


def add(a, b):
    return (a.astype(jnp.float32) + b.astype(jnp.float32)).astype(jnp.bfloat16)


def per_device(features, adj_tiles, tile_row, tile_col, tile_count, weight, cotangent):
    adj0 = adj_tiles[0, 0]
    block = features[0]

    x_block = quad_permute(block, 2)
    keep, message, own_lists = prepare(tile_row[0, 0], tile_col[0, 0], tile_count, block)
    keep, message = join(keep, message, x_block)
    from_core = quad_permute(message, 1)
    core_keep = from_core[16:].reshape(2, TILE, HALF)
    chunk = jnp.stack([keep[0], core_keep[0], keep[1], core_keep[1]])
    partner_lists = from_core[0, :25].astype(jnp.int32)
    adj1 = quad_permute(adj0, 1)
    cot1 = quad_permute(cotangent, 1)

    up1, down1 = z_shift(chunk, 1), z_shift(chunk, -1)
    up2, down2 = z_shift(up1, 1), z_shift(down1, -1)
    up3, down3 = z_shift(up2, 1), z_shift(down2, -1)
    far_a, far_b = z_shift(up3[:2], 1), z_shift(down3[2:], -1)
    near, lists = forward_near(
        own_lists, partner_lists, adj0, adj1, [chunk, down1, down2, down3, up3, up2, up1]
    )
    shares = forward_far(lists, adj0, adj1, near, far_a, far_b)
    agg = sum(
        (col_move(share, k) if k else share).astype(jnp.float32)
        for k, share in zip(MOVES, shares)
    ).reshape(2 * TILE, HALF)
    agg_other = quad_permute(agg, 1)
    activated, send, send_x = dense(agg, agg_other, weight, cotangent, cot1)
    received = [col_move(send if k < 4 else send_x, k) if k else send for k in MOVES]

    half, size = 2 * TILE, QUAD * TILE
    own, own_down, back = backward_far(lists, adj0, adj1, received)
    blocks = backward_near(lists, adj0, adj1, back)
    parts = blocks.reshape(NZ, size, HALF)
    up1, down1 = z_shift(own, 1), z_shift(own_down, -1)
    up = [add(parts[3, :half], up1[:half]), parts[3, half:], up1[half:]]
    down = [parts[5, :half], add(parts[5, half:], down1[:half]), down1[half:]]
    up2, down2 = z_shift(jnp.concatenate(up), 1), z_shift(jnp.concatenate(down), -1)
    up = [add(parts[2], up2[:size]), up2[size:]]
    down = [add(parts[6], down2[:size]), down2[size:]]
    up3, down3 = z_shift(jnp.concatenate(up), 1), z_shift(jnp.concatenate(down), -1)
    up4 = z_shift(jnp.concatenate([add(parts[1], up3[:size]), up3[size:]]), 1)
    down4 = z_shift(add(parts[7], down3[:size]), -1)

    kept, to_x = ring_end(blocks, own, up1, up2, up3, up4, down1, down2, down3, down4)
    w_send = to_x[half:]
    from_x = quad_permute(to_x, 2)
    w_lo = lax.ppermute(w_send, "col", [(c, c ^ 4) for c in range(NCOL)])
    both = [
        (r * NCOL + c, (r ^ 2) * NCOL + (c ^ 4)) for r in range(NZ * QUAD) for c in range(NCOL)
    ]
    w_both = lax.ppermute(w_send, ("row", "col"), both)
    mine, to_core, w_here = middle(kept, to_x, from_x, w_lo, w_both)
    grad, weight_grad = last(mine, quad_permute(to_core, 1), w_here)
    return (activated, weight_grad, grad[None])


def solution(mesh):
    return jax.shard_map(
        per_device,
        mesh=mesh,
        in_specs=(
            P("col", "row", None),
            P("row", "col", None, None, None),
            P("row", "col", None),
            P("row", "col", None),
            P("row", "col"),
            P(),
            P(("row", "col"), None),
        ),
        out_specs=(P(("row", "col"), None), P(), P("col", "row", None)),
        check_vma=False,
    )
```

```python
import functools
import math

import jax
import jax.numpy as jnp
from jax import lax
from jax.experimental import pallas as pl
from jax.experimental.pallas import tpu as pltpu
from jax.sharding import PartitionSpec as P

NZ = 8
QUAD = 4
NCOL = 8
TILE = 256
HALF = 128
SLOTS = 12
W_ROWS = 128
UNROLL = 4
PART = 16
LIST = 4 * PART + 4
MOVES = (0, 4, 1, 6, 2, 3, 5, 7)


def row_pairs(move):
    pairs = []
    for r in range(NZ * QUAD):
        z, q = move(r // QUAD, r % QUAD)
        pairs.append((r, (z % NZ) * QUAD + q))
    return pairs


def quad_permute(x, flip):
    return lax.ppermute(x, "row", row_pairs(lambda z, q: (z, q ^ flip)))


def col_move(x, k):
    pairs = [(c, ((c >> 2) ^ (k >> 2)) * 4 + (c + k) % 4) for c in range(NCOL)]
    return lax.ppermute(x, "col", pairs)


def col_target(k, sign):
    c = lax.axis_index("col")
    return (((c >> 2) ^ (k >> 2)) << 2) + ((c + sign * (k & 3)) & 3)


def z_shift(x, step):
    return lax.ppermute(x, "row", row_pairs(lambda z, q: (z + step, q)))


def prepare_kernel(rows, cols, count, block, keep, message, own_lists):
    core = lax.axis_index("row") & 1

    @pl.when(core == 0)
    def _():
        keep[...] = block[:, :HALF]
        message[16:, :] = block[:, HALF:]

    @pl.when(core == 1)
    def _():
        keep[...] = block[:, HALF:]
        message[16:, :] = block[:, :HALF]

    lane = lax.broadcasted_iota(jnp.int32, (16, HALF), 1)
    values = jnp.zeros((16, HALF), jnp.float32)
    listed = [rows[s] for s in range(SLOTS)] + [cols[s] for s in range(SLOTS)] + [count[0, 0]]
    for n, value in enumerate(listed):
        values = jnp.where(lane == n, value.astype(jnp.float32), values)
        own_lists[n] = value
    message[:16, :] = values.astype(jnp.bfloat16)


def join_kernel(own_keep, own_message, x_block, keep, message):
    core = lax.axis_index("row") & 1
    keep[0] = own_keep[...]
    message[: TILE + 16, :] = own_message[...]

    @pl.when(core == 0)
    def _():
        keep[1] = x_block[:, :HALF]
        message[TILE + 16 :, :] = x_block[:, HALF:]

    @pl.when(core == 1)
    def _():
        keep[1] = x_block[:, HALF:]
        message[TILE + 16 :, :] = x_block[:, :HALF]


def list_slots(own, partner, lists):
    device = lax.axis_index("row")
    z, q = device >> 2, device & 3
    for i, slots in enumerate((own, partner)):
        near, far = jnp.int32(0), jnp.int32(0)
        for s in range(SLOTS):
            tile = slots[12 + s]
            place = (((tile >> 2) - z) & 7) * QUAD + ((tile & 3) ^ q)
            live = (s < slots[24]).astype(jnp.int32)
            is_far = ((place >> 2) == 4).astype(jnp.int32)
            lists[i * PART + is_far * (2 * PART + far - near) + near] = (
                s * 1024 + slots[s] * 64 + place
            )
            far = far + live * is_far
            near = near + live * (1 - is_far)
        for u in range(UNROLL - 1):
            lists[i * PART + near + u] = 8 * 64 + 32
        lists[4 * PART + i] = near
        lists[4 * PART + 2 + i] = far


def slot_products(lists, far, adj_refs, product, add_to):
    unroll = 1 if far else UNROLL
    for i, adj in enumerate(adj_refs):
        part = 2 * far + i

        @pl.loop(0, (lists[4 * PART + part] + unroll - 1) // unroll)
        def _(step, i=i, adj=adj, part=part):
            codes = [lists[part * PART + step * unroll + u] for u in range(unroll)]
            places = [((code >> 6) & 15, i, code & 63) for code in codes]
            values = [product(adj[code >> 10], *at) for code, at in zip(codes, places)]
            for value, at in zip(values, places):
                add_to(value, *at)


def forward_near_kernel(own_any, partner_any, cotangent_any, adj0, adj1, *refs):
    del cotangent_any
    pieces, (acc, lists, panel, own, partner, sems) = refs[:7], refs[7:]
    copies = [
        pltpu.make_async_copy(own_any, own, sems.at[0]),
        pltpu.make_async_copy(partner_any, partner, sems.at[1]),
    ]
    for copy in copies:
        copy.start()
    for place, piece in zip((0, 1, 2, 3, 5, 6, 7), pieces):
        panel[place * QUAD : (place + 1) * QUAD] = piece[...]
    acc[...] = jnp.zeros_like(acc)
    for copy in copies:
        copy.wait()
    list_slots(own, partner, lists)

    def product(tile, row, i, place):
        return jnp.dot(tile, panel[place & 31], preferred_element_type=jnp.float32)

    def add_to(value, row, i, place):
        acc[2 * row + i] += value

    slot_products(lists, False, (adj0, adj1), product, add_to)


def forward_far_kernel(lists_any, adj0, adj1, near, far_a, far_b, *refs):
    outs, (acc, far, lists, sem) = refs[:NCOL], refs[NCOL:]
    copy = pltpu.make_async_copy(lists_any, lists, sem)
    copy.start()
    far[:2] = far_a[...]
    far[2:] = far_b[...]
    acc[...] = near[...]
    copy.wait()

    def product(tile, row, i, place):
        return jnp.dot(tile, far[place & 3], preferred_element_type=jnp.float32)

    def add_to(value, row, i, place):
        acc[2 * row + i] += value

    slot_products(lists, True, (adj0, adj1), product, add_to)
    for k, out in zip(MOVES, outs):
        row = col_target(k, 1)
        for i in range(2):
            out[i] = acc[2 * row + i].astype(jnp.bfloat16)


def backward_products(lists, adj_refs, back, acc, far):
    def product(tile, row, i, place):
        return lax.dot_general(
            tile,
            back[row & 7, pl.ds(i * TILE, TILE), :],
            (((0,), (0,)), ((), ())),
            preferred_element_type=jnp.float32,
        )

    def add_to(value, row, i, place):
        acc[place & 3 if far else place] += value

    slot_products(lists, far, adj_refs, product, add_to)


def backward_far_kernel(lists_any, adj0, adj1, *refs):
    received, (up, down, back, acc, lists, sem, pieces) = refs[:NCOL], refs[NCOL:]
    copy = pltpu.make_async_copy(lists_any, lists, sem)
    copy.start()
    for k, ref in zip(MOVES, received):
        source = col_target(k, -1)
        back[source] = ref[: 2 * TILE, :]
        pieces[source] = ref[2 * TILE :, :]
    acc[...] = jnp.zeros_like(acc)
    piece = pieces[0].astype(jnp.float32)
    for c in range(1, NCOL):
        piece = piece + pieces[c].astype(jnp.float32)
    for out in (up, down):
        out[2 * TILE :, :] = piece.astype(jnp.bfloat16)
    copy.wait()
    backward_products(lists, (adj0, adj1), back, acc, True)
    for k in range(QUAD):
        part = pl.ds((k & 1) * TILE, TILE)
        (up, down)[k >> 1][part, :] = acc[k].astype(jnp.bfloat16)


def backward_near_kernel(lists_any, adj0, adj1, back, out, acc, lists, sem):
    copy = pltpu.make_async_copy(lists_any, lists, sem)
    copy.start()
    acc[...] = jnp.zeros_like(acc)
    copy.wait()
    backward_products(lists, (adj0, adj1), back, acc, False)
    out[...] = acc[: NZ * QUAD].astype(jnp.bfloat16)


def split(x):
    high = x.astype(jnp.bfloat16)
    return high, (x - high.astype(jnp.float32)).astype(jnp.bfloat16)


def dense_kernel(agg_own, agg_other, weight, cot_own, cot_other, act_out, send, send_x):
    first = (lax.axis_index("row") & 1) == 0
    own = agg_own[...]
    other = jnp.concatenate([agg_other[TILE:, :], agg_other[:TILE, :]], axis=0)
    w = weight[...]
    w_other_half = jnp.where(first, w[HALF:], w[:HALF])
    w_half = jnp.where(first, w[:HALF], w[HALF:])

    def dot(a, b, dims=((1,), (0,))):
        return lax.dot_general(a, b, (dims, ((), ())), preferred_element_type=jnp.float32)

    own_hi, own_lo = split(own)
    other_hi, other_lo = split(other)
    v = (dot(own_hi, w_half) + dot(own_lo, w_half)) + (
        dot(other_hi, w_other_half) + dot(other_lo, w_other_half)
    )
    scale = math.sqrt(2.0 / math.pi)
    square = v * v
    t = jnp.tanh(scale * (v + 0.044715 * (square * v)))
    cdf = 0.5 * (1.0 + t)
    act_out[...] = (v[:TILE] * cdf[:TILE]).astype(jnp.bfloat16)
    slope = cdf + 0.5 * v * ((1.0 - t) * (1.0 + t)) * (scale * (1.0 + 3.0 * 0.044715 * square))
    cot = jnp.concatenate([cot_own[...], cot_other[...]], axis=0).astype(jnp.float32)
    grad_hi, grad_lo = split(cot * slope)
    nodes = ((1,), (1,))
    back = (dot(grad_hi, w_half, nodes) + dot(grad_lo, w_half, nodes)).astype(jnp.bfloat16)
    rows = ((0,), (0,))
    w_part = (
        dot(own_hi, grad_hi, rows) + dot(own_lo, grad_hi, rows) + dot(own_hi, grad_lo, rows)
    )
    x_lo = lax.axis_index("col") >> 2
    for out, dest in ((send, x_lo), (send_x, 1 - x_lo)):
        out[: 2 * TILE, :] = back
        piece = jnp.where(dest == 0, w_part[:64], w_part[64:]).astype(jnp.bfloat16)
        out[2 * TILE : 2 * TILE + 64, :] = piece[:, :HALF]
        out[2 * TILE + 64 :, :] = piece[:, HALF:]


def f32(ref, start, rows=TILE):
    return ref[start : start + rows, :].astype(jnp.float32)


def ring_end_kernel(
    parts, own, up1, up2, up3, up4, down1, down2, down3, down4, kept, message, by_step
):
    z = lax.axis_index("row") >> 2
    half, size = 2 * TILE, QUAD * TILE
    pieces = (
        (own, half),
        (down1, half),
        (down2, size),
        (down3, size),
        (up4, size),
        (up3, size),
        (up2, size),
        (up1, half),
    )
    for k, (ref, start) in enumerate(pieces):
        by_step[(k + z) & 7] = ref[start:, :]
    w_sum = by_step[0].astype(jnp.float32)
    for a in range(1, NZ):
        w_sum = w_sum + by_step[a].astype(jnp.float32)
    message[half:, :] = w_sum.astype(jnp.bfloat16)
    for k in range(QUAD):
        start = k * TILE
        total = parts[k].astype(jnp.float32) + f32(up4, start) + f32(down4, start)
        if k < 2:
            kept[k] = total
        else:
            message[start - half : start - half + TILE, :] = total.astype(jnp.bfloat16)


def middle_kernel(kept, sent, from_x, w_lo, w_both, mine, message, w_here):
    x_lo = lax.axis_index("col") >> 2
    half = 2 * TILE
    for k, ref in enumerate((mine, message)):
        ref[:TILE, :] = (kept[k] + f32(from_x, k * TILE)).astype(jnp.bfloat16)
    sums = (
        f32(sent, half, W_ROWS) + f32(from_x, half, W_ROWS),
        w_lo[...].astype(jnp.float32) + w_both[...].astype(jnp.float32),
    )
    for value, place in zip(sums, (x_lo, 1 - x_lo)):
        high, low = split(value)
        w_here[place] = high.astype(jnp.float32) + low.astype(jnp.float32)
        start = pl.multiple_of(TILE + place * 2 * W_ROWS, W_ROWS)
        message[pl.ds(start, W_ROWS), :] = high
        message[pl.ds(start + W_ROWS, W_ROWS), :] = low


def last_kernel(mine, from_core, w_here, grad_out, w_out):
    core = lax.axis_index("row") & 1
    scale = 1.0 / 256.0

    def place(value, start):
        rows = pl.ds(pl.multiple_of(start, 64), 64)
        w_out[rows, :HALF] = value[:64, :] * scale
        w_out[rows, HALF:] = value[64:, :] * scale

    for x_lo in range(2):
        start = TILE + x_lo * 2 * W_ROWS
        place(w_here[x_lo], core * HALF + x_lo * 64)
        w_core = f32(from_core, start, W_ROWS) + f32(from_core, start + W_ROWS, W_ROWS)
        place(w_core, (1 - core) * HALF + x_lo * 64)

    @pl.when(core == 0)
    def _():
        grad_out[:, :HALF] = mine[...]
        grad_out[:, HALF:] = from_core[:TILE, :]

    @pl.when(core == 1)
    def _():
        grad_out[:, HALF:] = mine[...]
        grad_out[:, :HALF] = from_core[:TILE, :]


SMEM = pl.BlockSpec(memory_space=pltpu.SMEM)
VMEM = pl.BlockSpec(memory_space=pltpu.VMEM)
ANY = pl.BlockSpec(memory_space=pl.ANY)


def params(mib):
    return pltpu.CompilerParams(vmem_limit_bytes=mib << 20)


LIST_SCRATCH = [pltpu.SMEM((LIST,), jnp.int32), pltpu.SemaphoreType.DMA]


def cost(slots, size):
    return pl.CostEstimate(
        flops=slots * 2 * TILE * TILE * HALF, bytes_accessed=size << 20, transcendentals=0
    )


LISTS = [SMEM] * 4


def shape(*dims, dtype=jnp.bfloat16):
    return jax.ShapeDtypeStruct(dims, dtype)


def local(kernel, outs, n_in, name, scalars=0, any_in=0, scratch=(), cost=None, scalar_out=0):
    return pl.pallas_call(
        kernel,
        out_shape=outs,
        in_specs=[SMEM] * scalars + [ANY] * any_in + [VMEM] * (n_in - scalars - any_in),
        out_specs=(VMEM,) * (len(outs) - scalar_out) + (SMEM,) * scalar_out,
        scratch_shapes=scratch,
        compiler_params=params(20),
        cost_estimate=cost,
        name=name,
    )


def prepare(rows, cols, count, block):
    return local(
        prepare_kernel,
        (shape(TILE, HALF), shape(TILE + 16, HALF), shape(25, dtype=jnp.int32)),
        4,
        "prepare",
        scalars=3,
        scalar_out=1,
    )(rows, cols, count, block)


def join(own_keep, own_message, x_block):
    return local(
        join_kernel, (shape(2, TILE, HALF), shape(2 * TILE + 16, HALF)), 3, "join"
    )(own_keep, own_message, x_block)


def forward_near(own, partner, cotangent, adj0, adj1, pieces):
    return local(
        forward_near_kernel,
        (shape(18, TILE, HALF, dtype=jnp.float32), shape(LIST, dtype=jnp.int32)),
        12,
        "forward_near",
        any_in=3,
        scalar_out=1,
        scratch=[
            pltpu.VMEM((NZ * QUAD, TILE, HALF), jnp.bfloat16),
            pltpu.SMEM((25,), jnp.int32),
            pltpu.SMEM((25,), jnp.int32),
            pltpu.SemaphoreType.DMA((2,)),
        ],
        cost=cost(21, 6),
    )(own, partner, cotangent, adj0, adj1, *pieces)


def forward_far(lists, adj0, adj1, near, far_a, far_b):
    return local(
        forward_far_kernel,
        (shape(2, TILE, HALF),) * NCOL,
        6,
        "forward_far",
        any_in=1,
        scratch=[
            pltpu.VMEM((18, TILE, HALF), jnp.float32),
            pltpu.VMEM((QUAD, TILE, HALF), jnp.bfloat16),
        ]
        + LIST_SCRATCH,
        cost=cost(3, 4),
    )(lists, adj0, adj1, near, far_a, far_b)


def backward_far(lists, adj0, adj1, received):
    message = shape(2 * TILE + W_ROWS, HALF)
    return local(
        backward_far_kernel,
        (message, message, shape(NCOL, 2 * TILE, HALF)),
        11,
        "backward_far",
        any_in=1,
        scratch=[pltpu.VMEM((QUAD, TILE, HALF), jnp.float32)]
        + LIST_SCRATCH
        + [pltpu.VMEM((NCOL, W_ROWS, HALF), jnp.bfloat16)],
        cost=cost(3, 2),
    )(lists, adj0, adj1, *received)


def backward_near(lists, adj0, adj1, back):
    return local(
        backward_near_kernel,
        (shape(NZ * QUAD, TILE, HALF),),
        4,
        "backward_near",
        any_in=1,
        scratch=[pltpu.VMEM((NZ * QUAD + 1, TILE, HALF), jnp.float32)] + LIST_SCRATCH,
        cost=cost(21, 6),
    )(lists, adj0, adj1, back)[0]


def dense(agg_own, agg_other, weight, cot_own, cot_other):
    return local(
        dense_kernel,
        (shape(TILE, 2 * HALF),) + (shape(2 * TILE + W_ROWS, HALF),) * 2,
        5,
        "dense",
    )(agg_own, agg_other, weight, cot_own, cot_other)


def ring_end(parts, *messages):
    return local(
        ring_end_kernel,
        (shape(2, TILE, HALF, dtype=jnp.float32), shape(2 * TILE + W_ROWS, HALF)),
        10,
        "ring_end",
        scratch=[pltpu.VMEM((NZ, W_ROWS, HALF), jnp.bfloat16)],
    )(parts, *messages)


def middle(*operands):
    return local(
        middle_kernel,
        (
            shape(TILE, HALF),
            shape(TILE + 4 * W_ROWS, HALF),
            shape(2, W_ROWS, HALF, dtype=jnp.float32),
        ),
        5,
        "middle",
    )(*operands)


def last(mine, from_core, w_here):
    return local(
        last_kernel,
        (shape(TILE, 2 * HALF), shape(2 * HALF, 2 * HALF, dtype=jnp.float32)),
        3,
        "last",
    )(mine, from_core, w_here)


def add(a, b):
    return (a.astype(jnp.float32) + b.astype(jnp.float32)).astype(jnp.bfloat16)


def per_device(features, adj_tiles, tile_row, tile_col, tile_count, weight, cotangent):
    adj0 = adj_tiles[0, 0]
    block = features[0]

    x_block = quad_permute(block, 2)
    keep, message, own_lists = prepare(tile_row[0, 0], tile_col[0, 0], tile_count, block)
    keep, message = join(keep, message, x_block)
    from_core = quad_permute(message, 1)
    core_keep = from_core[16:].reshape(2, TILE, HALF)
    chunk = jnp.stack([keep[0], core_keep[0], keep[1], core_keep[1]])
    partner_lists = from_core[0, :25].astype(jnp.int32)
    adj1 = quad_permute(adj0, 1)
    cot1 = quad_permute(cotangent, 1)

    up1, down1 = z_shift(chunk, 1), z_shift(chunk, -1)
    up2, down2 = z_shift(up1, 1), z_shift(down1, -1)
    up3, down3 = z_shift(up2, 1), z_shift(down2, -1)
    far_a, far_b = z_shift(up3[:2], 1), z_shift(down3[2:], -1)
    near, lists = forward_near(
        own_lists, partner_lists, cot1, adj0, adj1, [chunk, down1, down2, down3, up3, up2, up1]
    )
    shares = forward_far(lists, adj0, adj1, near, far_a, far_b)
    agg = sum(
        (col_move(share, k) if k else share).astype(jnp.float32)
        for k, share in zip(MOVES, shares)
    ).reshape(2 * TILE, HALF)
    agg_other = quad_permute(agg, 1)
    activated, send, send_x = dense(agg, agg_other, weight, cotangent, cot1)
    received = [col_move(send if k < 4 else send_x, k) if k else send for k in MOVES]

    half, size = 2 * TILE, QUAD * TILE
    own, own_down, back = backward_far(lists, adj0, adj1, received)
    blocks = backward_near(lists, adj0, adj1, back)
    parts = blocks.reshape(NZ, size, HALF)
    up1, down1 = z_shift(own, 1), z_shift(own_down, -1)
    up = [add(parts[3, :half], up1[:half]), parts[3, half:], up1[half:]]
    down = [parts[5, :half], add(parts[5, half:], down1[:half]), down1[half:]]
    up2, down2 = z_shift(jnp.concatenate(up), 1), z_shift(jnp.concatenate(down), -1)
    up = [add(parts[2], up2[:size]), up2[size:]]
    down = [add(parts[6], down2[:size]), down2[size:]]
    up3, down3 = z_shift(jnp.concatenate(up), 1), z_shift(jnp.concatenate(down), -1)
    up4 = z_shift(jnp.concatenate([add(parts[1], up3[:size]), up3[size:]]), 1)
    down4 = z_shift(add(parts[7], down3[:size]), -1)

    kept, to_x = ring_end(blocks, own, up1, up2, up3, up4, down1, down2, down3, down4)
    w_send = to_x[half:]
    from_x = quad_permute(to_x, 2)
    w_lo = lax.ppermute(w_send, "col", [(c, c ^ 4) for c in range(NCOL)])
    both = [
        (r * NCOL + c, (r ^ 2) * NCOL + (c ^ 4)) for r in range(NZ * QUAD) for c in range(NCOL)
    ]
    w_both = lax.ppermute(w_send, ("row", "col"), both)
    mine, to_core, w_here = middle(kept, to_x, from_x, w_lo, w_both)
    grad, weight_grad = last(mine, quad_permute(to_core, 1), w_here)
    return (activated, weight_grad, grad[None])


def solution(mesh):
    return jax.shard_map(
        per_device,
        mesh=mesh,
        in_specs=(
            P("col", "row", None),
            P("row", "col", None, None, None),
            P("row", "col", None),
            P("row", "col", None),
            P("row", "col"),
            P(),
            P(("row", "col"), None),
        ),
        out_specs=(P(("row", "col"), None), P(), P("col", "row", None)),
        check_vma=False,
    )
```

```python
import functools
import math

import jax
import jax.numpy as jnp
from jax import lax
from jax.experimental import pallas as pl
from jax.experimental.pallas import tpu as pltpu
from jax.sharding import PartitionSpec as P

NZ = 8
QUAD = 4
NCOL = 8
TILE = 256
HALF = 128
SLOTS = 12
W_ROWS = 128
UNROLL = 4
PART = 16
LIST = 4 * PART + 4
NEAR_MOVES = (0, 1, 5, 3, 7, 4)
MOVES = (0, 6, 2, 5, 7, 1, 3, 4)


def row_pairs(move):
    pairs = []
    for r in range(NZ * QUAD):
        z, q = move(r // QUAD, r % QUAD)
        pairs.append((r, (z % NZ) * QUAD + q))
    return pairs


def quad_permute(x, flip):
    return lax.ppermute(x, "row", row_pairs(lambda z, q: (z, q ^ flip)))


def col_move(x, k):
    pairs = [(c, ((c >> 2) ^ (k >> 2)) * 4 + (c + k) % 4) for c in range(NCOL)]
    return lax.ppermute(x, "col", pairs)


def col_target(k, sign):
    c = lax.axis_index("col")
    return (((c >> 2) ^ (k >> 2)) << 2) + ((c + sign * (k & 3)) & 3)


def z_shift(x, step):
    return lax.ppermute(x, "row", row_pairs(lambda z, q: (z + step, q)))


def prepare_kernel(rows, cols, count, block, keep, message, own_lists):
    core = lax.axis_index("row") & 1

    @pl.when(core == 0)
    def _():
        keep[...] = block[:, :HALF]
        message[16:, :] = block[:, HALF:]

    @pl.when(core == 1)
    def _():
        keep[...] = block[:, HALF:]
        message[16:, :] = block[:, :HALF]

    lane = lax.broadcasted_iota(jnp.int32, (16, HALF), 1)
    values = jnp.zeros((16, HALF), jnp.float32)
    listed = [rows[s] for s in range(SLOTS)] + [cols[s] for s in range(SLOTS)] + [count[0, 0]]
    for n, value in enumerate(listed):
        values = jnp.where(lane == n, value.astype(jnp.float32), values)
        own_lists[n] = value
    message[:16, :] = values.astype(jnp.bfloat16)


def join_kernel(own_keep, own_message, x_block, keep, message):
    core = lax.axis_index("row") & 1
    keep[0] = own_keep[...]
    message[: TILE + 16, :] = own_message[...]

    @pl.when(core == 0)
    def _():
        keep[1] = x_block[:, :HALF]
        message[TILE + 16 :, :] = x_block[:, HALF:]

    @pl.when(core == 1)
    def _():
        keep[1] = x_block[:, HALF:]
        message[TILE + 16 :, :] = x_block[:, :HALF]


def list_slots(own, partner, lists):
    device = lax.axis_index("row")
    z, q = device >> 2, device & 3
    for i, slots in enumerate((own, partner)):
        near, far = jnp.int32(0), jnp.int32(0)
        for s in range(SLOTS):
            tile = slots[12 + s]
            place = (((tile >> 2) - z) & 7) * QUAD + ((tile & 3) ^ q)
            live = (s < slots[24]).astype(jnp.int32)
            is_far = ((place >> 2) == 4).astype(jnp.int32)
            lists[i * PART + is_far * (2 * PART + far - near) + near] = (
                s * 1024 + slots[s] * 64 + place
            )
            far = far + live * is_far
            near = near + live * (1 - is_far)
        for u in range(UNROLL - 1):
            lists[i * PART + near + u] = 8 * 64 + 32
        lists[4 * PART + i] = near
        lists[4 * PART + 2 + i] = far


def slot_products(lists, far, adj_refs, product, add_to):
    unroll = 1 if far else UNROLL
    for i, adj in enumerate(adj_refs):
        part = 2 * far + i

        @pl.loop(0, (lists[4 * PART + part] + unroll - 1) // unroll)
        def _(step, i=i, adj=adj, part=part):
            codes = [lists[part * PART + step * unroll + u] for u in range(unroll)]
            places = [((code >> 6) & 15, i, code & 63) for code in codes]
            values = [product(adj[code >> 10], *at) for code, at in zip(codes, places)]
            for value, at in zip(values, places):
                add_to(value, *at)


def forward_near_kernel(own_any, partner_any, adj0, adj1, *refs):
    pieces, (acc, lists, panel, own, partner, sems) = refs[:7], refs[7:]
    copies = [
        pltpu.make_async_copy(own_any, own, sems.at[0]),
        pltpu.make_async_copy(partner_any, partner, sems.at[1]),
    ]
    for copy in copies:
        copy.start()
    for place, piece in zip((0, 1, 2, 3, 5, 6, 7), pieces):
        panel[place * QUAD : (place + 1) * QUAD] = piece[...]
    acc[...] = jnp.zeros_like(acc)
    for copy in copies:
        copy.wait()
    list_slots(own, partner, lists)

    def product(tile, row, i, place):
        return jnp.dot(tile, panel[place & 31], preferred_element_type=jnp.float32)

    def add_to(value, row, i, place):
        acc[2 * row + i] += value

    slot_products(lists, False, (adj0, adj1), product, add_to)


def forward_far_kernel(lists_any, adj0, adj1, near, far_a, far_b, *refs):
    outs, (acc, far, lists, sem) = refs[:NCOL], refs[NCOL:]
    copy = pltpu.make_async_copy(lists_any, lists, sem)
    copy.start()
    far[:2] = far_a[...]
    far[2:] = far_b[...]
    acc[...] = near[...]
    copy.wait()

    def product(tile, row, i, place):
        return jnp.dot(tile, far[place & 3], preferred_element_type=jnp.float32)

    def add_to(value, row, i, place):
        acc[2 * row + i] += value

    slot_products(lists, True, (adj0, adj1), product, add_to)
    for k, out in zip(MOVES, outs):
        row = col_target(k, 1)
        for i in range(2):
            out[i] = acc[2 * row + i].astype(jnp.bfloat16)


def backward_products(lists, adj_refs, back, acc, far):
    def product(tile, row, i, place):
        return lax.dot_general(
            tile,
            back[row & 7, pl.ds(i * TILE, TILE), :],
            (((0,), (0,)), ((), ())),
            preferred_element_type=jnp.float32,
        )

    def add_to(value, row, i, place):
        acc[place & 3 if far else place] += value

    slot_products(lists, far, adj_refs, product, add_to)


def backward_far_kernel(lists_any, adj0, adj1, *refs):
    received, (up, down, back, acc, lists, sem, pieces) = refs[:NCOL], refs[NCOL:]
    copy = pltpu.make_async_copy(lists_any, lists, sem)
    copy.start()
    for k, ref in zip(NEAR_MOVES, received):
        source = col_target(k, -1)
        back[source] = ref[: 2 * TILE, :]
        pieces[source] = ref[2 * TILE :, :]
    for h, ref in enumerate(received[len(NEAR_MOVES) :]):
        for j, k in enumerate((2, 6)):
            source = col_target(k, -1)
            start = j * (TILE + W_ROWS // 2)
            back[source, h * TILE : (h + 1) * TILE, :] = ref[start : start + TILE, :]
            pieces[source, h * W_ROWS // 2 : (h + 1) * W_ROWS // 2, :] = ref[
                start + TILE : start + TILE + W_ROWS // 2, :
            ]
    acc[...] = jnp.zeros_like(acc)
    piece = pieces[0].astype(jnp.float32)
    for c in range(1, NCOL):
        piece = piece + pieces[c].astype(jnp.float32)
    for out in (up, down):
        out[2 * TILE :, :] = piece.astype(jnp.bfloat16)
    copy.wait()
    backward_products(lists, (adj0, adj1), back, acc, True)
    for k in range(QUAD):
        part = pl.ds((k & 1) * TILE, TILE)
        (up, down)[k >> 1][part, :] = acc[k].astype(jnp.bfloat16)


def backward_near_kernel(lists_any, adj0, adj1, back, out, acc, lists, sem):
    copy = pltpu.make_async_copy(lists_any, lists, sem)
    copy.start()
    acc[...] = jnp.zeros_like(acc)
    copy.wait()
    backward_products(lists, (adj0, adj1), back, acc, False)
    out[...] = acc[: NZ * QUAD].astype(jnp.bfloat16)


def split(x):
    high = x.astype(jnp.bfloat16)
    return high, (x - high.astype(jnp.float32)).astype(jnp.bfloat16)


def dense_kernel(agg_own, agg_other, weight, cot_own, cot_other, act_out, send, send_x):
    first = (lax.axis_index("row") & 1) == 0
    own = agg_own[...]
    other = jnp.concatenate([agg_other[TILE:, :], agg_other[:TILE, :]], axis=0)
    w = weight[...]
    w_other_half = jnp.where(first, w[HALF:], w[:HALF])
    w_half = jnp.where(first, w[:HALF], w[HALF:])

    def dot(a, b, dims=((1,), (0,))):
        return lax.dot_general(a, b, (dims, ((), ())), preferred_element_type=jnp.float32)

    own_hi, own_lo = split(own)
    other_hi, other_lo = split(other)
    v = (dot(own_hi, w_half) + dot(own_lo, w_half)) + (
        dot(other_hi, w_other_half) + dot(other_lo, w_other_half)
    )
    scale = math.sqrt(2.0 / math.pi)
    square = v * v
    t = jnp.tanh(scale * (v + 0.044715 * (square * v)))
    cdf = 0.5 * (1.0 + t)
    act_out[...] = (v[:TILE] * cdf[:TILE]).astype(jnp.bfloat16)
    slope = cdf + 0.5 * v * ((1.0 - t) * (1.0 + t)) * (scale * (1.0 + 3.0 * 0.044715 * square))
    cot = jnp.concatenate([cot_own[...], cot_other[...]], axis=0).astype(jnp.float32)
    grad_hi, grad_lo = split(cot * slope)
    nodes = ((1,), (1,))
    back = (dot(grad_hi, w_half, nodes) + dot(grad_lo, w_half, nodes)).astype(jnp.bfloat16)
    rows = ((0,), (0,))
    w_part = (
        dot(own_hi, grad_hi, rows) + dot(own_lo, grad_hi, rows) + dot(own_hi, grad_lo, rows)
    )
    x_lo = lax.axis_index("col") >> 2
    for out, dest in ((send, x_lo), (send_x, 1 - x_lo)):
        out[: 2 * TILE, :] = back
        piece = jnp.where(dest == 0, w_part[:64], w_part[64:]).astype(jnp.bfloat16)
        out[2 * TILE : 2 * TILE + 64, :] = piece[:, :HALF]
        out[2 * TILE + 64 :, :] = piece[:, HALF:]


def f32(ref, start, rows=TILE):
    return ref[start : start + rows, :].astype(jnp.float32)


def ring_end_kernel(
    parts, own, up1, up2, up3, up4, down1, down2, down3, down4, kept, message, by_step
):
    z = lax.axis_index("row") >> 2
    half, size = 2 * TILE, QUAD * TILE
    pieces = (
        (own, half),
        (down1, half),
        (down2, size),
        (down3, size),
        (up4, size),
        (up3, size),
        (up2, size),
        (up1, half),
    )
    for k, (ref, start) in enumerate(pieces):
        by_step[(k + z) & 7] = ref[start:, :]
    w_sum = by_step[0].astype(jnp.float32)
    for a in range(1, NZ):
        w_sum = w_sum + by_step[a].astype(jnp.float32)
    message[half:, :] = w_sum.astype(jnp.bfloat16)
    for k in range(QUAD):
        start = k * TILE
        total = parts[k].astype(jnp.float32) + f32(up4, start) + f32(down4, start)
        if k < 2:
            kept[k] = total
        else:
            message[start - half : start - half + TILE, :] = total.astype(jnp.bfloat16)


def middle_kernel(kept, sent, from_x, w_lo, w_both, mine, message, w_here):
    x_lo = lax.axis_index("col") >> 2
    half = 2 * TILE
    for k, ref in enumerate((mine, message)):
        ref[:TILE, :] = (kept[k] + f32(from_x, k * TILE)).astype(jnp.bfloat16)
    sums = (
        f32(sent, half, W_ROWS) + f32(from_x, half, W_ROWS),
        w_lo[...].astype(jnp.float32) + w_both[...].astype(jnp.float32),
    )
    for value, place in zip(sums, (x_lo, 1 - x_lo)):
        high, low = split(value)
        w_here[place] = high.astype(jnp.float32) + low.astype(jnp.float32)
        start = pl.multiple_of(TILE + place * 2 * W_ROWS, W_ROWS)
        message[pl.ds(start, W_ROWS), :] = high
        message[pl.ds(start + W_ROWS, W_ROWS), :] = low


def last_kernel(mine, from_core, w_here, grad_out, w_out):
    core = lax.axis_index("row") & 1
    scale = 1.0 / 256.0

    def place(value, start):
        rows = pl.ds(pl.multiple_of(start, 64), 64)
        w_out[rows, :HALF] = value[:64, :] * scale
        w_out[rows, HALF:] = value[64:, :] * scale

    for x_lo in range(2):
        start = TILE + x_lo * 2 * W_ROWS
        place(w_here[x_lo], core * HALF + x_lo * 64)
        w_core = f32(from_core, start, W_ROWS) + f32(from_core, start + W_ROWS, W_ROWS)
        place(w_core, (1 - core) * HALF + x_lo * 64)

    @pl.when(core == 0)
    def _():
        grad_out[:, :HALF] = mine[...]
        grad_out[:, HALF:] = from_core[:TILE, :]

    @pl.when(core == 1)
    def _():
        grad_out[:, HALF:] = mine[...]
        grad_out[:, :HALF] = from_core[:TILE, :]


SMEM = pl.BlockSpec(memory_space=pltpu.SMEM)
VMEM = pl.BlockSpec(memory_space=pltpu.VMEM)
ANY = pl.BlockSpec(memory_space=pl.ANY)


def params(mib):
    return pltpu.CompilerParams(vmem_limit_bytes=mib << 20)


LIST_SCRATCH = [pltpu.SMEM((LIST,), jnp.int32), pltpu.SemaphoreType.DMA]


def cost(slots, size):
    return pl.CostEstimate(
        flops=slots * 2 * TILE * TILE * HALF, bytes_accessed=size << 20, transcendentals=0
    )


LISTS = [SMEM] * 4


def shape(*dims, dtype=jnp.bfloat16):
    return jax.ShapeDtypeStruct(dims, dtype)


def local(kernel, outs, n_in, name, scalars=0, any_in=0, scratch=(), cost=None, scalar_out=0):
    return pl.pallas_call(
        kernel,
        out_shape=outs,
        in_specs=[SMEM] * scalars + [ANY] * any_in + [VMEM] * (n_in - scalars - any_in),
        out_specs=(VMEM,) * (len(outs) - scalar_out) + (SMEM,) * scalar_out,
        scratch_shapes=scratch,
        compiler_params=params(20),
        cost_estimate=cost,
        name=name,
    )


def prepare(rows, cols, count, block):
    return local(
        prepare_kernel,
        (shape(TILE, HALF), shape(TILE + 16, HALF), shape(25, dtype=jnp.int32)),
        4,
        "prepare",
        scalars=3,
        scalar_out=1,
    )(rows, cols, count, block)


def join(own_keep, own_message, x_block):
    return local(
        join_kernel, (shape(2, TILE, HALF), shape(2 * TILE + 16, HALF)), 3, "join"
    )(own_keep, own_message, x_block)


def forward_near(own, partner, adj0, adj1, pieces):
    return local(
        forward_near_kernel,
        (shape(18, TILE, HALF, dtype=jnp.float32), shape(LIST, dtype=jnp.int32)),
        11,
        "forward_near",
        any_in=2,
        scalar_out=1,
        scratch=[
            pltpu.VMEM((NZ * QUAD, TILE, HALF), jnp.bfloat16),
            pltpu.SMEM((25,), jnp.int32),
            pltpu.SMEM((25,), jnp.int32),
            pltpu.SemaphoreType.DMA((2,)),
        ],
        cost=cost(21, 6),
    )(own, partner, adj0, adj1, *pieces)


def forward_far(lists, adj0, adj1, near, far_a, far_b):
    return local(
        forward_far_kernel,
        (shape(2, TILE, HALF),) * NCOL,
        6,
        "forward_far",
        any_in=1,
        scratch=[
            pltpu.VMEM((18, TILE, HALF), jnp.float32),
            pltpu.VMEM((QUAD, TILE, HALF), jnp.bfloat16),
        ]
        + LIST_SCRATCH,
        cost=cost(3, 4),
    )(lists, adj0, adj1, near, far_a, far_b)


def backward_far(lists, adj0, adj1, received):
    message = shape(2 * TILE + W_ROWS, HALF)
    return local(
        backward_far_kernel,
        (message, message, shape(NCOL, 2 * TILE, HALF)),
        11,
        "backward_far",
        any_in=1,
        scratch=[pltpu.VMEM((QUAD, TILE, HALF), jnp.float32)]
        + LIST_SCRATCH
        + [pltpu.VMEM((NCOL, W_ROWS, HALF), jnp.bfloat16)],
        cost=cost(3, 2),
    )(lists, adj0, adj1, *received)


def backward_near(lists, adj0, adj1, back):
    return local(
        backward_near_kernel,
        (shape(NZ * QUAD, TILE, HALF),),
        4,
        "backward_near",
        any_in=1,
        scratch=[pltpu.VMEM((NZ * QUAD + 1, TILE, HALF), jnp.float32)] + LIST_SCRATCH,
        cost=cost(21, 6),
    )(lists, adj0, adj1, back)[0]


def dense(agg_own, agg_other, weight, cot_own, cot_other):
    return local(
        dense_kernel,
        (shape(TILE, 2 * HALF),) + (shape(2 * TILE + W_ROWS, HALF),) * 2,
        5,
        "dense",
    )(agg_own, agg_other, weight, cot_own, cot_other)


def ring_end(parts, *messages):
    return local(
        ring_end_kernel,
        (shape(2, TILE, HALF, dtype=jnp.float32), shape(2 * TILE + W_ROWS, HALF)),
        10,
        "ring_end",
        scratch=[pltpu.VMEM((NZ, W_ROWS, HALF), jnp.bfloat16)],
    )(parts, *messages)


def middle(*operands):
    return local(
        middle_kernel,
        (
            shape(TILE, HALF),
            shape(TILE + 4 * W_ROWS, HALF),
            shape(2, W_ROWS, HALF, dtype=jnp.float32),
        ),
        5,
        "middle",
    )(*operands)


def last(mine, from_core, w_here):
    return local(
        last_kernel,
        (shape(TILE, 2 * HALF), shape(2 * HALF, 2 * HALF, dtype=jnp.float32)),
        3,
        "last",
    )(mine, from_core, w_here)


def add(a, b):
    return (a.astype(jnp.float32) + b.astype(jnp.float32)).astype(jnp.bfloat16)


def per_device(features, adj_tiles, tile_row, tile_col, tile_count, weight, cotangent):
    adj0 = adj_tiles[0, 0]
    block = features[0]

    x_block = quad_permute(block, 2)
    keep, message, own_lists = prepare(tile_row[0, 0], tile_col[0, 0], tile_count, block)
    keep, message = join(keep, message, x_block)
    from_core = quad_permute(message, 1)
    core_keep = from_core[16:].reshape(2, TILE, HALF)
    chunk = jnp.stack([keep[0], core_keep[0], keep[1], core_keep[1]])
    partner_lists = from_core[0, :25].astype(jnp.int32)
    adj1 = quad_permute(adj0, 1)
    cot1 = quad_permute(cotangent, 1)

    up1, down1 = z_shift(chunk, 1), z_shift(chunk, -1)
    up2, down2 = z_shift(up1, 1), z_shift(down1, -1)
    up3, down3 = z_shift(up2, 1), z_shift(down2, -1)
    far_a, far_b = z_shift(up3[:2], 1), z_shift(down3[2:], -1)
    near, lists = forward_near(
        own_lists, partner_lists, adj0, adj1, [chunk, down1, down2, down3, up3, up2, up1]
    )
    shares = forward_far(lists, adj0, adj1, near, far_a, far_b)
    agg = sum(
        (col_move(share, k) if k else share).astype(jnp.float32)
        for k, share in zip(MOVES, shares)
    ).reshape(2 * TILE, HALF)
    agg_other = quad_permute(agg, 1)
    activated, send, send_x = dense(agg, agg_other, weight, cotangent, cot1)
    received = [col_move(send if k < 4 else send_x, k) if k else send for k in NEAR_MOVES]

    def forward(near, across, h):
        rows = [slice(h * TILE, (h + 1) * TILE)]
        rows += [slice(2 * TILE + h * W_ROWS // 2, 2 * TILE + (h + 1) * W_ROWS // 2)]
        message = jnp.concatenate([x[r] for x in (near, across) for r in rows])
        return col_move(message, 3 if h else 1)

    received += [forward(received[1], received[2], 0), forward(received[3], received[4], 1)]

    half, size = 2 * TILE, QUAD * TILE
    own, own_down, back = backward_far(lists, adj0, adj1, received)
    blocks = backward_near(lists, adj0, adj1, back)
    parts = blocks.reshape(NZ, size, HALF)
    up1, down1 = z_shift(own, 1), z_shift(own_down, -1)
    up = [add(parts[3, :half], up1[:half]), parts[3, half:], up1[half:]]
    down = [parts[5, :half], add(parts[5, half:], down1[:half]), down1[half:]]
    up2, down2 = z_shift(jnp.concatenate(up), 1), z_shift(jnp.concatenate(down), -1)
    up = [add(parts[2], up2[:size]), up2[size:]]
    down = [add(parts[6], down2[:size]), down2[size:]]
    up3, down3 = z_shift(jnp.concatenate(up), 1), z_shift(jnp.concatenate(down), -1)
    up4 = z_shift(jnp.concatenate([add(parts[1], up3[:size]), up3[size:]]), 1)
    down4 = z_shift(add(parts[7], down3[:size]), -1)

    kept, to_x = ring_end(blocks, own, up1, up2, up3, up4, down1, down2, down3, down4)
    w_send = to_x[half:]
    from_x = quad_permute(to_x, 2)
    w_lo = lax.ppermute(w_send, "col", [(c, c ^ 4) for c in range(NCOL)])
    both = [
        (r * NCOL + c, (r ^ 2) * NCOL + (c ^ 4)) for r in range(NZ * QUAD) for c in range(NCOL)
    ]
    w_both = lax.ppermute(w_send, ("row", "col"), both)
    mine, to_core, w_here = middle(kept, to_x, from_x, w_lo, w_both)
    grad, weight_grad = last(mine, quad_permute(to_core, 1), w_here)
    return (activated, weight_grad, grad[None])


def solution(mesh):
    return jax.shard_map(
        per_device,
        mesh=mesh,
        in_specs=(
            P("col", "row", None),
            P("row", "col", None, None, None),
            P("row", "col", None),
            P("row", "col", None),
            P("row", "col"),
            P(),
            P(("row", "col"), None),
        ),
        out_specs=(P(("row", "col"), None), P(), P("col", "row", None)),
        check_vma=False,
    )
```

```python
import functools
import math

import jax
import jax.numpy as jnp
from jax import lax
from jax.experimental import pallas as pl
from jax.experimental.pallas import tpu as pltpu
from jax.sharding import PartitionSpec as P

NZ = 8
QUAD = 4
NCOL = 8
TILE = 256
HALF = 128
SLOTS = 12
W_ROWS = 128
UNROLL = 4
PART = 16
LIST = 4 * PART + 4
NEAR_MOVES = (0, 1, 5, 3, 7, 4)
MOVES = (0, 6, 2, 5, 7, 1, 3, 4)


def row_pairs(move):
    pairs = []
    for r in range(NZ * QUAD):
        z, q = move(r // QUAD, r % QUAD)
        pairs.append((r, (z % NZ) * QUAD + q))
    return pairs


def quad_permute(x, flip):
    return lax.ppermute(x, "row", row_pairs(lambda z, q: (z, q ^ flip)))


def col_move(x, k):
    pairs = [(c, ((c >> 2) ^ (k >> 2)) * 4 + (c + k) % 4) for c in range(NCOL)]
    return lax.ppermute(x, "col", pairs)


def col_target(k, sign):
    c = lax.axis_index("col")
    return (((c >> 2) ^ (k >> 2)) << 2) + ((c + sign * (k & 3)) & 3)


def z_shift(x, step):
    return lax.ppermute(x, "row", row_pairs(lambda z, q: (z + step, q)))


def prepare_kernel(rows, cols, count, block, keep, message, own_lists):
    core = lax.axis_index("row") & 1

    @pl.when(core == 0)
    def _():
        keep[...] = block[:, :HALF]
        message[16:, :] = block[:, HALF:]

    @pl.when(core == 1)
    def _():
        keep[...] = block[:, HALF:]
        message[16:, :] = block[:, :HALF]

    lane = lax.broadcasted_iota(jnp.int32, (16, HALF), 1)
    values = jnp.zeros((16, HALF), jnp.float32)
    listed = [rows[s] for s in range(SLOTS)] + [cols[s] for s in range(SLOTS)] + [count[0, 0]]
    for n, value in enumerate(listed):
        values = jnp.where(lane == n, value.astype(jnp.float32), values)
        own_lists[n] = value
    message[:16, :] = values.astype(jnp.bfloat16)


def join_kernel(own_keep, own_message, x_block, keep, message):
    core = lax.axis_index("row") & 1
    keep[0] = own_keep[...]
    message[: TILE + 16, :] = own_message[...]

    @pl.when(core == 0)
    def _():
        keep[1] = x_block[:, :HALF]
        message[TILE + 16 :, :] = x_block[:, HALF:]

    @pl.when(core == 1)
    def _():
        keep[1] = x_block[:, HALF:]
        message[TILE + 16 :, :] = x_block[:, :HALF]


def list_slots(own, partner, lists):
    device = lax.axis_index("row")
    z, q = device >> 2, device & 3
    for i, slots in enumerate((own, partner)):
        near, far = jnp.int32(0), jnp.int32(0)
        for s in range(SLOTS):
            tile = slots[12 + s]
            place = (((tile >> 2) - z) & 7) * QUAD + ((tile & 3) ^ q)
            live = (s < slots[24]).astype(jnp.int32)
            is_far = ((place >> 2) == 4).astype(jnp.int32)
            lists[i * PART + is_far * (2 * PART + far - near) + near] = (
                s * 1024 + slots[s] * 64 + place
            )
            far = far + live * is_far
            near = near + live * (1 - is_far)
        for u in range(UNROLL - 1):
            lists[i * PART + near + u] = 8 * 64 + 32
        lists[4 * PART + i] = near
        lists[4 * PART + 2 + i] = far


def slot_products(lists, far, adj_refs, product, add_to):
    unroll = 1 if far else UNROLL
    for i, adj in enumerate(adj_refs):
        part = 2 * far + i

        @pl.loop(0, (lists[4 * PART + part] + unroll - 1) // unroll)
        def _(step, i=i, adj=adj, part=part):
            codes = [lists[part * PART + step * unroll + u] for u in range(unroll)]
            places = [((code >> 6) & 15, i, code & 63) for code in codes]
            values = [product(adj[code >> 10], *at) for code, at in zip(codes, places)]
            for value, at in zip(values, places):
                add_to(value, *at)


def forward_near_kernel(own_any, partner_any, adj0, adj1, *refs):
    pieces, (acc, lists, panel, own, partner, sems) = refs[:7], refs[7:]
    copies = [
        pltpu.make_async_copy(own_any, own, sems.at[0]),
        pltpu.make_async_copy(partner_any, partner, sems.at[1]),
    ]
    for copy in copies:
        copy.start()
    for place, piece in zip((0, 1, 2, 3, 5, 6, 7), pieces):
        panel[place * QUAD : (place + 1) * QUAD] = piece[...]
    acc[...] = jnp.zeros_like(acc)
    for copy in copies:
        copy.wait()
    list_slots(own, partner, lists)

    def product(tile, row, i, place):
        return jnp.dot(tile, panel[place & 31], preferred_element_type=jnp.float32)

    def add_to(value, row, i, place):
        acc[2 * row + i] += value

    slot_products(lists, False, (adj0, adj1), product, add_to)


def forward_far_kernel(lists_any, adj0, adj1, near, far_a, far_b, *refs):
    outs, (acc, far, lists, sem) = refs[:NCOL], refs[NCOL:]
    copy = pltpu.make_async_copy(lists_any, lists, sem)
    copy.start()
    far[:2] = far_a[...]
    far[2:] = far_b[...]
    acc[...] = near[...]
    copy.wait()

    def product(tile, row, i, place):
        return jnp.dot(tile, far[place & 3], preferred_element_type=jnp.float32)

    def add_to(value, row, i, place):
        acc[2 * row + i] += value

    slot_products(lists, True, (adj0, adj1), product, add_to)
    for k, out in zip(MOVES, outs):
        row = col_target(k, 1)
        for i in range(2):
            out[i] = acc[2 * row + i].astype(jnp.bfloat16)


def backward_products(lists, adj_refs, back, acc, far):
    def product(tile, row, i, place):
        return lax.dot_general(
            tile,
            back[row & 7, pl.ds(i * TILE, TILE), :],
            (((0,), (0,)), ((), ())),
            preferred_element_type=jnp.float32,
        )

    def add_to(value, row, i, place):
        acc[place & 3 if far else place] += value

    slot_products(lists, far, adj_refs, product, add_to)


def backward_far_kernel(lists_any, in_step_any, adj0, adj1, *refs):
    del in_step_any
    received, (up, down, back, acc, lists, sem, pieces) = refs[:NCOL], refs[NCOL:]
    copy = pltpu.make_async_copy(lists_any, lists, sem)
    copy.start()
    for k, ref in zip(NEAR_MOVES, received):
        source = col_target(k, -1)
        back[source] = ref[: 2 * TILE, :]
        pieces[source] = ref[2 * TILE :, :]
    for h, ref in enumerate(received[len(NEAR_MOVES) :]):
        for j, k in enumerate((2, 6)):
            source = col_target(k, -1)
            start = j * (TILE + W_ROWS // 2)
            back[source, h * TILE : (h + 1) * TILE, :] = ref[start : start + TILE, :]
            pieces[source, h * W_ROWS // 2 : (h + 1) * W_ROWS // 2, :] = ref[
                start + TILE : start + TILE + W_ROWS // 2, :
            ]
    acc[...] = jnp.zeros_like(acc)
    piece = pieces[0].astype(jnp.float32)
    for c in range(1, NCOL):
        piece = piece + pieces[c].astype(jnp.float32)
    for out in (up, down):
        out[2 * TILE :, :] = piece.astype(jnp.bfloat16)
    copy.wait()
    backward_products(lists, (adj0, adj1), back, acc, True)
    for k in range(QUAD):
        part = pl.ds((k & 1) * TILE, TILE)
        (up, down)[k >> 1][part, :] = acc[k].astype(jnp.bfloat16)


def backward_near_kernel(lists_any, adj0, adj1, back, out, acc, lists, sem):
    copy = pltpu.make_async_copy(lists_any, lists, sem)
    copy.start()
    acc[...] = jnp.zeros_like(acc)
    copy.wait()
    backward_products(lists, (adj0, adj1), back, acc, False)
    out[...] = acc[: NZ * QUAD].astype(jnp.bfloat16)


def split(x):
    high = x.astype(jnp.bfloat16)
    return high, (x - high.astype(jnp.float32)).astype(jnp.bfloat16)


def dense_kernel(agg_own, agg_other, weight, cot_own, cot_other, act_out, send, send_x):
    first = (lax.axis_index("row") & 1) == 0
    own = agg_own[...]
    other = jnp.concatenate([agg_other[TILE:, :], agg_other[:TILE, :]], axis=0)
    w = weight[...]
    w_other_half = jnp.where(first, w[HALF:], w[:HALF])
    w_half = jnp.where(first, w[:HALF], w[HALF:])

    def dot(a, b, dims=((1,), (0,))):
        return lax.dot_general(a, b, (dims, ((), ())), preferred_element_type=jnp.float32)

    own_hi, own_lo = split(own)
    other_hi, other_lo = split(other)
    v = (dot(own_hi, w_half) + dot(own_lo, w_half)) + (
        dot(other_hi, w_other_half) + dot(other_lo, w_other_half)
    )
    scale = math.sqrt(2.0 / math.pi)
    square = v * v
    t = jnp.tanh(scale * (v + 0.044715 * (square * v)))
    cdf = 0.5 * (1.0 + t)
    act_out[...] = (v[:TILE] * cdf[:TILE]).astype(jnp.bfloat16)
    slope = cdf + 0.5 * v * ((1.0 - t) * (1.0 + t)) * (scale * (1.0 + 3.0 * 0.044715 * square))
    cot = jnp.concatenate([cot_own[...], cot_other[...]], axis=0).astype(jnp.float32)
    grad_hi, grad_lo = split(cot * slope)
    nodes = ((1,), (1,))
    back = (dot(grad_hi, w_half, nodes) + dot(grad_lo, w_half, nodes)).astype(jnp.bfloat16)
    rows = ((0,), (0,))
    w_part = (
        dot(own_hi, grad_hi, rows) + dot(own_lo, grad_hi, rows) + dot(own_hi, grad_lo, rows)
    )
    x_lo = lax.axis_index("col") >> 2
    for out, dest in ((send, x_lo), (send_x, 1 - x_lo)):
        out[: 2 * TILE, :] = back
        piece = jnp.where(dest == 0, w_part[:64], w_part[64:]).astype(jnp.bfloat16)
        out[2 * TILE : 2 * TILE + 64, :] = piece[:, :HALF]
        out[2 * TILE + 64 :, :] = piece[:, HALF:]


def f32(ref, start, rows=TILE):
    return ref[start : start + rows, :].astype(jnp.float32)


def ring_end_kernel(
    parts, own, up1, up2, up3, up4, down1, down2, down3, down4, kept, message, by_step
):
    z = lax.axis_index("row") >> 2
    half, size = 2 * TILE, QUAD * TILE
    pieces = (
        (own, half),
        (down1, half),
        (down2, size),
        (down3, size),
        (up4, size),
        (up3, size),
        (up2, size),
        (up1, half),
    )
    for k, (ref, start) in enumerate(pieces):
        by_step[(k + z) & 7] = ref[start:, :]
    w_sum = by_step[0].astype(jnp.float32)
    for a in range(1, NZ):
        w_sum = w_sum + by_step[a].astype(jnp.float32)
    message[half:, :] = w_sum.astype(jnp.bfloat16)
    for k in range(QUAD):
        start = k * TILE
        total = parts[k].astype(jnp.float32) + f32(up4, start) + f32(down4, start)
        if k < 2:
            kept[k] = total
        else:
            message[start - half : start - half + TILE, :] = total.astype(jnp.bfloat16)


def middle_kernel(kept, sent, from_x, w_lo, w_both, mine, message, w_here):
    x_lo = lax.axis_index("col") >> 2
    half = 2 * TILE
    for k, ref in enumerate((mine, message)):
        ref[:TILE, :] = (kept[k] + f32(from_x, k * TILE)).astype(jnp.bfloat16)
    sums = (
        f32(sent, half, W_ROWS) + f32(from_x, half, W_ROWS),
        w_lo[...].astype(jnp.float32) + w_both[...].astype(jnp.float32),
    )
    for value, place in zip(sums, (x_lo, 1 - x_lo)):
        high, low = split(value)
        w_here[place] = high.astype(jnp.float32) + low.astype(jnp.float32)
        start = pl.multiple_of(TILE + place * 2 * W_ROWS, W_ROWS)
        message[pl.ds(start, W_ROWS), :] = high
        message[pl.ds(start + W_ROWS, W_ROWS), :] = low


def last_kernel(mine, from_core, w_here, grad_out, w_out):
    core = lax.axis_index("row") & 1
    scale = 1.0 / 256.0

    def place(value, start):
        rows = pl.ds(pl.multiple_of(start, 64), 64)
        w_out[rows, :HALF] = value[:64, :] * scale
        w_out[rows, HALF:] = value[64:, :] * scale

    for x_lo in range(2):
        start = TILE + x_lo * 2 * W_ROWS
        place(w_here[x_lo], core * HALF + x_lo * 64)
        w_core = f32(from_core, start, W_ROWS) + f32(from_core, start + W_ROWS, W_ROWS)
        place(w_core, (1 - core) * HALF + x_lo * 64)

    @pl.when(core == 0)
    def _():
        grad_out[:, :HALF] = mine[...]
        grad_out[:, HALF:] = from_core[:TILE, :]

    @pl.when(core == 1)
    def _():
        grad_out[:, HALF:] = mine[...]
        grad_out[:, :HALF] = from_core[:TILE, :]


SMEM = pl.BlockSpec(memory_space=pltpu.SMEM)
VMEM = pl.BlockSpec(memory_space=pltpu.VMEM)
ANY = pl.BlockSpec(memory_space=pl.ANY)


def params(mib):
    return pltpu.CompilerParams(vmem_limit_bytes=mib << 20)


LIST_SCRATCH = [pltpu.SMEM((LIST,), jnp.int32), pltpu.SemaphoreType.DMA]


def cost(slots, size):
    return pl.CostEstimate(
        flops=slots * 2 * TILE * TILE * HALF, bytes_accessed=size << 20, transcendentals=0
    )


LISTS = [SMEM] * 4


def shape(*dims, dtype=jnp.bfloat16):
    return jax.ShapeDtypeStruct(dims, dtype)


def local(kernel, outs, n_in, name, scalars=0, any_in=0, scratch=(), cost=None, scalar_out=0):
    return pl.pallas_call(
        kernel,
        out_shape=outs,
        in_specs=[SMEM] * scalars + [ANY] * any_in + [VMEM] * (n_in - scalars - any_in),
        out_specs=(VMEM,) * (len(outs) - scalar_out) + (SMEM,) * scalar_out,
        scratch_shapes=scratch,
        compiler_params=params(20),
        cost_estimate=cost,
        name=name,
    )


def prepare(rows, cols, count, block):
    return local(
        prepare_kernel,
        (shape(TILE, HALF), shape(TILE + 16, HALF), shape(25, dtype=jnp.int32)),
        4,
        "prepare",
        scalars=3,
        scalar_out=1,
    )(rows, cols, count, block)


def join(own_keep, own_message, x_block):
    return local(
        join_kernel, (shape(2, TILE, HALF), shape(2 * TILE + 16, HALF)), 3, "join"
    )(own_keep, own_message, x_block)


def forward_near(own, partner, adj0, adj1, pieces):
    return local(
        forward_near_kernel,
        (shape(18, TILE, HALF, dtype=jnp.float32), shape(LIST, dtype=jnp.int32)),
        11,
        "forward_near",
        any_in=2,
        scalar_out=1,
        scratch=[
            pltpu.VMEM((NZ * QUAD, TILE, HALF), jnp.bfloat16),
            pltpu.SMEM((25,), jnp.int32),
            pltpu.SMEM((25,), jnp.int32),
            pltpu.SemaphoreType.DMA((2,)),
        ],
        cost=cost(21, 6),
    )(own, partner, adj0, adj1, *pieces)


def forward_far(lists, adj0, adj1, near, far_a, far_b):
    return local(
        forward_far_kernel,
        (shape(2, TILE, HALF),) * NCOL,
        6,
        "forward_far",
        any_in=1,
        scratch=[
            pltpu.VMEM((18, TILE, HALF), jnp.float32),
            pltpu.VMEM((QUAD, TILE, HALF), jnp.bfloat16),
        ]
        + LIST_SCRATCH,
        cost=cost(3, 4),
    )(lists, adj0, adj1, near, far_a, far_b)


def backward_far(lists, in_step, adj0, adj1, received):
    message = shape(2 * TILE + W_ROWS, HALF)
    return local(
        backward_far_kernel,
        (message, message, shape(NCOL, 2 * TILE, HALF)),
        12,
        "backward_far",
        any_in=2,
        scratch=[pltpu.VMEM((QUAD, TILE, HALF), jnp.float32)]
        + LIST_SCRATCH
        + [pltpu.VMEM((NCOL, W_ROWS, HALF), jnp.bfloat16)],
        cost=cost(3, 2),
    )(lists, in_step, adj0, adj1, *received)


def backward_near(lists, adj0, adj1, back):
    return local(
        backward_near_kernel,
        (shape(NZ * QUAD, TILE, HALF),),
        4,
        "backward_near",
        any_in=1,
        scratch=[pltpu.VMEM((NZ * QUAD + 1, TILE, HALF), jnp.float32)] + LIST_SCRATCH,
        cost=cost(21, 6),
    )(lists, adj0, adj1, back)[0]


def dense(agg_own, agg_other, weight, cot_own, cot_other):
    return local(
        dense_kernel,
        (shape(TILE, 2 * HALF),) + (shape(2 * TILE + W_ROWS, HALF),) * 2,
        5,
        "dense",
    )(agg_own, agg_other, weight, cot_own, cot_other)


def ring_end(parts, *messages):
    return local(
        ring_end_kernel,
        (shape(2, TILE, HALF, dtype=jnp.float32), shape(2 * TILE + W_ROWS, HALF)),
        10,
        "ring_end",
        scratch=[pltpu.VMEM((NZ, W_ROWS, HALF), jnp.bfloat16)],
    )(parts, *messages)


def middle(*operands):
    return local(
        middle_kernel,
        (
            shape(TILE, HALF),
            shape(TILE + 4 * W_ROWS, HALF),
            shape(2, W_ROWS, HALF, dtype=jnp.float32),
        ),
        5,
        "middle",
    )(*operands)


def last(mine, from_core, w_here):
    return local(
        last_kernel,
        (shape(TILE, 2 * HALF), shape(2 * HALF, 2 * HALF, dtype=jnp.float32)),
        3,
        "last",
    )(mine, from_core, w_here)


def add(a, b):
    return (a.astype(jnp.float32) + b.astype(jnp.float32)).astype(jnp.bfloat16)


def per_device(features, adj_tiles, tile_row, tile_col, tile_count, weight, cotangent):
    adj0 = adj_tiles[0, 0]
    block = features[0]

    x_block = quad_permute(block, 2)
    keep, message, own_lists = prepare(tile_row[0, 0], tile_col[0, 0], tile_count, block)
    keep, message = join(keep, message, x_block)
    from_core = quad_permute(message, 1)
    core_keep = from_core[16:].reshape(2, TILE, HALF)
    chunk = jnp.stack([keep[0], core_keep[0], keep[1], core_keep[1]])
    partner_lists = from_core[0, :25].astype(jnp.int32)
    adj1 = quad_permute(adj0, 1)
    cot1 = quad_permute(cotangent, 1)

    up1, down1 = z_shift(chunk, 1), z_shift(chunk, -1)
    up2, down2 = z_shift(up1, 1), z_shift(down1, -1)
    up3, down3 = z_shift(up2, 1), z_shift(down2, -1)
    far_a, far_b = z_shift(up3[:2], 1), z_shift(down3[2:], -1)
    near, lists = forward_near(
        own_lists, partner_lists, adj0, adj1, [chunk, down1, down2, down3, up3, up2, up1]
    )
    shares = forward_far(lists, adj0, adj1, near, far_a, far_b)
    agg = sum(
        (col_move(share, k) if k else share).astype(jnp.float32)
        for k, share in zip(MOVES, shares)
    ).reshape(2 * TILE, HALF)
    agg_other = quad_permute(agg, 1)
    activated, send, send_x = dense(agg, agg_other, weight, cotangent, cot1)
    received = [col_move(send if k < 4 else send_x, k) if k else send for k in NEAR_MOVES]

    def forward(near, across, h):
        rows = [slice(h * TILE, (h + 1) * TILE)]
        rows += [slice(2 * TILE + h * W_ROWS // 2, 2 * TILE + (h + 1) * W_ROWS // 2)]
        message = jnp.concatenate([x[r] for x in (near, across) for r in rows])
        return col_move(message, 3 if h else 1)

    received += [forward(received[1], received[2], 0), forward(received[3], received[4], 1)]

    half, size = 2 * TILE, QUAD * TILE
    in_step = quad_permute(received[4][:16], 1)
    own, own_down, back = backward_far(lists, in_step, adj0, adj1, received)
    blocks = backward_near(lists, adj0, adj1, back)
    parts = blocks.reshape(NZ, size, HALF)
    up1, down1 = z_shift(own, 1), z_shift(own_down, -1)
    up = [add(parts[3, :half], up1[:half]), parts[3, half:], up1[half:]]
    down = [parts[5, :half], add(parts[5, half:], down1[:half]), down1[half:]]
    up2, down2 = z_shift(jnp.concatenate(up), 1), z_shift(jnp.concatenate(down), -1)
    up = [add(parts[2], up2[:size]), up2[size:]]
    down = [add(parts[6], down2[:size]), down2[size:]]
    up3, down3 = z_shift(jnp.concatenate(up), 1), z_shift(jnp.concatenate(down), -1)
    up4 = z_shift(jnp.concatenate([add(parts[1], up3[:size]), up3[size:]]), 1)
    down4 = z_shift(add(parts[7], down3[:size]), -1)

    kept, to_x = ring_end(blocks, own, up1, up2, up3, up4, down1, down2, down3, down4)
    w_send = to_x[half:]
    from_x = quad_permute(to_x, 2)
    w_lo = lax.ppermute(w_send, "col", [(c, c ^ 4) for c in range(NCOL)])
    both = [
        (r * NCOL + c, (r ^ 2) * NCOL + (c ^ 4)) for r in range(NZ * QUAD) for c in range(NCOL)
    ]
    w_both = lax.ppermute(w_send, ("row", "col"), both)
    mine, to_core, w_here = middle(kept, to_x, from_x, w_lo, w_both)
    grad, weight_grad = last(mine, quad_permute(to_core, 1), w_here)
    return (activated, weight_grad, grad[None])


def solution(mesh):
    return jax.shard_map(
        per_device,
        mesh=mesh,
        in_specs=(
            P("col", "row", None),
            P("row", "col", None, None, None),
            P("row", "col", None),
            P("row", "col", None),
            P("row", "col"),
            P(),
            P(("row", "col"), None),
        ),
        out_specs=(P(("row", "col"), None), P(), P("col", "row", None)),
        check_vma=False,
    )
```

```python
import functools
import math

import jax
import jax.numpy as jnp
from jax import lax
from jax.experimental import pallas as pl
from jax.experimental.pallas import tpu as pltpu
from jax.sharding import PartitionSpec as P

NZ = 8
QUAD = 4
NCOL = 8
TILE = 256
HALF = 128
SLOTS = 12
W_ROWS = 128
UNROLL = 4
PART = 16
LIST = 4 * PART + 4
MOVES = (0, 6, 2, 5, 7, 1, 3, 4)


def row_pairs(move):
    pairs = []
    for r in range(NZ * QUAD):
        z, q = move(r // QUAD, r % QUAD)
        pairs.append((r, (z % NZ) * QUAD + q))
    return pairs


def quad_permute(x, flip):
    return lax.ppermute(x, "row", row_pairs(lambda z, q: (z, q ^ flip)))


def col_move(x, k):
    pairs = [(c, ((c >> 2) ^ (k >> 2)) * 4 + (c + k) % 4) for c in range(NCOL)]
    return lax.ppermute(x, "col", pairs)


def col_target(k, sign):
    c = lax.axis_index("col")
    return (((c >> 2) ^ (k >> 2)) << 2) + ((c + sign * (k & 3)) & 3)


def z_shift(x, step):
    return lax.ppermute(
        x, "row", row_pairs(lambda z, q: (z + step * (1 - 2 * (q & 1)), q))
    )


def z_ahead(z, core, steps):
    return (z + steps * (1 - 2 * core)) & 7


def prepare_kernel(rows, cols, count, block, keep, message, own_lists):
    core = lax.axis_index("row") & 1

    @pl.when(core == 0)
    def _():
        keep[...] = block[:, :HALF]
        message[16:, :] = block[:, HALF:]

    @pl.when(core == 1)
    def _():
        keep[...] = block[:, HALF:]
        message[16:, :] = block[:, :HALF]

    lane = lax.broadcasted_iota(jnp.int32, (16, HALF), 1)
    values = jnp.zeros((16, HALF), jnp.float32)
    listed = [rows[s] for s in range(SLOTS)] + [cols[s] for s in range(SLOTS)] + [count[0, 0]]
    for n, value in enumerate(listed):
        values = jnp.where(lane == n, value.astype(jnp.float32), values)
        own_lists[n] = value
    message[:16, :] = values.astype(jnp.bfloat16)


def join_kernel(own_keep, own_message, x_block, keep, message):
    core = lax.axis_index("row") & 1
    keep[0] = own_keep[...]
    message[: TILE + 16, :] = own_message[...]

    @pl.when(core == 0)
    def _():
        keep[1] = x_block[:, :HALF]
        message[TILE + 16 :, :] = x_block[:, HALF:]

    @pl.when(core == 1)
    def _():
        keep[1] = x_block[:, HALF:]
        message[TILE + 16 :, :] = x_block[:, :HALF]


def list_slots(own, partner, lists):
    device = lax.axis_index("row")
    z, q = device >> 2, device & 3
    for i, slots in enumerate((own, partner)):
        near, far = jnp.int32(0), jnp.int32(0)
        for s in range(SLOTS):
            tile = slots[12 + s]
            place = z_ahead(0, q & 1, (tile >> 2) - z) * QUAD + ((tile & 3) ^ q)
            live = (s < slots[24]).astype(jnp.int32)
            is_far = ((place >> 2) == 4).astype(jnp.int32)
            lists[i * PART + is_far * (2 * PART + far - near) + near] = (
                s * 1024 + slots[s] * 64 + place
            )
            far = far + live * is_far
            near = near + live * (1 - is_far)
        for u in range(UNROLL - 1):
            lists[i * PART + near + u] = 8 * 64 + 32
        lists[4 * PART + i] = near
        lists[4 * PART + 2 + i] = far


def slot_products(lists, far, adj_refs, product, add_to):
    unroll = 1 if far else UNROLL
    for i, adj in enumerate(adj_refs):
        part = 2 * far + i

        @pl.loop(0, (lists[4 * PART + part] + unroll - 1) // unroll)
        def _(step, i=i, adj=adj, part=part):
            codes = [lists[part * PART + step * unroll + u] for u in range(unroll)]
            places = [((code >> 6) & 15, i, code & 63) for code in codes]
            values = [product(adj[code >> 10], *at) for code, at in zip(codes, places)]
            for value, at in zip(values, places):
                add_to(value, *at)


def forward_near_kernel(own_any, partner_any, adj0, adj1, *refs):
    pieces, (acc, lists, panel, own, partner, sems) = refs[:7], refs[7:]
    copies = [
        pltpu.make_async_copy(own_any, own, sems.at[0]),
        pltpu.make_async_copy(partner_any, partner, sems.at[1]),
    ]
    for copy in copies:
        copy.start()
    for place, piece in zip((0, 1, 2, 3, 5, 6, 7), pieces):
        panel[place * QUAD : (place + 1) * QUAD] = piece[...]
    acc[...] = jnp.zeros_like(acc)
    for copy in copies:
        copy.wait()
    list_slots(own, partner, lists)

    def product(tile, row, i, place):
        return jnp.dot(tile, panel[place & 31], preferred_element_type=jnp.float32)

    def add_to(value, row, i, place):
        acc[2 * row + i] += value

    slot_products(lists, False, (adj0, adj1), product, add_to)


def forward_far_kernel(lists_any, adj0, adj1, near, far_a, far_b, *refs):
    outs, (acc, far, lists, sem) = refs[:NCOL], refs[NCOL:]
    copy = pltpu.make_async_copy(lists_any, lists, sem)
    copy.start()
    far[:2] = far_a[...]
    far[2:] = far_b[...]
    acc[...] = near[...]
    copy.wait()

    def product(tile, row, i, place):
        return jnp.dot(tile, far[place & 3], preferred_element_type=jnp.float32)

    def add_to(value, row, i, place):
        acc[2 * row + i] += value

    slot_products(lists, True, (adj0, adj1), product, add_to)
    for k, out in zip(MOVES, outs):
        row = col_target(k, 1)
        for i in range(2):
            out[i] = acc[2 * row + i].astype(jnp.bfloat16)


def backward_products(lists, adj_refs, back, acc, far):
    def product(tile, row, i, place):
        return lax.dot_general(
            tile,
            back[row & 7, pl.ds(i * TILE, TILE), :],
            (((0,), (0,)), ((), ())),
            preferred_element_type=jnp.float32,
        )

    def add_to(value, row, i, place):
        acc[place & 3 if far else place] += value

    slot_products(lists, far, adj_refs, product, add_to)


def backward_far_kernel(lists_any, adj0, adj1, *refs):
    received, (up, down, back, acc, lists, sem, pieces) = refs[:NCOL], refs[NCOL:]
    copy = pltpu.make_async_copy(lists_any, lists, sem)
    copy.start()
    for k, ref in zip(MOVES, received):
        source = col_target(k, -1)
        back[source] = ref[: 2 * TILE, :]
        pieces[source] = ref[2 * TILE :, :]
    acc[...] = jnp.zeros_like(acc)
    piece = pieces[0].astype(jnp.float32)
    for c in range(1, NCOL):
        piece = piece + pieces[c].astype(jnp.float32)
    for out in (up, down):
        out[2 * TILE :, :] = piece.astype(jnp.bfloat16)
    copy.wait()
    backward_products(lists, (adj0, adj1), back, acc, True)
    for k in range(QUAD):
        part = pl.ds((k & 1) * TILE, TILE)
        (up, down)[k >> 1][part, :] = acc[k].astype(jnp.bfloat16)


def backward_near_kernel(lists_any, adj0, adj1, back, out, acc, lists, sem):
    copy = pltpu.make_async_copy(lists_any, lists, sem)
    copy.start()
    acc[...] = jnp.zeros_like(acc)
    copy.wait()
    backward_products(lists, (adj0, adj1), back, acc, False)
    out[...] = acc[: NZ * QUAD].astype(jnp.bfloat16)


def split(x):
    high = x.astype(jnp.bfloat16)
    return high, (x - high.astype(jnp.float32)).astype(jnp.bfloat16)


def dense_kernel(agg_own, agg_other, weight, cot_own, cot_other, act_out, send, send_x):
    first = (lax.axis_index("row") & 1) == 0
    own = agg_own[...]
    other = jnp.concatenate([agg_other[TILE:, :], agg_other[:TILE, :]], axis=0)
    w = weight[...]
    w_other_half = jnp.where(first, w[HALF:], w[:HALF])
    w_half = jnp.where(first, w[:HALF], w[HALF:])

    def dot(a, b, dims=((1,), (0,))):
        return lax.dot_general(a, b, (dims, ((), ())), preferred_element_type=jnp.float32)

    own_hi, own_lo = split(own)
    other_hi, other_lo = split(other)
    v = (dot(own_hi, w_half) + dot(own_lo, w_half)) + (
        dot(other_hi, w_other_half) + dot(other_lo, w_other_half)
    )
    scale = math.sqrt(2.0 / math.pi)
    square = v * v
    t = jnp.tanh(scale * (v + 0.044715 * (square * v)))
    cdf = 0.5 * (1.0 + t)
    act_out[...] = (v[:TILE] * cdf[:TILE]).astype(jnp.bfloat16)
    slope = cdf + 0.5 * v * ((1.0 - t) * (1.0 + t)) * (scale * (1.0 + 3.0 * 0.044715 * square))
    cot = jnp.concatenate([cot_own[...], cot_other[...]], axis=0).astype(jnp.float32)
    grad_hi, grad_lo = split(cot * slope)
    nodes = ((1,), (1,))
    back = (dot(grad_hi, w_half, nodes) + dot(grad_lo, w_half, nodes)).astype(jnp.bfloat16)
    rows = ((0,), (0,))
    w_part = (
        dot(own_hi, grad_hi, rows) + dot(own_lo, grad_hi, rows) + dot(own_hi, grad_lo, rows)
    )
    x_lo = lax.axis_index("col") >> 2
    for out, dest in ((send, x_lo), (send_x, 1 - x_lo)):
        out[: 2 * TILE, :] = back
        piece = jnp.where(dest == 0, w_part[:64], w_part[64:]).astype(jnp.bfloat16)
        out[2 * TILE : 2 * TILE + 64, :] = piece[:, :HALF]
        out[2 * TILE + 64 :, :] = piece[:, HALF:]


def f32(ref, start, rows=TILE):
    return ref[start : start + rows, :].astype(jnp.float32)


def ring_end_kernel(
    parts, own, up1, up2, up3, up4, down1, down2, down3, down4, kept, message, by_step
):
    device = lax.axis_index("row")
    z, core = device >> 2, device & 1
    half, size = 2 * TILE, QUAD * TILE
    pieces = (
        (own, half),
        (down1, half),
        (down2, size),
        (down3, size),
        (up4, size),
        (up3, size),
        (up2, size),
        (up1, half),
    )
    for k, (ref, start) in enumerate(pieces):
        by_step[z_ahead(z, core, k)] = ref[start:, :]
    w_sum = by_step[0].astype(jnp.float32)
    for a in range(1, NZ):
        w_sum = w_sum + by_step[a].astype(jnp.float32)
    message[half:, :] = w_sum.astype(jnp.bfloat16)
    for k in range(QUAD):
        start = k * TILE
        total = parts[k].astype(jnp.float32) + f32(up4, start) + f32(down4, start)
        if k < 2:
            kept[k] = total
        else:
            message[start - half : start - half + TILE, :] = total.astype(jnp.bfloat16)


def middle_kernel(kept, sent, from_x, w_lo, w_both, mine, message, w_here):
    x_lo = lax.axis_index("col") >> 2
    half = 2 * TILE
    for k, ref in enumerate((mine, message)):
        ref[:TILE, :] = (kept[k] + f32(from_x, k * TILE)).astype(jnp.bfloat16)
    sums = (
        f32(sent, half, W_ROWS) + f32(from_x, half, W_ROWS),
        w_lo[...].astype(jnp.float32) + w_both[...].astype(jnp.float32),
    )
    for value, place in zip(sums, (x_lo, 1 - x_lo)):
        high, low = split(value)
        w_here[place] = high.astype(jnp.float32) + low.astype(jnp.float32)
        start = pl.multiple_of(TILE + place * 2 * W_ROWS, W_ROWS)
        message[pl.ds(start, W_ROWS), :] = high
        message[pl.ds(start + W_ROWS, W_ROWS), :] = low


def last_kernel(mine, from_core, w_here, grad_out, w_out):
    core = lax.axis_index("row") & 1
    scale = 1.0 / 256.0

    def place(value, start):
        rows = pl.ds(pl.multiple_of(start, 64), 64)
        w_out[rows, :HALF] = value[:64, :] * scale
        w_out[rows, HALF:] = value[64:, :] * scale

    for x_lo in range(2):
        start = TILE + x_lo * 2 * W_ROWS
        place(w_here[x_lo], core * HALF + x_lo * 64)
        w_core = f32(from_core, start, W_ROWS) + f32(from_core, start + W_ROWS, W_ROWS)
        place(w_core, (1 - core) * HALF + x_lo * 64)

    @pl.when(core == 0)
    def _():
        grad_out[:, :HALF] = mine[...]
        grad_out[:, HALF:] = from_core[:TILE, :]

    @pl.when(core == 1)
    def _():
        grad_out[:, HALF:] = mine[...]
        grad_out[:, :HALF] = from_core[:TILE, :]


SMEM = pl.BlockSpec(memory_space=pltpu.SMEM)
VMEM = pl.BlockSpec(memory_space=pltpu.VMEM)
ANY = pl.BlockSpec(memory_space=pl.ANY)


def params(mib):
    return pltpu.CompilerParams(vmem_limit_bytes=mib << 20)


LIST_SCRATCH = [pltpu.SMEM((LIST,), jnp.int32), pltpu.SemaphoreType.DMA]


def cost(slots, size):
    return pl.CostEstimate(
        flops=slots * 2 * TILE * TILE * HALF, bytes_accessed=size << 20, transcendentals=0
    )


LISTS = [SMEM] * 4


def shape(*dims, dtype=jnp.bfloat16):
    return jax.ShapeDtypeStruct(dims, dtype)


def local(kernel, outs, n_in, name, scalars=0, any_in=0, scratch=(), cost=None, scalar_out=0):
    return pl.pallas_call(
        kernel,
        out_shape=outs,
        in_specs=[SMEM] * scalars + [ANY] * any_in + [VMEM] * (n_in - scalars - any_in),
        out_specs=(VMEM,) * (len(outs) - scalar_out) + (SMEM,) * scalar_out,
        scratch_shapes=scratch,
        compiler_params=params(20),
        cost_estimate=cost,
        name=name,
    )


def prepare(rows, cols, count, block):
    return local(
        prepare_kernel,
        (shape(TILE, HALF), shape(TILE + 16, HALF), shape(25, dtype=jnp.int32)),
        4,
        "prepare",
        scalars=3,
        scalar_out=1,
    )(rows, cols, count, block)


def join(own_keep, own_message, x_block):
    return local(
        join_kernel, (shape(2, TILE, HALF), shape(2 * TILE + 16, HALF)), 3, "join"
    )(own_keep, own_message, x_block)


def forward_near(own, partner, adj0, adj1, pieces):
    return local(
        forward_near_kernel,
        (shape(18, TILE, HALF, dtype=jnp.float32), shape(LIST, dtype=jnp.int32)),
        11,
        "forward_near",
        any_in=2,
        scalar_out=1,
        scratch=[
            pltpu.VMEM((NZ * QUAD, TILE, HALF), jnp.bfloat16),
            pltpu.SMEM((25,), jnp.int32),
            pltpu.SMEM((25,), jnp.int32),
            pltpu.SemaphoreType.DMA((2,)),
        ],
        cost=cost(21, 6),
    )(own, partner, adj0, adj1, *pieces)


def forward_far(lists, adj0, adj1, near, far_a, far_b):
    return local(
        forward_far_kernel,
        (shape(2, TILE, HALF),) * NCOL,
        6,
        "forward_far",
        any_in=1,
        scratch=[
            pltpu.VMEM((18, TILE, HALF), jnp.float32),
            pltpu.VMEM((QUAD, TILE, HALF), jnp.bfloat16),
        ]
        + LIST_SCRATCH,
        cost=cost(3, 4),
    )(lists, adj0, adj1, near, far_a, far_b)


def backward_far(lists, adj0, adj1, received):
    message = shape(2 * TILE + W_ROWS, HALF)
    return local(
        backward_far_kernel,
        (message, message, shape(NCOL, 2 * TILE, HALF)),
        11,
        "backward_far",
        any_in=1,
        scratch=[pltpu.VMEM((QUAD, TILE, HALF), jnp.float32)]
        + LIST_SCRATCH
        + [pltpu.VMEM((NCOL, W_ROWS, HALF), jnp.bfloat16)],
        cost=cost(3, 2),
    )(lists, adj0, adj1, *received)


def backward_near(lists, adj0, adj1, back):
    return local(
        backward_near_kernel,
        (shape(NZ * QUAD, TILE, HALF),),
        4,
        "backward_near",
        any_in=1,
        scratch=[pltpu.VMEM((NZ * QUAD + 1, TILE, HALF), jnp.float32)] + LIST_SCRATCH,
        cost=cost(21, 6),
    )(lists, adj0, adj1, back)[0]


def dense(agg_own, agg_other, weight, cot_own, cot_other):
    return local(
        dense_kernel,
        (shape(TILE, 2 * HALF),) + (shape(2 * TILE + W_ROWS, HALF),) * 2,
        5,
        "dense",
    )(agg_own, agg_other, weight, cot_own, cot_other)


def ring_end(parts, *messages):
    return local(
        ring_end_kernel,
        (shape(2, TILE, HALF, dtype=jnp.float32), shape(2 * TILE + W_ROWS, HALF)),
        10,
        "ring_end",
        scratch=[pltpu.VMEM((NZ, W_ROWS, HALF), jnp.bfloat16)],
    )(parts, *messages)


def middle(*operands):
    return local(
        middle_kernel,
        (
            shape(TILE, HALF),
            shape(TILE + 4 * W_ROWS, HALF),
            shape(2, W_ROWS, HALF, dtype=jnp.float32),
        ),
        5,
        "middle",
    )(*operands)


def last(mine, from_core, w_here):
    return local(
        last_kernel,
        (shape(TILE, 2 * HALF), shape(2 * HALF, 2 * HALF, dtype=jnp.float32)),
        3,
        "last",
    )(mine, from_core, w_here)


def add(a, b):
    return (a.astype(jnp.float32) + b.astype(jnp.float32)).astype(jnp.bfloat16)


def per_device(features, adj_tiles, tile_row, tile_col, tile_count, weight, cotangent):
    adj0 = adj_tiles[0, 0]
    block = features[0]

    x_block = quad_permute(block, 2)
    keep, message, own_lists = prepare(tile_row[0, 0], tile_col[0, 0], tile_count, block)
    keep, message = join(keep, message, x_block)
    from_core = quad_permute(message, 1)
    core_keep = from_core[16:].reshape(2, TILE, HALF)
    chunk = jnp.stack([keep[0], core_keep[0], keep[1], core_keep[1]])
    partner_lists = from_core[0, :25].astype(jnp.int32)
    adj1 = quad_permute(adj0, 1)
    cot1 = quad_permute(cotangent, 1)

    up1, down1 = z_shift(chunk, 1), z_shift(chunk, -1)
    up2, down2 = z_shift(up1, 1), z_shift(down1, -1)
    up3, down3 = z_shift(up2, 1), z_shift(down2, -1)
    far_a, far_b = z_shift(up3[:2], 1), z_shift(down3[2:], -1)
    near, lists = forward_near(
        own_lists, partner_lists, adj0, adj1, [chunk, down1, down2, down3, up3, up2, up1]
    )
    shares = forward_far(lists, adj0, adj1, near, far_a, far_b)
    agg = sum(
        (col_move(share, k) if k else share).astype(jnp.float32)
        for k, share in zip(MOVES, shares)
    ).reshape(2 * TILE, HALF)
    agg_other = quad_permute(agg, 1)
    activated, send, send_x = dense(agg, agg_other, weight, cotangent, cot1)
    received = [col_move(send if k < 4 else send_x, k) if k else send for k in MOVES]

    half, size = 2 * TILE, QUAD * TILE
    own, own_down, back = backward_far(lists, adj0, adj1, received)
    blocks = backward_near(lists, adj0, adj1, back)
    parts = blocks.reshape(NZ, size, HALF)
    up1, down1 = z_shift(own, 1), z_shift(own_down, -1)
    up = [add(parts[3, :half], up1[:half]), parts[3, half:], up1[half:]]
    down = [parts[5, :half], add(parts[5, half:], down1[:half]), down1[half:]]
    up2, down2 = z_shift(jnp.concatenate(up), 1), z_shift(jnp.concatenate(down), -1)
    up = [add(parts[2], up2[:size]), up2[size:]]
    down = [add(parts[6], down2[:size]), down2[size:]]
    up3, down3 = z_shift(jnp.concatenate(up), 1), z_shift(jnp.concatenate(down), -1)
    up4 = z_shift(jnp.concatenate([add(parts[1], up3[:size]), up3[size:]]), 1)
    down4 = z_shift(add(parts[7], down3[:size]), -1)

    kept, to_x = ring_end(blocks, own, up1, up2, up3, up4, down1, down2, down3, down4)
    w_send = to_x[half:]
    from_x = quad_permute(to_x, 2)
    w_lo = lax.ppermute(w_send, "col", [(c, c ^ 4) for c in range(NCOL)])
    both = [
        (r * NCOL + c, (r ^ 2) * NCOL + (c ^ 4)) for r in range(NZ * QUAD) for c in range(NCOL)
    ]
    w_both = lax.ppermute(w_send, ("row", "col"), both)
    mine, to_core, w_here = middle(kept, to_x, from_x, w_lo, w_both)
    grad, weight_grad = last(mine, quad_permute(to_core, 1), w_here)
    return (activated, weight_grad, grad[None])


def solution(mesh):
    return jax.shard_map(
        per_device,
        mesh=mesh,
        in_specs=(
            P("col", "row", None),
            P("row", "col", None, None, None),
            P("row", "col", None),
            P("row", "col", None),
            P("row", "col"),
            P(),
            P(("row", "col"), None),
        ),
        out_specs=(P(("row", "col"), None), P(), P("col", "row", None)),
        check_vma=False,
    )
```

```python
import functools
import math

import jax
import jax.numpy as jnp
from jax import lax
from jax.experimental import pallas as pl
from jax.experimental.pallas import tpu as pltpu
from jax.sharding import PartitionSpec as P

NZ = 8
QUAD = 4
NCOL = 8
TILE = 256
HALF = 128
SLOTS = 12
W_ROWS = 128
UNROLL = 4
PART = 16
LIST = 4 * PART + 4
NEAR_MOVES = (0, 1, 5, 3, 7, 4)
MOVES = (0, 6, 2, 5, 7, 1, 3, 4)


def row_pairs(move):
    pairs = []
    for r in range(NZ * QUAD):
        z, q = move(r // QUAD, r % QUAD)
        pairs.append((r, (z % NZ) * QUAD + q))
    return pairs


def quad_permute(x, flip):
    return lax.ppermute(x, "row", row_pairs(lambda z, q: (z, q ^ flip)))


def col_move(x, k):
    pairs = [(c, ((c >> 2) ^ (k >> 2)) * 4 + (c + k) % 4) for c in range(NCOL)]
    return lax.ppermute(x, "col", pairs)


def col_target(k, sign):
    c = lax.axis_index("col")
    return (((c >> 2) ^ (k >> 2)) << 2) + ((c + sign * (k & 3)) & 3)


def z_shift(x, step):
    return lax.ppermute(x, "row", row_pairs(lambda z, q: (z + step, q)))


def prepare_kernel(rows, cols, count, block, keep, message, own_lists):
    core = lax.axis_index("row") & 1

    @pl.when(core == 0)
    def _():
        keep[...] = block[:, :HALF]
        message[16:, :] = block[:, HALF:]

    @pl.when(core == 1)
    def _():
        keep[...] = block[:, HALF:]
        message[16:, :] = block[:, :HALF]

    lane = lax.broadcasted_iota(jnp.int32, (16, HALF), 1)
    values = jnp.zeros((16, HALF), jnp.float32)
    listed = [rows[s] for s in range(SLOTS)] + [cols[s] for s in range(SLOTS)] + [count[0, 0]]
    for n, value in enumerate(listed):
        values = jnp.where(lane == n, value.astype(jnp.float32), values)
        own_lists[n] = value
    message[:16, :] = values.astype(jnp.bfloat16)


def join_kernel(own_keep, own_message, x_block, keep, message):
    core = lax.axis_index("row") & 1
    keep[0] = own_keep[...]
    message[: TILE + 16, :] = own_message[...]

    @pl.when(core == 0)
    def _():
        keep[1] = x_block[:, :HALF]
        message[TILE + 16 :, :] = x_block[:, HALF:]

    @pl.when(core == 1)
    def _():
        keep[1] = x_block[:, HALF:]
        message[TILE + 16 :, :] = x_block[:, :HALF]


def list_slots(own, partner, lists):
    device = lax.axis_index("row")
    z, q = device >> 2, device & 3
    for i, slots in enumerate((own, partner)):
        near, far = jnp.int32(0), jnp.int32(0)
        for s in range(SLOTS):
            tile = slots[12 + s]
            place = (((tile >> 2) - z) & 7) * QUAD + ((tile & 3) ^ q)
            live = (s < slots[24]).astype(jnp.int32)
            is_far = ((place >> 2) == 4).astype(jnp.int32)
            lists[i * PART + is_far * (2 * PART + far - near) + near] = (
                s * 1024 + slots[s] * 64 + place
            )
            far = far + live * is_far
            near = near + live * (1 - is_far)
        for u in range(UNROLL - 1):
            lists[i * PART + near + u] = 8 * 64 + 32
        lists[4 * PART + i] = near
        lists[4 * PART + 2 + i] = far


def slot_products(lists, far, adj_refs, product, add_to):
    unroll = 1 if far else UNROLL
    for i, adj in enumerate(adj_refs):
        part = 2 * far + i

        @pl.loop(0, (lists[4 * PART + part] + unroll - 1) // unroll)
        def _(step, i=i, adj=adj, part=part):
            codes = [lists[part * PART + step * unroll + u] for u in range(unroll)]
            places = [((code >> 6) & 15, i, code & 63) for code in codes]
            values = [product(adj[code >> 10], *at) for code, at in zip(codes, places)]
            for value, at in zip(values, places):
                add_to(value, *at)


def forward_near_kernel(own_any, partner_any, adj0, adj1, *refs):
    pieces, (acc, lists, panel, own, partner, sems) = refs[:7], refs[7:]
    copies = [
        pltpu.make_async_copy(own_any, own, sems.at[0]),
        pltpu.make_async_copy(partner_any, partner, sems.at[1]),
    ]
    for copy in copies:
        copy.start()
    for place, piece in zip((0, 1, 2, 3, 5, 6, 7), pieces):
        panel[place * QUAD : (place + 1) * QUAD] = piece[...]
    acc[...] = jnp.zeros_like(acc)
    for copy in copies:
        copy.wait()
    list_slots(own, partner, lists)

    def product(tile, row, i, place):
        return jnp.dot(tile, panel[place & 31], preferred_element_type=jnp.float32)

    def add_to(value, row, i, place):
        acc[2 * row + i] += value

    slot_products(lists, False, (adj0, adj1), product, add_to)


def forward_far_kernel(lists_any, adj0, adj1, near, far_a, far_b, *refs):
    outs, (acc, far, lists, sem) = refs[:NCOL], refs[NCOL:]
    copy = pltpu.make_async_copy(lists_any, lists, sem)
    copy.start()
    far[:2] = far_a[...]
    far[2:] = far_b[...]
    acc[...] = near[...]
    copy.wait()

    def product(tile, row, i, place):
        return jnp.dot(tile, far[place & 3], preferred_element_type=jnp.float32)

    def add_to(value, row, i, place):
        acc[2 * row + i] += value

    slot_products(lists, True, (adj0, adj1), product, add_to)
    for k, out in zip(MOVES, outs):
        row = col_target(k, 1)
        for i in range(2):
            out[i] = acc[2 * row + i].astype(jnp.bfloat16)


def backward_products(lists, adj_refs, back, acc, far):
    def product(tile, row, i, place):
        return lax.dot_general(
            tile,
            back[row & 7, pl.ds(i * TILE, TILE), :],
            (((0,), (0,)), ((), ())),
            preferred_element_type=jnp.float32,
        )

    def add_to(value, row, i, place):
        acc[place & 3 if far else place] += value

    slot_products(lists, far, adj_refs, product, add_to)


def backward_far_kernel(lists_any, adj0, adj1, *refs):
    received, (up, down, back, acc, lists, sem, pieces) = refs[:NCOL], refs[NCOL:]
    copy = pltpu.make_async_copy(lists_any, lists, sem)
    copy.start()
    for k, ref in zip(NEAR_MOVES, received):
        source = col_target(k, -1)
        back[source] = ref[: 2 * TILE, :]
        pieces[source] = ref[2 * TILE :, :]
    for h, ref in enumerate(received[len(NEAR_MOVES) :]):
        for j, k in enumerate((2, 6)):
            source = col_target(k, -1)
            start = j * (TILE + W_ROWS // 2)
            back[source, h * TILE : (h + 1) * TILE, :] = ref[start : start + TILE, :]
            pieces[source, h * W_ROWS // 2 : (h + 1) * W_ROWS // 2, :] = ref[
                start + TILE : start + TILE + W_ROWS // 2, :
            ]
    acc[...] = jnp.zeros_like(acc)
    piece = pieces[0].astype(jnp.float32)
    for c in range(1, NCOL):
        piece = piece + pieces[c].astype(jnp.float32)
    for out in (up, down):
        out[2 * TILE :, :] = piece.astype(jnp.bfloat16)
    copy.wait()
    backward_products(lists, (adj0, adj1), back, acc, True)
    for k in range(QUAD):
        part = pl.ds((k & 1) * TILE, TILE)
        (up, down)[k >> 1][part, :] = acc[k].astype(jnp.bfloat16)


def backward_near_kernel(lists_any, adj0, adj1, back, out, acc, lists, sem):
    copy = pltpu.make_async_copy(lists_any, lists, sem)
    copy.start()
    acc[...] = jnp.zeros_like(acc)
    copy.wait()
    backward_products(lists, (adj0, adj1), back, acc, False)
    out[...] = acc[: NZ * QUAD].astype(jnp.bfloat16)


def split(x):
    high = x.astype(jnp.bfloat16)
    return high, (x - high.astype(jnp.float32)).astype(jnp.bfloat16)


def dense_kernel(agg_own, agg_other, weight, cot_own, cot_other, act_out, send, send_x):
    first = (lax.axis_index("row") & 1) == 0
    own = agg_own[...]
    other = jnp.concatenate([agg_other[TILE:, :], agg_other[:TILE, :]], axis=0)
    w = weight[...]
    w_other_half = jnp.where(first, w[HALF:], w[:HALF])
    w_half = jnp.where(first, w[:HALF], w[HALF:])

    def dot(a, b, dims=((1,), (0,))):
        return lax.dot_general(a, b, (dims, ((), ())), preferred_element_type=jnp.float32)

    own_hi, own_lo = split(own)
    other_hi, other_lo = split(other)
    v = (dot(own_hi, w_half) + dot(own_lo, w_half)) + (
        dot(other_hi, w_other_half) + dot(other_lo, w_other_half)
    )
    scale = math.sqrt(2.0 / math.pi)
    square = v * v
    t = jnp.tanh(scale * (v + 0.044715 * (square * v)))
    cdf = 0.5 * (1.0 + t)
    act_out[...] = (v[:TILE] * cdf[:TILE]).astype(jnp.bfloat16)
    slope = cdf + 0.5 * v * ((1.0 - t) * (1.0 + t)) * (scale * (1.0 + 3.0 * 0.044715 * square))
    cot = jnp.concatenate([cot_own[...], cot_other[...]], axis=0).astype(jnp.float32)
    grad_hi, grad_lo = split(cot * slope)
    nodes = ((1,), (1,))
    back = (dot(grad_hi, w_half, nodes) + dot(grad_lo, w_half, nodes)).astype(jnp.bfloat16)
    rows = ((0,), (0,))
    w_part = (
        dot(own_hi, grad_hi, rows) + dot(own_lo, grad_hi, rows) + dot(own_hi, grad_lo, rows)
    )
    x_lo = lax.axis_index("col") >> 2
    for out, dest in ((send, x_lo), (send_x, 1 - x_lo)):
        out[: 2 * TILE, :] = back
        piece = jnp.where(dest == 0, w_part[:64], w_part[64:]).astype(jnp.bfloat16)
        out[2 * TILE : 2 * TILE + 64, :] = piece[:, :HALF]
        out[2 * TILE + 64 :, :] = piece[:, HALF:]


def f32(ref, start, rows=TILE):
    return ref[start : start + rows, :].astype(jnp.float32)


def ring_end_kernel(
    parts, own, up1, up2, up3, up4, down1, down2, down3, down4, kept, message, by_step
):
    z = lax.axis_index("row") >> 2
    half, size = 2 * TILE, QUAD * TILE
    pieces = (
        (own, half),
        (down1, half),
        (down2, size),
        (down3, size),
        (up4, size),
        (up3, size),
        (up2, size),
        (up1, half),
    )
    for k, (ref, start) in enumerate(pieces):
        by_step[(k + z) & 7] = ref[start:, :]
    w_sum = by_step[0].astype(jnp.float32)
    for a in range(1, NZ):
        w_sum = w_sum + by_step[a].astype(jnp.float32)
    message[half:, :] = w_sum.astype(jnp.bfloat16)
    for k in range(QUAD):
        start = k * TILE
        total = parts[k].astype(jnp.float32) + f32(up4, start) + f32(down4, start)
        if k < 2:
            kept[k] = total
        else:
            message[start - half : start - half + TILE, :] = total.astype(jnp.bfloat16)


def middle_kernel(kept, sent, from_x, w_lo, w_both, mine, message, w_here):
    x_lo = lax.axis_index("col") >> 2
    half = 2 * TILE
    for k, ref in enumerate((mine, message)):
        ref[:TILE, :] = (kept[k] + f32(from_x, k * TILE)).astype(jnp.bfloat16)
    sums = (
        f32(sent, half, W_ROWS) + f32(from_x, half, W_ROWS),
        w_lo[...].astype(jnp.float32) + w_both[...].astype(jnp.float32),
    )
    for value, place in zip(sums, (x_lo, 1 - x_lo)):
        high, low = split(value)
        w_here[place] = high.astype(jnp.float32) + low.astype(jnp.float32)
        start = pl.multiple_of(TILE + place * 2 * W_ROWS, W_ROWS)
        message[pl.ds(start, W_ROWS), :] = high
        message[pl.ds(start + W_ROWS, W_ROWS), :] = low


def last_kernel(mine, from_core, w_here, grad_out, w_out):
    core = lax.axis_index("row") & 1
    scale = 1.0 / 256.0

    def place(value, start):
        rows = pl.ds(pl.multiple_of(start, 64), 64)
        w_out[rows, :HALF] = value[:64, :] * scale
        w_out[rows, HALF:] = value[64:, :] * scale

    for x_lo in range(2):
        start = TILE + x_lo * 2 * W_ROWS
        place(w_here[x_lo], core * HALF + x_lo * 64)
        w_core = f32(from_core, start, W_ROWS) + f32(from_core, start + W_ROWS, W_ROWS)
        place(w_core, (1 - core) * HALF + x_lo * 64)

    @pl.when(core == 0)
    def _():
        grad_out[:, :HALF] = mine[...]
        grad_out[:, HALF:] = from_core[:TILE, :]

    @pl.when(core == 1)
    def _():
        grad_out[:, HALF:] = mine[...]
        grad_out[:, :HALF] = from_core[:TILE, :]


SMEM = pl.BlockSpec(memory_space=pltpu.SMEM)
VMEM = pl.BlockSpec(memory_space=pltpu.VMEM)
ANY = pl.BlockSpec(memory_space=pl.ANY)


def params(mib):
    return pltpu.CompilerParams(vmem_limit_bytes=mib << 20)


LIST_SCRATCH = [pltpu.SMEM((LIST,), jnp.int32), pltpu.SemaphoreType.DMA]


def cost(slots, size):
    return pl.CostEstimate(
        flops=slots * 2 * TILE * TILE * HALF, bytes_accessed=size << 20, transcendentals=0
    )


LISTS = [SMEM] * 4


def shape(*dims, dtype=jnp.bfloat16):
    return jax.ShapeDtypeStruct(dims, dtype)


def local(kernel, outs, n_in, name, scalars=0, any_in=0, scratch=(), cost=None, scalar_out=0):
    return pl.pallas_call(
        kernel,
        out_shape=outs,
        in_specs=[SMEM] * scalars + [ANY] * any_in + [VMEM] * (n_in - scalars - any_in),
        out_specs=(VMEM,) * (len(outs) - scalar_out) + (SMEM,) * scalar_out,
        scratch_shapes=scratch,
        compiler_params=params(20),
        cost_estimate=cost,
        name=name,
    )


def prepare(rows, cols, count, block):
    return local(
        prepare_kernel,
        (shape(TILE, HALF), shape(TILE + 16, HALF), shape(25, dtype=jnp.int32)),
        4,
        "prepare",
        scalars=3,
        scalar_out=1,
    )(rows, cols, count, block)


def join(own_keep, own_message, x_block):
    return local(
        join_kernel, (shape(2, TILE, HALF), shape(2 * TILE + 16, HALF)), 3, "join"
    )(own_keep, own_message, x_block)


def forward_near(own, partner, adj0, adj1, pieces):
    return local(
        forward_near_kernel,
        (shape(18, TILE, HALF, dtype=jnp.float32), shape(LIST, dtype=jnp.int32)),
        11,
        "forward_near",
        any_in=2,
        scalar_out=1,
        scratch=[
            pltpu.VMEM((NZ * QUAD, TILE, HALF), jnp.bfloat16),
            pltpu.SMEM((25,), jnp.int32),
            pltpu.SMEM((25,), jnp.int32),
            pltpu.SemaphoreType.DMA((2,)),
        ],
        cost=cost(21, 6),
    )(own, partner, adj0, adj1, *pieces)


def forward_far(lists, adj0, adj1, near, far_a, far_b):
    return local(
        forward_far_kernel,
        (shape(2, TILE, HALF),) * NCOL,
        6,
        "forward_far",
        any_in=1,
        scratch=[
            pltpu.VMEM((18, TILE, HALF), jnp.float32),
            pltpu.VMEM((QUAD, TILE, HALF), jnp.bfloat16),
        ]
        + LIST_SCRATCH,
        cost=cost(3, 4),
    )(lists, adj0, adj1, near, far_a, far_b)


def backward_far(lists, adj0, adj1, received):
    message = shape(2 * TILE + W_ROWS, HALF)
    return local(
        backward_far_kernel,
        (message, message, shape(NCOL, 2 * TILE, HALF)),
        11,
        "backward_far",
        any_in=1,
        scratch=[pltpu.VMEM((QUAD, TILE, HALF), jnp.float32)]
        + LIST_SCRATCH
        + [pltpu.VMEM((NCOL, W_ROWS, HALF), jnp.bfloat16)],
        cost=cost(3, 2),
    )(lists, adj0, adj1, *received)


def backward_near(lists, adj0, adj1, back):
    return local(
        backward_near_kernel,
        (shape(NZ * QUAD, TILE, HALF),),
        4,
        "backward_near",
        any_in=1,
        scratch=[pltpu.VMEM((NZ * QUAD + 1, TILE, HALF), jnp.float32)] + LIST_SCRATCH,
        cost=cost(21, 6),
    )(lists, adj0, adj1, back)[0]


def dense(agg_own, agg_other, weight, cot_own, cot_other):
    return local(
        dense_kernel,
        (shape(TILE, 2 * HALF),) + (shape(2 * TILE + W_ROWS, HALF),) * 2,
        5,
        "dense",
    )(agg_own, agg_other, weight, cot_own, cot_other)


def enter_kernel(in_step_any, up, down, up_out, down_out):
    del in_step_any
    up_out[...] = up[...]
    down_out[...] = down[...]


def enter(in_step, up, down):
    message = shape(2 * TILE + W_ROWS, HALF)
    return local(enter_kernel, (message, message), 3, "enter", any_in=1)(in_step, up, down)


def ring_end(parts, *messages):
    return local(
        ring_end_kernel,
        (shape(2, TILE, HALF, dtype=jnp.float32), shape(2 * TILE + W_ROWS, HALF)),
        10,
        "ring_end",
        scratch=[pltpu.VMEM((NZ, W_ROWS, HALF), jnp.bfloat16)],
    )(parts, *messages)


def middle(*operands):
    return local(
        middle_kernel,
        (
            shape(TILE, HALF),
            shape(TILE + 4 * W_ROWS, HALF),
            shape(2, W_ROWS, HALF, dtype=jnp.float32),
        ),
        5,
        "middle",
    )(*operands)


def last(mine, from_core, w_here):
    return local(
        last_kernel,
        (shape(TILE, 2 * HALF), shape(2 * HALF, 2 * HALF, dtype=jnp.float32)),
        3,
        "last",
    )(mine, from_core, w_here)


def add(a, b):
    return (a.astype(jnp.float32) + b.astype(jnp.float32)).astype(jnp.bfloat16)


def per_device(features, adj_tiles, tile_row, tile_col, tile_count, weight, cotangent):
    adj0 = adj_tiles[0, 0]
    block = features[0]

    x_block = quad_permute(block, 2)
    keep, message, own_lists = prepare(tile_row[0, 0], tile_col[0, 0], tile_count, block)
    keep, message = join(keep, message, x_block)
    from_core = quad_permute(message, 1)
    core_keep = from_core[16:].reshape(2, TILE, HALF)
    chunk = jnp.stack([keep[0], core_keep[0], keep[1], core_keep[1]])
    partner_lists = from_core[0, :25].astype(jnp.int32)
    adj1 = quad_permute(adj0, 1)
    cot1 = quad_permute(cotangent, 1)

    up1, down1 = z_shift(chunk, 1), z_shift(chunk, -1)
    up2, down2 = z_shift(up1, 1), z_shift(down1, -1)
    up3, down3 = z_shift(up2, 1), z_shift(down2, -1)
    far_a, far_b = z_shift(up3[:2], 1), z_shift(down3[2:], -1)
    near, lists = forward_near(
        own_lists, partner_lists, adj0, adj1, [chunk, down1, down2, down3, up3, up2, up1]
    )
    shares = forward_far(lists, adj0, adj1, near, far_a, far_b)
    agg = sum(
        (col_move(share, k) if k else share).astype(jnp.float32)
        for k, share in zip(MOVES, shares)
    ).reshape(2 * TILE, HALF)
    agg_other = quad_permute(agg, 1)
    activated, send, send_x = dense(agg, agg_other, weight, cotangent, cot1)
    received = [col_move(send if k < 4 else send_x, k) if k else send for k in NEAR_MOVES]

    def forward(near, across, h):
        rows = [slice(h * TILE, (h + 1) * TILE)]
        rows += [slice(2 * TILE + h * W_ROWS // 2, 2 * TILE + (h + 1) * W_ROWS // 2)]
        message = jnp.concatenate([x[r] for x in (near, across) for r in rows])
        return col_move(message, 3 if h else 1)

    received += [forward(received[1], received[2], 0), forward(received[3], received[4], 1)]

    half, size = 2 * TILE, QUAD * TILE
    in_step = quad_permute(received[-1][:16], 1)
    own, own_down, back = backward_far(lists, adj0, adj1, received)
    own, own_down = enter(in_step, own, own_down)
    blocks = backward_near(lists, adj0, adj1, back)
    parts = blocks.reshape(NZ, size, HALF)
    up1, down1 = z_shift(own, 1), z_shift(own_down, -1)
    up = [add(parts[3, :half], up1[:half]), parts[3, half:], up1[half:]]
    down = [parts[5, :half], add(parts[5, half:], down1[:half]), down1[half:]]
    up2, down2 = z_shift(jnp.concatenate(up), 1), z_shift(jnp.concatenate(down), -1)
    up = [add(parts[2], up2[:size]), up2[size:]]
    down = [add(parts[6], down2[:size]), down2[size:]]
    up3, down3 = z_shift(jnp.concatenate(up), 1), z_shift(jnp.concatenate(down), -1)
    up4 = z_shift(jnp.concatenate([add(parts[1], up3[:size]), up3[size:]]), 1)
    down4 = z_shift(add(parts[7], down3[:size]), -1)

    kept, to_x = ring_end(blocks, own, up1, up2, up3, up4, down1, down2, down3, down4)
    w_send = to_x[half:]
    from_x = quad_permute(to_x, 2)
    w_lo = lax.ppermute(w_send, "col", [(c, c ^ 4) for c in range(NCOL)])
    both = [
        (r * NCOL + c, (r ^ 2) * NCOL + (c ^ 4)) for r in range(NZ * QUAD) for c in range(NCOL)
    ]
    w_both = lax.ppermute(w_send, ("row", "col"), both)
    mine, to_core, w_here = middle(kept, to_x, from_x, w_lo, w_both)
    grad, weight_grad = last(mine, quad_permute(to_core, 1), w_here)
    return (activated, weight_grad, grad[None])


def solution(mesh):
    return jax.shard_map(
        per_device,
        mesh=mesh,
        in_specs=(
            P("col", "row", None),
            P("row", "col", None, None, None),
            P("row", "col", None),
            P("row", "col", None),
            P("row", "col"),
            P(),
            P(("row", "col"), None),
        ),
        out_specs=(P(("row", "col"), None), P(), P("col", "row", None)),
        check_vma=False,
    )
```

```python
import functools
import math

import jax
import jax.numpy as jnp
from jax import lax
from jax.experimental import pallas as pl
from jax.experimental.pallas import tpu as pltpu
from jax.sharding import PartitionSpec as P

NZ = 8
QUAD = 4
NCOL = 8
TILE = 256
HALF = 128
SLOTS = 12
W_ROWS = 128
UNROLL = 4
PART = 16
LIST = 4 * PART + 4
MOVES = (0, 6, 2, 5, 7, 1, 3, 4)


def row_pairs(move):
    pairs = []
    for r in range(NZ * QUAD):
        z, q = move(r // QUAD, r % QUAD)
        pairs.append((r, (z % NZ) * QUAD + q))
    return pairs


def quad_permute(x, flip):
    return lax.ppermute(x, "row", row_pairs(lambda z, q: (z, q ^ flip)))


def col_move(x, k):
    pairs = [(c, ((c >> 2) ^ (k >> 2)) * 4 + (c + k) % 4) for c in range(NCOL)]
    return lax.ppermute(x, "col", pairs)


def col_target(k, sign):
    c = lax.axis_index("col")
    return (((c >> 2) ^ (k >> 2)) << 2) + ((c + sign * (k & 3)) & 3)


def z_shift(x, step):
    return lax.ppermute(x, "row", row_pairs(lambda z, q: (z + step, q)))


def prepare_kernel(rows, cols, count, block, keep, message, own_lists):
    core = lax.axis_index("row") & 1

    @pl.when(core == 0)
    def _():
        keep[...] = block[:, :HALF]
        message[16:, :] = block[:, HALF:]

    @pl.when(core == 1)
    def _():
        keep[...] = block[:, HALF:]
        message[16:, :] = block[:, :HALF]

    lane = lax.broadcasted_iota(jnp.int32, (16, HALF), 1)
    values = jnp.zeros((16, HALF), jnp.float32)
    listed = [rows[s] for s in range(SLOTS)] + [cols[s] for s in range(SLOTS)] + [count[0, 0]]
    for n, value in enumerate(listed):
        values = jnp.where(lane == n, value.astype(jnp.float32), values)
        own_lists[n] = value
    message[:16, :] = values.astype(jnp.bfloat16)


def join_kernel(own_keep, own_message, x_block, keep, message):
    core = lax.axis_index("row") & 1
    keep[0] = own_keep[...]
    message[: TILE + 16, :] = own_message[...]

    @pl.when(core == 0)
    def _():
        keep[1] = x_block[:, :HALF]
        message[TILE + 16 :, :] = x_block[:, HALF:]

    @pl.when(core == 1)
    def _():
        keep[1] = x_block[:, HALF:]
        message[TILE + 16 :, :] = x_block[:, :HALF]


def list_slots(own, partner, lists):
    device = lax.axis_index("row")
    z, q = device >> 2, device & 3
    for i, slots in enumerate((own, partner)):
        near, far = jnp.int32(0), jnp.int32(0)
        for s in range(SLOTS):
            tile = slots[12 + s]
            place = (((tile >> 2) - z) & 7) * QUAD + ((tile & 3) ^ q)
            live = (s < slots[24]).astype(jnp.int32)
            is_far = ((place >> 2) == 4).astype(jnp.int32)
            lists[i * PART + is_far * (2 * PART + far - near) + near] = (
                s * 1024 + slots[s] * 64 + place
            )
            far = far + live * is_far
            near = near + live * (1 - is_far)
        for u in range(UNROLL - 1):
            lists[i * PART + near + u] = 8 * 64 + 32
        lists[4 * PART + i] = near
        lists[4 * PART + 2 + i] = far


def slot_products(lists, far, adj_refs, product, add_to):
    unroll = 1 if far else UNROLL
    for i, adj in enumerate(adj_refs):
        part = 2 * far + i

        @pl.loop(0, (lists[4 * PART + part] + unroll - 1) // unroll)
        def _(step, i=i, adj=adj, part=part):
            codes = [lists[part * PART + step * unroll + u] for u in range(unroll)]
            places = [((code >> 6) & 15, i, code & 63) for code in codes]
            values = [product(adj[code >> 10], *at) for code, at in zip(codes, places)]
            for value, at in zip(values, places):
                add_to(value, *at)


def forward_near_kernel(own_any, partner_any, adj0, adj1, *refs):
    pieces, (acc, lists, panel, own, partner, sems) = refs[:7], refs[7:]
    copies = [
        pltpu.make_async_copy(own_any, own, sems.at[0]),
        pltpu.make_async_copy(partner_any, partner, sems.at[1]),
    ]
    for copy in copies:
        copy.start()
    for place, piece in zip((0, 1, 2, 3, 5, 6, 7), pieces):
        panel[place * QUAD : (place + 1) * QUAD] = piece[...]
    acc[...] = jnp.zeros_like(acc)
    for copy in copies:
        copy.wait()
    list_slots(own, partner, lists)

    def product(tile, row, i, place):
        return jnp.dot(tile, panel[place & 31], preferred_element_type=jnp.float32)

    def add_to(value, row, i, place):
        acc[2 * row + i] += value

    slot_products(lists, False, (adj0, adj1), product, add_to)


def forward_far_kernel(lists_any, adj0, adj1, near, far_a, far_b, *refs):
    outs, (acc, far, lists, sem) = refs[:NCOL], refs[NCOL:]
    copy = pltpu.make_async_copy(lists_any, lists, sem)
    copy.start()
    far[:2] = far_a[...]
    far[2:] = far_b[...]
    acc[...] = near[...]
    copy.wait()

    def product(tile, row, i, place):
        return jnp.dot(tile, far[place & 3], preferred_element_type=jnp.float32)

    def add_to(value, row, i, place):
        acc[2 * row + i] += value

    slot_products(lists, True, (adj0, adj1), product, add_to)
    for k, out in zip(MOVES, outs):
        row = col_target(k, 1)
        for i in range(2):
            out[i] = acc[2 * row + i].astype(jnp.bfloat16)


def backward_products(lists, adj_refs, back, acc, far):
    def product(tile, row, i, place):
        return lax.dot_general(
            tile,
            back[row & 7, pl.ds(i * TILE, TILE), :],
            (((0,), (0,)), ((), ())),
            preferred_element_type=jnp.float32,
        )

    def add_to(value, row, i, place):
        acc[place & 3 if far else place] += value

    slot_products(lists, far, adj_refs, product, add_to)


def backward_far_kernel(lists_any, adj0, adj1, back, up, down, acc, lists, sem):
    copy = pltpu.make_async_copy(lists_any, lists, sem)
    copy.start()
    acc[...] = jnp.zeros_like(acc)
    piece = back[0, 2 * TILE :, :].astype(jnp.float32)
    for c in range(1, NCOL):
        piece = piece + back[c, 2 * TILE :, :].astype(jnp.float32)
    for out in (up, down):
        out[2 * TILE :, :] = piece.astype(jnp.bfloat16)
    copy.wait()
    backward_products(lists, (adj0, adj1), back, acc, True)
    for k in range(QUAD):
        part = pl.ds((k & 1) * TILE, TILE)
        (up, down)[k >> 1][part, :] = acc[k].astype(jnp.bfloat16)


def backward_near_kernel(lists_any, adj0, adj1, back, out, acc, lists, sem):
    copy = pltpu.make_async_copy(lists_any, lists, sem)
    copy.start()
    acc[...] = jnp.zeros_like(acc)
    copy.wait()
    backward_products(lists, (adj0, adj1), back, acc, False)
    out[...] = acc[: NZ * QUAD].astype(jnp.bfloat16)


def split(x):
    high = x.astype(jnp.bfloat16)
    return high, (x - high.astype(jnp.float32)).astype(jnp.bfloat16)


def dense_kernel(agg_own, agg_other, weight, cot_own, cot_other, act_out, send):
    first = (lax.axis_index("row") & 1) == 0
    own = agg_own[...]
    other = jnp.concatenate([agg_other[TILE:, :], agg_other[:TILE, :]], axis=0)
    w = weight[...]
    w_other_half = jnp.where(first, w[HALF:], w[:HALF])
    w_half = jnp.where(first, w[:HALF], w[HALF:])

    def dot(a, b, dims=((1,), (0,))):
        return lax.dot_general(a, b, (dims, ((), ())), preferred_element_type=jnp.float32)

    own_hi, own_lo = split(own)
    other_hi, other_lo = split(other)
    v = (dot(own_hi, w_half) + dot(own_lo, w_half)) + (
        dot(other_hi, w_other_half) + dot(other_lo, w_other_half)
    )
    scale = math.sqrt(2.0 / math.pi)
    square = v * v
    t = jnp.tanh(scale * (v + 0.044715 * (square * v)))
    cdf = 0.5 * (1.0 + t)
    act_out[...] = (v[:TILE] * cdf[:TILE]).astype(jnp.bfloat16)
    slope = cdf + 0.5 * v * ((1.0 - t) * (1.0 + t)) * (scale * (1.0 + 3.0 * 0.044715 * square))
    cot = jnp.concatenate([cot_own[...], cot_other[...]], axis=0).astype(jnp.float32)
    grad_hi, grad_lo = split(cot * slope)
    nodes = ((1,), (1,))
    back = (dot(grad_hi, w_half, nodes) + dot(grad_lo, w_half, nodes)).astype(jnp.bfloat16)
    rows = ((0,), (0,))
    w_part = (
        dot(own_hi, grad_hi, rows) + dot(own_lo, grad_hi, rows) + dot(own_hi, grad_lo, rows)
    )
    w_part = w_part.astype(jnp.bfloat16)
    for c in range(NCOL):
        send[c, : 2 * TILE, :] = back
        piece = w_part[64 * (c // 4) : 64 * (c // 4) + 64]
        send[c, 2 * TILE : 2 * TILE + 64, :] = piece[:, :HALF]
        send[c, 2 * TILE + 64 :, :] = piece[:, HALF:]


def f32(ref, start, rows=TILE):
    return ref[start : start + rows, :].astype(jnp.float32)


def ring_end_kernel(
    parts, own, up1, up2, up3, up4, down1, down2, down3, down4, kept, message, by_step
):
    z = lax.axis_index("row") >> 2
    half, size = 2 * TILE, QUAD * TILE
    pieces = (
        (own, half),
        (down1, half),
        (down2, size),
        (down3, size),
        (up4, size),
        (up3, size),
        (up2, size),
        (up1, half),
    )
    for k, (ref, start) in enumerate(pieces):
        by_step[(k + z) & 7] = ref[start:, :]
    w_sum = by_step[0].astype(jnp.float32)
    for a in range(1, NZ):
        w_sum = w_sum + by_step[a].astype(jnp.float32)
    message[half:, :] = w_sum.astype(jnp.bfloat16)
    for k in range(QUAD):
        start = k * TILE
        total = parts[k].astype(jnp.float32) + f32(up4, start) + f32(down4, start)
        if k < 2:
            kept[k] = total
        else:
            message[start - half : start - half + TILE, :] = total.astype(jnp.bfloat16)


def middle_kernel(kept, sent, from_x, w_lo, w_both, mine, message, w_here):
    x_lo = lax.axis_index("col") >> 2
    half = 2 * TILE
    for k, ref in enumerate((mine, message)):
        ref[:TILE, :] = (kept[k] + f32(from_x, k * TILE)).astype(jnp.bfloat16)
    sums = (
        f32(sent, half, W_ROWS) + f32(from_x, half, W_ROWS),
        w_lo[...].astype(jnp.float32) + w_both[...].astype(jnp.float32),
    )
    for value, place in zip(sums, (x_lo, 1 - x_lo)):
        high, low = split(value)
        w_here[place] = high.astype(jnp.float32) + low.astype(jnp.float32)
        start = pl.multiple_of(TILE + place * 2 * W_ROWS, W_ROWS)
        message[pl.ds(start, W_ROWS), :] = high
        message[pl.ds(start + W_ROWS, W_ROWS), :] = low


def last_kernel(mine, from_core, w_here, grad_out, w_out):
    core = lax.axis_index("row") & 1
    scale = 1.0 / 256.0

    def place(value, start):
        rows = pl.ds(pl.multiple_of(start, 64), 64)
        w_out[rows, :HALF] = value[:64, :] * scale
        w_out[rows, HALF:] = value[64:, :] * scale

    for x_lo in range(2):
        start = TILE + x_lo * 2 * W_ROWS
        place(w_here[x_lo], core * HALF + x_lo * 64)
        w_core = f32(from_core, start, W_ROWS) + f32(from_core, start + W_ROWS, W_ROWS)
        place(w_core, (1 - core) * HALF + x_lo * 64)

    @pl.when(core == 0)
    def _():
        grad_out[:, :HALF] = mine[...]
        grad_out[:, HALF:] = from_core[:TILE, :]

    @pl.when(core == 1)
    def _():
        grad_out[:, HALF:] = mine[...]
        grad_out[:, :HALF] = from_core[:TILE, :]


SMEM = pl.BlockSpec(memory_space=pltpu.SMEM)
VMEM = pl.BlockSpec(memory_space=pltpu.VMEM)
ANY = pl.BlockSpec(memory_space=pl.ANY)


def params(mib):
    return pltpu.CompilerParams(vmem_limit_bytes=mib << 20)


LIST_SCRATCH = [pltpu.SMEM((LIST,), jnp.int32), pltpu.SemaphoreType.DMA]


def cost(slots, size):
    return pl.CostEstimate(
        flops=slots * 2 * TILE * TILE * HALF, bytes_accessed=size << 20, transcendentals=0
    )


LISTS = [SMEM] * 4


def shape(*dims, dtype=jnp.bfloat16):
    return jax.ShapeDtypeStruct(dims, dtype)


def local(kernel, outs, n_in, name, scalars=0, any_in=0, scratch=(), cost=None, scalar_out=0):
    return pl.pallas_call(
        kernel,
        out_shape=outs,
        in_specs=[SMEM] * scalars + [ANY] * any_in + [VMEM] * (n_in - scalars - any_in),
        out_specs=(VMEM,) * (len(outs) - scalar_out) + (SMEM,) * scalar_out,
        scratch_shapes=scratch,
        compiler_params=params(20),
        cost_estimate=cost,
        name=name,
    )


def prepare(rows, cols, count, block):
    return local(
        prepare_kernel,
        (shape(TILE, HALF), shape(TILE + 16, HALF), shape(25, dtype=jnp.int32)),
        4,
        "prepare",
        scalars=3,
        scalar_out=1,
    )(rows, cols, count, block)


def join(own_keep, own_message, x_block):
    return local(
        join_kernel, (shape(2, TILE, HALF), shape(2 * TILE + 16, HALF)), 3, "join"
    )(own_keep, own_message, x_block)


def forward_near(own, partner, adj0, adj1, pieces):
    return local(
        forward_near_kernel,
        (shape(18, TILE, HALF, dtype=jnp.float32), shape(LIST, dtype=jnp.int32)),
        11,
        "forward_near",
        any_in=2,
        scalar_out=1,
        scratch=[
            pltpu.VMEM((NZ * QUAD, TILE, HALF), jnp.bfloat16),
            pltpu.SMEM((25,), jnp.int32),
            pltpu.SMEM((25,), jnp.int32),
            pltpu.SemaphoreType.DMA((2,)),
        ],
        cost=cost(21, 6),
    )(own, partner, adj0, adj1, *pieces)


def forward_far(lists, adj0, adj1, near, far_a, far_b):
    return local(
        forward_far_kernel,
        (shape(2, TILE, HALF),) * NCOL,
        6,
        "forward_far",
        any_in=1,
        scratch=[
            pltpu.VMEM((18, TILE, HALF), jnp.float32),
            pltpu.VMEM((QUAD, TILE, HALF), jnp.bfloat16),
        ]
        + LIST_SCRATCH,
        cost=cost(3, 4),
    )(lists, adj0, adj1, near, far_a, far_b)


def backward_far(lists, adj0, adj1, back):
    message = shape(2 * TILE + W_ROWS, HALF)
    return local(
        backward_far_kernel,
        (message, message),
        4,
        "backward_far",
        any_in=1,
        scratch=[pltpu.VMEM((QUAD, TILE, HALF), jnp.float32)] + LIST_SCRATCH,
        cost=cost(3, 2),
    )(lists, adj0, adj1, back)


def backward_near(lists, adj0, adj1, back):
    return local(
        backward_near_kernel,
        (shape(NZ * QUAD, TILE, HALF),),
        4,
        "backward_near",
        any_in=1,
        scratch=[pltpu.VMEM((NZ * QUAD + 1, TILE, HALF), jnp.float32)] + LIST_SCRATCH,
        cost=cost(21, 6),
    )(lists, adj0, adj1, back)[0]


def dense(agg_own, agg_other, weight, cot_own, cot_other):
    return local(
        dense_kernel,
        (shape(TILE, 2 * HALF), shape(NCOL, 2 * TILE + W_ROWS, HALF)),
        5,
        "dense",
    )(agg_own, agg_other, weight, cot_own, cot_other)


def ring_end(parts, *messages):
    return local(
        ring_end_kernel,
        (shape(2, TILE, HALF, dtype=jnp.float32), shape(2 * TILE + W_ROWS, HALF)),
        10,
        "ring_end",
        scratch=[pltpu.VMEM((NZ, W_ROWS, HALF), jnp.bfloat16)],
    )(parts, *messages)


def middle(*operands):
    return local(
        middle_kernel,
        (
            shape(TILE, HALF),
            shape(TILE + 4 * W_ROWS, HALF),
            shape(2, W_ROWS, HALF, dtype=jnp.float32),
        ),
        5,
        "middle",
    )(*operands)


def last(mine, from_core, w_here):
    return local(
        last_kernel,
        (shape(TILE, 2 * HALF), shape(2 * HALF, 2 * HALF, dtype=jnp.float32)),
        3,
        "last",
    )(mine, from_core, w_here)


def add(a, b):
    return (a.astype(jnp.float32) + b.astype(jnp.float32)).astype(jnp.bfloat16)


def per_device(features, adj_tiles, tile_row, tile_col, tile_count, weight, cotangent):
    adj0 = adj_tiles[0, 0]
    block = features[0]

    x_block = quad_permute(block, 2)
    keep, message, own_lists = prepare(tile_row[0, 0], tile_col[0, 0], tile_count, block)
    keep, message = join(keep, message, x_block)
    from_core = quad_permute(message, 1)
    core_keep = from_core[16:].reshape(2, TILE, HALF)
    chunk = jnp.stack([keep[0], core_keep[0], keep[1], core_keep[1]])
    partner_lists = from_core[0, :25].astype(jnp.int32)
    adj1 = quad_permute(adj0, 1)
    cot1 = quad_permute(cotangent, 1)

    up1, down1 = z_shift(chunk, 1), z_shift(chunk, -1)
    up2, down2 = z_shift(up1, 1), z_shift(down1, -1)
    up3, down3 = z_shift(up2, 1), z_shift(down2, -1)
    far_a, far_b = z_shift(up3[:2], 1), z_shift(down3[2:], -1)
    near, lists = forward_near(
        own_lists, partner_lists, adj0, adj1, [chunk, down1, down2, down3, up3, up2, up1]
    )
    shares = forward_far(lists, adj0, adj1, near, far_a, far_b)
    agg = sum(
        (col_move(share, k) if k else share).astype(jnp.float32)
        for k, share in zip(MOVES, shares)
    ).reshape(2 * TILE, HALF)
    agg_other = quad_permute(agg, 1)
    activated, send = dense(agg, agg_other, weight, cotangent, cot1)
    received = lax.all_to_all(send, "col", 0, 0, tiled=True)

    half, size = 2 * TILE, QUAD * TILE
    own, own_down = backward_far(lists, adj0, adj1, received)
    blocks = backward_near(lists, adj0, adj1, received)
    parts = blocks.reshape(NZ, size, HALF)
    up1, down1 = z_shift(own, 1), z_shift(own_down, -1)
    up = [add(parts[3, :half], up1[:half]), parts[3, half:], up1[half:]]
    down = [parts[5, :half], add(parts[5, half:], down1[:half]), down1[half:]]
    up2, down2 = z_shift(jnp.concatenate(up), 1), z_shift(jnp.concatenate(down), -1)
    up = [add(parts[2], up2[:size]), up2[size:]]
    down = [add(parts[6], down2[:size]), down2[size:]]
    up3, down3 = z_shift(jnp.concatenate(up), 1), z_shift(jnp.concatenate(down), -1)
    up4 = z_shift(jnp.concatenate([add(parts[1], up3[:size]), up3[size:]]), 1)
    down4 = z_shift(add(parts[7], down3[:size]), -1)

    kept, to_x = ring_end(blocks, own, up1, up2, up3, up4, down1, down2, down3, down4)
    w_send = to_x[half:]
    from_x = quad_permute(to_x, 2)
    w_lo = lax.ppermute(w_send, "col", [(c, c ^ 4) for c in range(NCOL)])
    both = [
        (r * NCOL + c, (r ^ 2) * NCOL + (c ^ 4)) for r in range(NZ * QUAD) for c in range(NCOL)
    ]
    w_both = lax.ppermute(w_send, ("row", "col"), both)
    mine, to_core, w_here = middle(kept, to_x, from_x, w_lo, w_both)
    grad, weight_grad = last(mine, quad_permute(to_core, 1), w_here)
    return (activated, weight_grad, grad[None])


def solution(mesh):
    return jax.shard_map(
        per_device,
        mesh=mesh,
        in_specs=(
            P("col", "row", None),
            P("row", "col", None, None, None),
            P("row", "col", None),
            P("row", "col", None),
            P("row", "col"),
            P(),
            P(("row", "col"), None),
        ),
        out_specs=(P(("row", "col"), None), P(), P("col", "row", None)),
        check_vma=False,
    )
```

```python
import functools
import math

import jax
import jax.numpy as jnp
from jax import lax
from jax.experimental import pallas as pl
from jax.experimental.pallas import tpu as pltpu
from jax.sharding import PartitionSpec as P

NZ = 8
QUAD = 4
NCOL = 8
TILE = 256
HALF = 128
SLOTS = 12
W_ROWS = 128
UNROLL = 4
PART = 16
LIST = 4 * PART + 4
MOVES = (0, 6, 2, 5, 7, 1, 3, 4)


def row_pairs(move):
    pairs = []
    for r in range(NZ * QUAD):
        z, q = move(r // QUAD, r % QUAD)
        pairs.append((r, (z % NZ) * QUAD + q))
    return pairs


def quad_permute(x, flip):
    return lax.ppermute(x, "row", row_pairs(lambda z, q: (z, q ^ flip)))


def col_move(x, k):
    pairs = [(c, ((c >> 2) ^ (k >> 2)) * 4 + (c + k) % 4) for c in range(NCOL)]
    return lax.ppermute(x, "col", pairs)


def col_target(k, sign):
    c = lax.axis_index("col")
    return (((c >> 2) ^ (k >> 2)) << 2) + ((c + sign * (k & 3)) & 3)


def z_shift(x, step):
    return lax.ppermute(x, "row", row_pairs(lambda z, q: (z + step, q)))


def prepare_kernel(rows, cols, count, block, keep, message, own_lists):
    core = lax.axis_index("row") & 1

    @pl.when(core == 0)
    def _():
        keep[...] = block[:, :HALF]
        message[16:, :] = block[:, HALF:]

    @pl.when(core == 1)
    def _():
        keep[...] = block[:, HALF:]
        message[16:, :] = block[:, :HALF]

    lane = lax.broadcasted_iota(jnp.int32, (16, HALF), 1)
    values = jnp.zeros((16, HALF), jnp.float32)
    listed = [rows[s] for s in range(SLOTS)] + [cols[s] for s in range(SLOTS)] + [count[0, 0]]
    for n, value in enumerate(listed):
        values = jnp.where(lane == n, value.astype(jnp.float32), values)
        own_lists[n] = value
    message[:16, :] = values.astype(jnp.bfloat16)


def join_kernel(own_keep, own_message, x_block, keep, message):
    core = lax.axis_index("row") & 1
    keep[0] = own_keep[...]
    message[: TILE + 16, :] = own_message[...]

    @pl.when(core == 0)
    def _():
        keep[1] = x_block[:, :HALF]
        message[TILE + 16 :, :] = x_block[:, HALF:]

    @pl.when(core == 1)
    def _():
        keep[1] = x_block[:, HALF:]
        message[TILE + 16 :, :] = x_block[:, :HALF]


def list_slots(own, partner, lists):
    device = lax.axis_index("row")
    z, q = device >> 2, device & 3
    for i, slots in enumerate((own, partner)):
        near, far = jnp.int32(0), jnp.int32(0)
        for s in range(SLOTS):
            tile = slots[12 + s]
            place = (((tile >> 2) - z) & 7) * QUAD + ((tile & 3) ^ q)
            live = (s < slots[24]).astype(jnp.int32)
            is_far = ((place >> 2) == 4).astype(jnp.int32)
            lists[i * PART + is_far * (2 * PART + far - near) + near] = (
                s * 1024 + slots[s] * 64 + place
            )
            far = far + live * is_far
            near = near + live * (1 - is_far)
        for u in range(UNROLL - 1):
            lists[i * PART + near + u] = 8 * 64 + 32
        lists[4 * PART + i] = near
        lists[4 * PART + 2 + i] = far


def slot_products(lists, far, adj_refs, product, add_to):
    unroll = 1 if far else UNROLL
    for i, adj in enumerate(adj_refs):
        part = 2 * far + i

        @pl.loop(0, (lists[4 * PART + part] + unroll - 1) // unroll)
        def _(step, i=i, adj=adj, part=part):
            codes = [lists[part * PART + step * unroll + u] for u in range(unroll)]
            places = [((code >> 6) & 15, i, code & 63) for code in codes]
            values = [product(adj[code >> 10], *at) for code, at in zip(codes, places)]
            for value, at in zip(values, places):
                add_to(value, *at)


def forward_near_kernel(own_any, partner_any, adj0, adj1, *refs):
    pieces, (acc, lists, panel, own, partner, sems) = refs[:7], refs[7:]
    copies = [
        pltpu.make_async_copy(own_any, own, sems.at[0]),
        pltpu.make_async_copy(partner_any, partner, sems.at[1]),
    ]
    for copy in copies:
        copy.start()
    for place, piece in zip((0, 1, 2, 3, 5, 6, 7), pieces):
        panel[place * QUAD : (place + 1) * QUAD] = piece[...]
    acc[...] = jnp.zeros_like(acc)
    for copy in copies:
        copy.wait()
    list_slots(own, partner, lists)

    def product(tile, row, i, place):
        return jnp.dot(tile, panel[place & 31], preferred_element_type=jnp.float32)

    def add_to(value, row, i, place):
        acc[2 * row + i] += value

    slot_products(lists, False, (adj0, adj1), product, add_to)


def forward_far_kernel(lists_any, adj0, adj1, near, far_a, far_b, *refs):
    outs, (acc, far, lists, sem) = refs[:NCOL], refs[NCOL:]
    copy = pltpu.make_async_copy(lists_any, lists, sem)
    copy.start()
    far[:2] = far_a[...]
    far[2:] = far_b[...]
    acc[...] = near[...]
    copy.wait()

    def product(tile, row, i, place):
        return jnp.dot(tile, far[place & 3], preferred_element_type=jnp.float32)

    def add_to(value, row, i, place):
        acc[2 * row + i] += value

    slot_products(lists, True, (adj0, adj1), product, add_to)
    for k, out in zip(MOVES, outs):
        row = col_target(k, 1)
        for i in range(2):
            out[i] = acc[2 * row + i].astype(jnp.bfloat16)


def backward_products(lists, adj_refs, back, acc, far):
    def product(tile, row, i, place):
        return lax.dot_general(
            tile,
            back[row & 7, pl.ds(i * TILE, TILE), :],
            (((0,), (0,)), ((), ())),
            preferred_element_type=jnp.float32,
        )

    def add_to(value, row, i, place):
        acc[place & 3 if far else place] += value

    slot_products(lists, far, adj_refs, product, add_to)


def backward_far_kernel(lists_any, adj0, adj1, *refs):
    received, (up, down, back, acc, lists, sem, pieces) = refs[:NCOL], refs[NCOL:]
    copy = pltpu.make_async_copy(lists_any, lists, sem)
    copy.start()
    for k, ref in zip(MOVES, received):
        source = col_target(k, -1)
        back[source] = ref[: 2 * TILE, :]
        pieces[source] = ref[2 * TILE :, :]
    acc[...] = jnp.zeros_like(acc)
    piece = pieces[0].astype(jnp.float32)
    for c in range(1, NCOL):
        piece = piece + pieces[c].astype(jnp.float32)
    for out in (up, down):
        out[2 * TILE :, :] = piece.astype(jnp.bfloat16)
    copy.wait()
    backward_products(lists, (adj0, adj1), back, acc, True)
    for k in range(QUAD):
        part = pl.ds((k & 1) * TILE, TILE)
        (up, down)[k >> 1][part, :] = acc[k].astype(jnp.bfloat16)


def backward_near_kernel(lists_any, adj0, adj1, back, act, out, act_out, acc, lists, sem):
    act_out[...] = act[...]
    copy = pltpu.make_async_copy(lists_any, lists, sem)
    copy.start()
    acc[...] = jnp.zeros_like(acc)
    copy.wait()
    backward_products(lists, (adj0, adj1), back, acc, False)
    out[...] = acc[: NZ * QUAD].astype(jnp.bfloat16)


def split(x):
    high = x.astype(jnp.bfloat16)
    return high, (x - high.astype(jnp.float32)).astype(jnp.bfloat16)


def dense_kernel(agg_own, agg_other, weight, cot_own, cot_other, act_out, send, send_x):
    first = (lax.axis_index("row") & 1) == 0
    own = agg_own[...]
    other = jnp.concatenate([agg_other[TILE:, :], agg_other[:TILE, :]], axis=0)
    w = weight[...]
    w_other_half = jnp.where(first, w[HALF:], w[:HALF])
    w_half = jnp.where(first, w[:HALF], w[HALF:])

    def dot(a, b, dims=((1,), (0,))):
        return lax.dot_general(a, b, (dims, ((), ())), preferred_element_type=jnp.float32)

    own_hi, own_lo = split(own)
    other_hi, other_lo = split(other)
    v = (dot(own_hi, w_half) + dot(own_lo, w_half)) + (
        dot(other_hi, w_other_half) + dot(other_lo, w_other_half)
    )
    scale = math.sqrt(2.0 / math.pi)
    square = v * v
    t = jnp.tanh(scale * (v + 0.044715 * (square * v)))
    cdf = 0.5 * (1.0 + t)
    act_out[...] = (v[:TILE] * cdf[:TILE]).astype(jnp.bfloat16)
    slope = cdf + 0.5 * v * ((1.0 - t) * (1.0 + t)) * (scale * (1.0 + 3.0 * 0.044715 * square))
    cot = jnp.concatenate([cot_own[...], cot_other[...]], axis=0).astype(jnp.float32)
    grad_hi, grad_lo = split(cot * slope)
    nodes = ((1,), (1,))
    back = (dot(grad_hi, w_half, nodes) + dot(grad_lo, w_half, nodes)).astype(jnp.bfloat16)
    rows = ((0,), (0,))
    w_part = (
        dot(own_hi, grad_hi, rows) + dot(own_lo, grad_hi, rows) + dot(own_hi, grad_lo, rows)
    )
    x_lo = lax.axis_index("col") >> 2
    for out, dest in ((send, x_lo), (send_x, 1 - x_lo)):
        out[: 2 * TILE, :] = back
        piece = jnp.where(dest == 0, w_part[:64], w_part[64:]).astype(jnp.bfloat16)
        out[2 * TILE : 2 * TILE + 64, :] = piece[:, :HALF]
        out[2 * TILE + 64 :, :] = piece[:, HALF:]


def f32(ref, start, rows=TILE):
    return ref[start : start + rows, :].astype(jnp.float32)


def ring_end_kernel(
    parts, own, up1, up2, up3, up4, down1, down2, down3, down4, kept, message, by_step
):
    z = lax.axis_index("row") >> 2
    half, size = 2 * TILE, QUAD * TILE
    pieces = (
        (own, half),
        (down1, half),
        (down2, size),
        (down3, size),
        (up4, size),
        (up3, size),
        (up2, size),
        (up1, half),
    )
    for k, (ref, start) in enumerate(pieces):
        by_step[(k + z) & 7] = ref[start:, :]
    w_sum = by_step[0].astype(jnp.float32)
    for a in range(1, NZ):
        w_sum = w_sum + by_step[a].astype(jnp.float32)
    message[half:, :] = w_sum.astype(jnp.bfloat16)
    for k in range(QUAD):
        start = k * TILE
        total = parts[k].astype(jnp.float32) + f32(up4, start) + f32(down4, start)
        if k < 2:
            kept[k] = total
        else:
            message[start - half : start - half + TILE, :] = total.astype(jnp.bfloat16)


def middle_kernel(kept, sent, from_x, w_lo, w_both, mine, message, w_here):
    x_lo = lax.axis_index("col") >> 2
    half = 2 * TILE
    for k, ref in enumerate((mine, message)):
        ref[:TILE, :] = (kept[k] + f32(from_x, k * TILE)).astype(jnp.bfloat16)
    sums = (
        f32(sent, half, W_ROWS) + f32(from_x, half, W_ROWS),
        w_lo[...].astype(jnp.float32) + w_both[...].astype(jnp.float32),
    )
    for value, place in zip(sums, (x_lo, 1 - x_lo)):
        high, low = split(value)
        w_here[place] = high.astype(jnp.float32) + low.astype(jnp.float32)
        start = pl.multiple_of(TILE + place * 2 * W_ROWS, W_ROWS)
        message[pl.ds(start, W_ROWS), :] = high
        message[pl.ds(start + W_ROWS, W_ROWS), :] = low


def last_kernel(mine, from_core, w_here, grad_out, w_out):
    core = lax.axis_index("row") & 1
    scale = 1.0 / 256.0

    def place(value, start):
        rows = pl.ds(pl.multiple_of(start, 64), 64)
        w_out[rows, :HALF] = value[:64, :] * scale
        w_out[rows, HALF:] = value[64:, :] * scale

    for x_lo in range(2):
        start = TILE + x_lo * 2 * W_ROWS
        place(w_here[x_lo], core * HALF + x_lo * 64)
        w_core = f32(from_core, start, W_ROWS) + f32(from_core, start + W_ROWS, W_ROWS)
        place(w_core, (1 - core) * HALF + x_lo * 64)

    @pl.when(core == 0)
    def _():
        grad_out[:, :HALF] = mine[...]
        grad_out[:, HALF:] = from_core[:TILE, :]

    @pl.when(core == 1)
    def _():
        grad_out[:, HALF:] = mine[...]
        grad_out[:, :HALF] = from_core[:TILE, :]


SMEM = pl.BlockSpec(memory_space=pltpu.SMEM)
VMEM = pl.BlockSpec(memory_space=pltpu.VMEM)
ANY = pl.BlockSpec(memory_space=pl.ANY)


def params(mib):
    return pltpu.CompilerParams(vmem_limit_bytes=mib << 20)


LIST_SCRATCH = [pltpu.SMEM((LIST,), jnp.int32), pltpu.SemaphoreType.DMA]


def cost(slots, size):
    return pl.CostEstimate(
        flops=slots * 2 * TILE * TILE * HALF, bytes_accessed=size << 20, transcendentals=0
    )


LISTS = [SMEM] * 4


def shape(*dims, dtype=jnp.bfloat16):
    return jax.ShapeDtypeStruct(dims, dtype)


def local(kernel, outs, n_in, name, scalars=0, any_in=0, scratch=(), cost=None, scalar_out=0):
    return pl.pallas_call(
        kernel,
        out_shape=outs,
        in_specs=[SMEM] * scalars + [ANY] * any_in + [VMEM] * (n_in - scalars - any_in),
        out_specs=(VMEM,) * (len(outs) - scalar_out) + (SMEM,) * scalar_out,
        scratch_shapes=scratch,
        compiler_params=params(20),
        cost_estimate=cost,
        name=name,
    )


def prepare(rows, cols, count, block):
    return local(
        prepare_kernel,
        (shape(TILE, HALF), shape(TILE + 16, HALF), shape(25, dtype=jnp.int32)),
        4,
        "prepare",
        scalars=3,
        scalar_out=1,
    )(rows, cols, count, block)


def join(own_keep, own_message, x_block):
    return local(
        join_kernel, (shape(2, TILE, HALF), shape(2 * TILE + 16, HALF)), 3, "join"
    )(own_keep, own_message, x_block)


def forward_near(own, partner, adj0, adj1, pieces):
    return local(
        forward_near_kernel,
        (shape(18, TILE, HALF, dtype=jnp.float32), shape(LIST, dtype=jnp.int32)),
        11,
        "forward_near",
        any_in=2,
        scalar_out=1,
        scratch=[
            pltpu.VMEM((NZ * QUAD, TILE, HALF), jnp.bfloat16),
            pltpu.SMEM((25,), jnp.int32),
            pltpu.SMEM((25,), jnp.int32),
            pltpu.SemaphoreType.DMA((2,)),
        ],
        cost=cost(21, 6),
    )(own, partner, adj0, adj1, *pieces)


def forward_far(lists, adj0, adj1, near, far_a, far_b):
    return local(
        forward_far_kernel,
        (shape(2, TILE, HALF),) * NCOL,
        6,
        "forward_far",
        any_in=1,
        scratch=[
            pltpu.VMEM((18, TILE, HALF), jnp.float32),
            pltpu.VMEM((QUAD, TILE, HALF), jnp.bfloat16),
        ]
        + LIST_SCRATCH,
        cost=cost(3, 4),
    )(lists, adj0, adj1, near, far_a, far_b)


def backward_far(lists, adj0, adj1, received):
    message = shape(2 * TILE + W_ROWS, HALF)
    return local(
        backward_far_kernel,
        (message, message, shape(NCOL, 2 * TILE, HALF)),
        11,
        "backward_far",
        any_in=1,
        scratch=[pltpu.VMEM((QUAD, TILE, HALF), jnp.float32)]
        + LIST_SCRATCH
        + [pltpu.VMEM((NCOL, W_ROWS, HALF), jnp.bfloat16)],
        cost=cost(3, 2),
    )(lists, adj0, adj1, *received)


def backward_near(lists, adj0, adj1, back, act):
    return local(
        backward_near_kernel,
        (shape(NZ * QUAD, TILE, HALF), shape(TILE, 2 * HALF)),
        5,
        "backward_near",
        any_in=1,
        scratch=[pltpu.VMEM((NZ * QUAD + 1, TILE, HALF), jnp.float32)] + LIST_SCRATCH,
        cost=cost(21, 6),
    )(lists, adj0, adj1, back, act)


def dense(agg_own, agg_other, weight, cot_own, cot_other):
    return local(
        dense_kernel,
        (shape(TILE, 2 * HALF),) + (shape(2 * TILE + W_ROWS, HALF),) * 2,
        5,
        "dense",
    )(agg_own, agg_other, weight, cot_own, cot_other)


def ring_end(parts, *messages):
    return local(
        ring_end_kernel,
        (shape(2, TILE, HALF, dtype=jnp.float32), shape(2 * TILE + W_ROWS, HALF)),
        10,
        "ring_end",
        scratch=[pltpu.VMEM((NZ, W_ROWS, HALF), jnp.bfloat16)],
    )(parts, *messages)


def middle(*operands):
    return local(
        middle_kernel,
        (
            shape(TILE, HALF),
            shape(TILE + 4 * W_ROWS, HALF),
            shape(2, W_ROWS, HALF, dtype=jnp.float32),
        ),
        5,
        "middle",
    )(*operands)


def last(mine, from_core, w_here):
    return local(
        last_kernel,
        (shape(TILE, 2 * HALF), shape(2 * HALF, 2 * HALF, dtype=jnp.float32)),
        3,
        "last",
    )(mine, from_core, w_here)


def add(a, b):
    return (a.astype(jnp.float32) + b.astype(jnp.float32)).astype(jnp.bfloat16)


def per_device(features, adj_tiles, tile_row, tile_col, tile_count, weight, cotangent):
    adj0 = adj_tiles[0, 0]
    block = features[0]

    x_block = quad_permute(block, 2)
    keep, message, own_lists = prepare(tile_row[0, 0], tile_col[0, 0], tile_count, block)
    keep, message = join(keep, message, x_block)
    from_core = quad_permute(message, 1)
    core_keep = from_core[16:].reshape(2, TILE, HALF)
    chunk = jnp.stack([keep[0], core_keep[0], keep[1], core_keep[1]])
    partner_lists = from_core[0, :25].astype(jnp.int32)
    adj1 = quad_permute(adj0, 1)
    cot1 = quad_permute(cotangent, 1)

    up1, down1 = z_shift(chunk, 1), z_shift(chunk, -1)
    up2, down2 = z_shift(up1, 1), z_shift(down1, -1)
    up3, down3 = z_shift(up2, 1), z_shift(down2, -1)
    far_a, far_b = z_shift(up3[:2], 1), z_shift(down3[2:], -1)
    near, lists = forward_near(
        own_lists, partner_lists, adj0, adj1, [chunk, down1, down2, down3, up3, up2, up1]
    )
    shares = forward_far(lists, adj0, adj1, near, far_a, far_b)
    agg = sum(
        (col_move(share, k) if k else share).astype(jnp.float32)
        for k, share in zip(MOVES, shares)
    ).reshape(2 * TILE, HALF)
    agg_other = quad_permute(agg, 1)
    activated, send, send_x = dense(agg, agg_other, weight, cotangent, cot1)
    received = [col_move(send if k < 4 else send_x, k) if k else send for k in MOVES]

    half, size = 2 * TILE, QUAD * TILE
    own, own_down, back = backward_far(lists, adj0, adj1, received)
    blocks, activated = backward_near(lists, adj0, adj1, back, activated)
    parts = blocks.reshape(NZ, size, HALF)
    up1, down1 = z_shift(own, 1), z_shift(own_down, -1)
    up = [add(parts[3, :half], up1[:half]), parts[3, half:], up1[half:]]
    down = [parts[5, :half], add(parts[5, half:], down1[:half]), down1[half:]]
    up2, down2 = z_shift(jnp.concatenate(up), 1), z_shift(jnp.concatenate(down), -1)
    up = [add(parts[2], up2[:size]), up2[size:]]
    down = [add(parts[6], down2[:size]), down2[size:]]
    up3, down3 = z_shift(jnp.concatenate(up), 1), z_shift(jnp.concatenate(down), -1)
    up4 = z_shift(jnp.concatenate([add(parts[1], up3[:size]), up3[size:]]), 1)
    down4 = z_shift(add(parts[7], down3[:size]), -1)

    kept, to_x = ring_end(blocks, own, up1, up2, up3, up4, down1, down2, down3, down4)
    w_send = to_x[half:]
    from_x = quad_permute(to_x, 2)
    w_lo = lax.ppermute(w_send, "col", [(c, c ^ 4) for c in range(NCOL)])
    both = [
        (r * NCOL + c, (r ^ 2) * NCOL + (c ^ 4)) for r in range(NZ * QUAD) for c in range(NCOL)
    ]
    w_both = lax.ppermute(w_send, ("row", "col"), both)
    mine, to_core, w_here = middle(kept, to_x, from_x, w_lo, w_both)
    grad, weight_grad = last(mine, quad_permute(to_core, 1), w_here)
    return (activated, weight_grad, grad[None])


def solution(mesh):
    return jax.shard_map(
        per_device,
        mesh=mesh,
        in_specs=(
            P("col", "row", None),
            P("row", "col", None, None, None),
            P("row", "col", None),
            P("row", "col", None),
            P("row", "col"),
            P(),
            P(("row", "col"), None),
        ),
        out_specs=(P(("row", "col"), None), P(), P("col", "row", None)),
        check_vma=False,
    )
```
